32 devices in a mesh: dp: 4 (over z), expert: 8 (over y, x, core).
Axes of the slice: x: 2, y: 2, z: 4, core: 2. Of those that a mesh axis runs over, the one named last changes fastest.
Arguments:
- tokens: bfloat16 [16384, 1536], P(('dp', 'expert')), may hold values from -6 to 6
- cotangent: bfloat16 [16384, 1536], P(('dp', 'expert')), may hold values from -6 to 6
- routes: int32 [16384, 4], P(('dp', 'expert')), may hold values from 0 to 7, all different within a row; in each aligned block of 512 rows (0 to 511, 512 to 1023, ...) at most 384 rows name the same one
- doc_lengths: int32 [32, 3], P(('dp', 'expert')), may hold values from 1 to 384, 512 in all within a row
- query_weight: float32 [1536, 1536], P(('dp', 'expert')), may hold values from -0.15625 to 0.15625
- query_first: float32 [1536, 1536], P(('dp', 'expert')), may hold values from -160 to 160
- query_second: float32 [1536, 1536], P(('dp', 'expert')), may hold values from 65.536 to 262.144
- keyvalue_weight: float32 [1536, 512], P(('dp', 'expert')), may hold values from -0.15625 to 0.15625
- keyvalue_first: float32 [1536, 512], P(('dp', 'expert')), may hold values from -160 to 160
- keyvalue_second: float32 [1536, 512], P(('dp', 'expert')), may hold values from 65.536 to 262.144
- output_weight: float32 [1536, 1536], P(('dp', 'expert')), may hold values from -0.875 to 0.875
- output_first: float32 [1536, 1536], P(('dp', 'expert')), may hold values from -16 to 16
- output_second: float32 [1536, 1536], P(('dp', 'expert')), may hold values from 0.65536 to 2.62144
- router_weight: float32 [1536, 8], P(('dp', 'expert')), may hold values from -0.078125 to 0.078125
- router_first: float32 [1536, 8], P(('dp', 'expert')), may hold values from -896 to 896
- router_second: float32 [1536, 8], P(('dp', 'expert')), may hold values from 1843.2 to 7372.8
- norm_gains: float32 [2, 1536], P(None, ('dp', 'expert')), may hold values from 0.5 to 1.5
- gains_first: float32 [2, 1536], P(None, ('dp', 'expert')), may hold values from -160 to 160
- gains_second: float32 [2, 1536], P(None, ('dp', 'expert')), may hold values from 65.536 to 262.144
- expert_in: float32 [8, 1536, 1536], P('expert', 'dp'), may hold values from -0.15625 to 0.15625
- expert_in_first: float32 [8, 1536, 1536], P('expert', 'dp'), may hold values from -32 to 32
- expert_in_second: float32 [8, 1536, 1536], P('expert', 'dp'), may hold values from 2.048 to 8.192
- expert_out: float32 [8, 768, 1536], P('expert', 'dp'), may hold values from -0.625 to 0.625
- expert_out_first: float32 [8, 768, 1536], P('expert', 'dp'), may hold values from -8 to 8
- expert_out_second: float32 [8, 768, 1536], P('expert', 'dp'), may hold values from 0.18432 to 0.73728
Outputs:
- mixed: bfloat16 [16384, 1536], P(('dp', 'expert'))
- tokens_grad: float32 [16384, 1536], P(('dp', 'expert'))
- query_first_new: float32 [1536, 1536], P(('dp', 'expert'))
- query_second_new: float32 [1536, 1536], P(('dp', 'expert'))
- query_new: float32 [1536, 1536], P(('dp', 'expert'))
- keyvalue_first_new: float32 [1536, 512], P(('dp', 'expert'))
- keyvalue_second_new: float32 [1536, 512], P(('dp', 'expert'))
- keyvalue_new: float32 [1536, 512], P(('dp', 'expert'))
- output_first_new: float32 [1536, 1536], P(('dp', 'expert'))
- output_second_new: float32 [1536, 1536], P(('dp', 'expert'))
- output_new: float32 [1536, 1536], P(('dp', 'expert'))
- router_first_new: float32 [1536, 8], P(('dp', 'expert'))
- router_second_new: float32 [1536, 8], P(('dp', 'expert'))
- router_new: float32 [1536, 8], P(('dp', 'expert'))
- gains_first_new: float32 [2, 1536], P(None, ('dp', 'expert'))
- gains_second_new: float32 [2, 1536], P(None, ('dp', 'expert'))
- gains_new: float32 [2, 1536], P(None, ('dp', 'expert'))
- expert_in_first_new: float32 [8, 1536, 1536], P('expert', 'dp')
- expert_in_second_new: float32 [8, 1536, 1536], P('expert', 'dp')
- expert_in_new: float32 [8, 1536, 1536], P('expert', 'dp')
- expert_out_first_new: float32 [8, 768, 1536], P('expert', 'dp')
- expert_out_second_new: float32 [8, 768, 1536], P('expert', 'dp')
- expert_out_new: float32 [8, 768, 1536], P('expert', 'dp')
The draws below stay inside these ranges and needn't reach their ends.
Inputs may be any that keep to these rules, and one draw needn't show every extreme that they name: `routes`: each row names 4 different experts. Among the rows of one device no expert is named more than 384 times, and some device's rows name some expert exactly 384 times. `doc_lengths`: each device's 3 lengths sum to 512, and the longest is exactly 384.
All inputs are finite; a program needn't handle non-finite values.
Results may differ from the reference program's by a relative error of at most 0.018.
Values may be sent and summed in bfloat16 or wider, within the bound.
No kernel may reach another device: no remote copies, remote signals or barrier semaphores. Data moves between devices by JAX's collectives and lax.ppermute only.
A program may use at most 256 MiB of HBM per device.

```python
import math
import jax
import jax.numpy as jnp
import numpy as np
from jax import lax

D = 1536
FF = 768
HEADS = 12
KV_HEADS = 2
HEAD_DIM = 128
TOP = 4
TOK_DEV = 512
DOCS = 3
STEP = 10
EXPERTS = 8
TOKENS = 16384
MOST = 384
CAP = 384
N_DP = 4
N_EXPERT = 8


def with_spikes(drawn, key, source, target, parts, factor):
    def block_of(dim):
        return (jnp.arange(drawn.shape[dim]) // (drawn.shape[dim] // parts)).reshape((-1,) + (1,) * (drawn.ndim - 1 - dim))

    near = jax.random.permutation(key, parts)[block_of(target)]
    second = (block_of(target) + parts // 2) % parts
    return jnp.where((block_of(source) == near) | (block_of(source) == second), factor * drawn, drawn)


def shard_levels(rng, extent, split, smallest, largest):
    def one(dim, blocks):
        draws = jax.random.uniform(jax.random.fold_in(jax.random.fold_in(rng, 6), dim), (blocks,), jnp.float32, smallest / len(split), largest / len(split))
        return jnp.repeat(jnp.exp(draws), extent[dim] // blocks).reshape((-1,) + (1,) * (len(extent) - dim - 1))

    gain = one(*split[0])
    for cut in split[1:]:
        gain = gain * one(*cut)
    return gain


def profile(amount, total, reach, skew):
    loads = [(1 << 20) // math.isqrt(rank ** skew) + 1 for rank in range(2, amount + 1)]
    surplus, holding = total - reach - (amount - 1), [1] * (amount - 1)
    while surplus > 0:
        free = [i for i in range(amount - 1) if holding[i] < reach]
        mass, left = sum([loads[i] for i in free]), surplus
        for i in free:
            extra = min(reach - holding[i], max(1, left * loads[i] // mass), surplus)
            holding[i] = holding[i] + extra
            surplus = surplus - extra
    return np.array([reach] + holding)


def ragged(rng, amount, total, reach, slope):
    if amount == 2:
        one = jax.random.randint(rng, (), max(1, total - reach), min(reach, total - 1) + 1)
        return jnp.stack([one, total - one])
    tallies = jnp.asarray(profile(amount, total, reach, slope), jnp.int32)
    pairs = (amount - 1) // 2
    donor, sink = tallies[1:1 + 2 * pairs:2], tallies[2:2 + 2 * pairs:2]
    room = jnp.minimum(donor - 1, reach - sink)
    shifted = jax.random.randint(jax.random.fold_in(rng, 1), (pairs,), 0, 1 << 20) % (room + 1)
    tallies = tallies.at[1:1 + 2 * pairs:2].set(donor - shifted).at[2:2 + 2 * pairs:2].set(sink + shifted)
    return tallies[jax.random.permutation(jax.random.fold_in(rng, 2), amount)]


def deal_out(key, own, number, rows, amount, top, limit, skew):
    order = jax.random.permutation(key, amount)
    heavy_load, usual = load_shares(amount, rows * top, limit, skew, True), load_shares(amount, rows * top, limit, skew, False)
    places = jnp.arange(amount)

    def named(sizes, rotation):
        used = int((sizes > 0).sum())
        fixed = max(1, used // 4)
        moved = fixed + (places - fixed + rotation * (used - fixed)) % max(1, amount - fixed)
        return jnp.zeros((amount,), jnp.int32).at[order[jnp.where(places < fixed, places, moved)]].set(jnp.asarray(sizes, jnp.int32))

    sizes = jnp.where(number % 4 == 0, named(heavy_load, number // 4), named(usual, number - number // 4 - 1))
    mixed = jax.random.permutation(jax.random.fold_in(own, 3), amount)
    giver, sink = mixed[0:amount // 2 * 2:2], mixed[1:amount // 2 * 2:2]
    room = jnp.minimum(sizes[giver] - 1, limit - sizes[sink]) // 2
    room = jnp.where((giver == order[0]) | (sink == order[0]) | (sizes[sink] == 0), 0, jnp.maximum(room, 0))
    moved = jax.random.randint(jax.random.fold_in(own, 4), (amount // 2,), 0, 1 << 20) % (room + 1)
    sizes = sizes.at[giver].add(-moved).at[sink].add(moved)
    items = jnp.searchsorted(jnp.cumsum(sizes), jnp.arange(rows * top), side="right").astype(jnp.int32)
    table = items.reshape(top, rows).T
    table = table[jax.random.permutation(jax.random.fold_in(own, 1), rows)]
    rotation = jax.random.randint(jax.random.fold_in(own, 2), (rows, 1), 0, top)
    return jnp.take_along_axis(table, (jnp.arange(top)[None, :] + rotation) % top, axis=1)


def load_shares(number_of, total, most, slope, full):
    loads = [(1 << 20) // math.isqrt(grade ** slope) + 1 for grade in range(1, number_of + 1)]
    largest = most if full else min(most, max(-(-total // number_of), total * loads[0] // sum(loads)))
    least = 1 if total - largest >= number_of - 1 else 0
    holding, surplus = [largest] + [least] * (number_of - 1), total - largest - least * (number_of - 1)
    while surplus > 0:
        free = [i for i in range(1, number_of) if holding[i] < largest] or [i for i in range(1, number_of) if holding[i] < most]
        whole, budget = sum([loads[i] for i in free]), surplus
        for i in free:
            more = min(most - holding[i], max(1, budget * loads[i] // whole), surplus)
            holding[i] = holding[i] + more
            surplus = surplus - more
    return np.array(holding)


def gaussian(stream_key, dims, spread, most, shards=(), kind=jnp.bfloat16):
    array = jax.random.normal(stream_key, dims, jnp.float32) * spread
    if len(shards) > 0:
        array = shard_levels(stream_key, dims, shards, -0.22, 0.18) * array
    return jnp.clip(array, min=-most, max=most).astype(kind)


def noise_with(key, shape, spread, reach, cuts, heavy, kind=jnp.bfloat16):
    values = spread * jax.random.normal(key, shape, jnp.float32)
    if cuts:
        values = values * shard_levels(key, shape, cuts, -0.22, 0.18)
    return jnp.clip(with_spikes(values, jax.random.fold_in(key, 3), *heavy), -reach, reach).astype(kind)


def setup_inputs(seed: int = 0) -> dict:
    streams_of = jax.random.split(jax.random.key(seed), 26)
    tokens = noise_with(streams_of[0], (TOKENS, D), 1.0, 6.0, ((0, 32),), (0, 1, 32, 2.75))
    cotangent = gaussian(streams_of[1], (TOKENS, D), 1.0, 6.0, ((0, 32),))
    routes_keys = jax.random.split(jax.random.fold_in(streams_of[2], 1), TOKENS // TOK_DEV)
    routes_turns = jax.random.permutation(jax.random.fold_in(streams_of[2], 3), TOKENS // TOK_DEV)
    routes = jax.vmap(lambda own, number: deal_out(jax.random.fold_in(streams_of[2], 2), own, number, TOK_DEV, EXPERTS, TOP, CAP, 1))(routes_keys, routes_turns).reshape((TOKENS, TOP))
    doc_lengths = jax.vmap(lambda own: ragged(own, DOCS, TOK_DEV, MOST, 2))(jax.random.split(streams_of[3], (N_DP * N_EXPERT))).reshape((N_DP * N_EXPERT, DOCS)).astype(jnp.int32)
    query_weight = gaussian(streams_of[4], (D, HEADS * HEAD_DIM), D ** -0.5, 0.15625, ((0, 32),), jnp.float32)
    query_first = gaussian(streams_of[5], (D, HEADS * HEAD_DIM), (0.22 * TOKENS ** 0.5), 160.0, ((0, 32),), jnp.float32)
    query_second = jnp.clip(jnp.exp(math.log(262.144) - 1.3862944 * jax.random.uniform(streams_of[6], (D, HEADS * HEAD_DIM), jnp.float32) ** shard_levels(streams_of[6], (D, HEADS * HEAD_DIM), ((0, 32),), -0.2, 0.2)), 65.536, 262.144)
    keyvalue_weight = gaussian(streams_of[7], (D, 2 * KV_HEADS * HEAD_DIM), D ** -0.5, 0.15625, ((0, 32),), jnp.float32)
    keyvalue_first = gaussian(streams_of[8], (D, 2 * KV_HEADS * HEAD_DIM), (0.22 * TOKENS ** 0.5), 160.0, ((0, 32),), jnp.float32)
    keyvalue_second = jnp.clip(jnp.exp(math.log(262.144) - 1.3862944 * jax.random.uniform(streams_of[9], (D, 2 * KV_HEADS * HEAD_DIM), jnp.float32) ** shard_levels(streams_of[9], (D, 2 * KV_HEADS * HEAD_DIM), ((0, 32),), -0.2, 0.2)), 65.536, 262.144)
    output_weight = gaussian(streams_of[10], (HEADS * HEAD_DIM, D), (D // 32) ** -0.5, 0.875, ((0, 32),), jnp.float32)
    output_first = gaussian(streams_of[11], (HEADS * HEAD_DIM, D), (0.022 * TOKENS ** 0.5), 16.0, ((0, 32),), jnp.float32)
    output_second = jnp.clip(jnp.exp(math.log(2.62144) - 1.3862944 * jax.random.uniform(streams_of[12], (HEADS * HEAD_DIM, D), jnp.float32) ** shard_levels(streams_of[12], (HEADS * HEAD_DIM, D), ((0, 32),), -0.2, 0.2)), 0.65536, 2.62144)
    router_weight = gaussian(streams_of[13], (D, EXPERTS), (4 * D) ** -0.5, 0.078125, ((0, 32),), jnp.float32)
    router_first = gaussian(streams_of[14], (D, EXPERTS), (1.67 * (TOKENS * TOP // EXPERTS) ** 0.5), 896.0, ((0, 32),), jnp.float32)
    router_second = jnp.clip(jnp.exp(math.log(7372.8) - 1.3862944 * jax.random.uniform(streams_of[15], (D, EXPERTS), jnp.float32) ** shard_levels(streams_of[15], (D, EXPERTS), ((0, 32),), -0.2, 0.2)), 1843.2, 7372.8)
    norm_gains = jnp.clip(1.0 + 0.1 * jax.random.normal(streams_of[16], (2, D), jnp.float32), 0.5, 1.5)
    gains_first = gaussian(streams_of[17], (2, D), (0.22 * TOKENS ** 0.5), 160.0, ((1, 32),), jnp.float32)
    gains_second = jnp.clip(jnp.exp(math.log(262.144) - 1.3862944 * jax.random.uniform(streams_of[18], (2, D), jnp.float32) ** shard_levels(streams_of[18], (2, D), ((1, 32),), -0.2, 0.2)), 65.536, 262.144)
    expert_in = gaussian(streams_of[19], (EXPERTS, D, 2 * FF), D ** -0.5, 0.15625, ((0, 8), (1, 4)), jnp.float32)
    expert_in_first = gaussian(streams_of[20], (EXPERTS, D, 2 * FF), (0.055 * (TOKENS * TOP // EXPERTS) ** 0.5), 32.0, ((0, 8), (1, 4)), jnp.float32)
    expert_in_second = jnp.clip(jnp.exp(math.log(8.192) - 1.3862944 * jax.random.uniform(streams_of[21], (EXPERTS, D, 2 * FF), jnp.float32) ** shard_levels(streams_of[21], (EXPERTS, D, 2 * FF), ((0, 8), (1, 4)), -0.2, 0.2)), 2.048, 8.192)
    expert_out = gaussian(streams_of[22], (EXPERTS, FF, D), (FF // 8) ** -0.5, 0.625, ((0, 8), (1, 4)), jnp.float32)
    expert_out_first = gaussian(streams_of[23], (EXPERTS, FF, D), (0.0167 * (TOKENS * TOP // EXPERTS) ** 0.5), 8.0, ((0, 8), (1, 4)), jnp.float32)
    expert_out_second = jnp.clip(jnp.exp(math.log(0.73728) - 1.3862944 * jax.random.uniform(streams_of[24], (EXPERTS, FF, D), jnp.float32) ** shard_levels(streams_of[24], (EXPERTS, FF, D), ((0, 8), (1, 4)), -0.2, 0.2)), 0.18432, 0.73728)
    return {"tokens": tokens, "cotangent": cotangent, "routes": routes, "doc_lengths": doc_lengths, "query_weight": query_weight, "query_first": query_first, "query_second": query_second, "keyvalue_weight": keyvalue_weight, "keyvalue_first": keyvalue_first, "keyvalue_second": keyvalue_second, "output_weight": output_weight, "output_first": output_first, "output_second": output_second, "router_weight": router_weight, "router_first": router_first, "router_second": router_second, "norm_gains": norm_gains, "gains_first": gains_first, "gains_second": gains_second, "expert_in": expert_in, "expert_in_first": expert_in_first, "expert_in_second": expert_in_second, "expert_out": expert_out, "expert_out_first": expert_out_first, "expert_out_second": expert_out_second}


EPS = 1e-06
NEG = -1e+30
BETA_ONE = 0.9
BETA_TWO = 0.999
ADAM_EPS = 1e-08
DECAY = 0.1
ROPE_BASE = 10000.0
RATE_SCALE = 2.5
GAIN_RATE = 0.6
PRECISE = lax.Precision.HIGHEST

@jax.custom_vjp
def low(v):
    return lax.optimization_barrier(v.astype(jnp.bfloat16)).astype(jnp.float32)

@jax.custom_vjp
def low_back(v):
    return v

def low_keep(v):
    return (low(v), None)

def low_pass(kept, grad):
    return (grad,)

def back_keep(v):
    return (v, None)

def back_low(kept, grad):
    return (low(grad),)
low.defvjp(low_keep, low_pass)
low_back.defvjp(back_keep, back_low)

def doc_tables(lengths, rows_count):
    position = jnp.arange(rows_count, dtype=jnp.int32)
    doc_ends = jnp.cumsum(lengths).astype(jnp.int32)
    doc_starts = (doc_ends - lengths).astype(jnp.int32)
    doc_index = lax.optimization_barrier(jnp.sum((position[:, None] >= doc_ends[None, :]).astype(jnp.int32), 1)).astype(jnp.int32)
    doc_hot = doc_index[:, None] == jnp.arange(lengths.shape[0], dtype=jnp.int32)[None, :]
    start_of = lax.optimization_barrier(jnp.sum(jnp.where(doc_hot, doc_starts[None, :], 0), 1)).astype(jnp.int32)
    offset = (position - start_of).astype(jnp.float32)
    frequency = ROPE_BASE ** (-2.0 * jnp.arange(HEAD_DIM // 2, dtype=jnp.float32) / HEAD_DIM)
    angles = offset[:, None] * frequency[None, :]
    allowed = (doc_index[:, None] == doc_index[None, :]) & (position[None, :] <= position[:, None])
    return (jnp.cos(angles), jnp.sin(angles), allowed)

def rotate(values, cos_table, sin_table):
    half_width = values.shape[-1] // 2
    first_half = values[..., :half_width]
    second_half = values[..., half_width:]
    cosine = cos_table[:, None, :]
    sine_part = sin_table[:, None, :]
    return jnp.concatenate([first_half * cosine - second_half * sine_part, second_half * cosine + first_half * sine_part], -1)

def gelu_tanh(values):
    return jax.nn.gelu(values, approximate=True)

def learning_rates():
    return (RATE_SCALE * D ** (-0.5), RATE_SCALE * D ** (-0.5), RATE_SCALE * (D // 32) ** (-0.5), RATE_SCALE * (4 * D) ** (-0.5), GAIN_RATE, RATE_SCALE * D ** (-0.5), RATE_SCALE * (FF // 8) ** (-0.5))

def adam_update(weight, first, second, grad, rate, decay):
    new_first = BETA_ONE * first + (1.0 - BETA_ONE) * grad
    new_second = BETA_TWO * second + (1.0 - BETA_TWO) * grad * grad
    first_hat = new_first / (1.0 - BETA_ONE ** STEP)
    second_hat = new_second / (1.0 - BETA_TWO ** STEP)
    new_weight = weight - rate * (first_hat / (jnp.sqrt(second_hat) + ADAM_EPS) + decay * weight)
    return (new_first, new_second, new_weight)

def layer_block(block_rows, block_routes, block_lengths, query_weight, keyvalue_weight, output_weight, router_weight, norm_gains, expert_in, expert_out):
    rows_count = block_rows.shape[0]
    groups = HEADS // KV_HEADS
    width_kv = KV_HEADS * HEAD_DIM
    cos_table, sin_table, allowed = doc_tables(block_lengths, rows_count)
    inv_one = lax.rsqrt(lax.optimization_barrier(jnp.mean(block_rows * block_rows, -1, keepdims=True)) + EPS)
    attn_in = low(block_rows * inv_one * norm_gains[0])
    query_raw = low_back(jnp.dot(attn_in, query_weight, precision=PRECISE))
    keyvalue_raw = low_back(jnp.dot(attn_in, keyvalue_weight, precision=PRECISE))
    queries = low(rotate(query_raw.reshape(rows_count, HEADS, HEAD_DIM), cos_table, sin_table)).reshape(rows_count, KV_HEADS, groups, HEAD_DIM)
    keys_rot = low(rotate(keyvalue_raw[:, :width_kv].reshape(rows_count, KV_HEADS, HEAD_DIM), cos_table, sin_table))
    values_in = low(keyvalue_raw[:, width_kv:].reshape(rows_count, KV_HEADS, HEAD_DIM))
    scores = low_back(jnp.einsum('tkgd,skd->kgts', queries, keys_rot, precision=PRECISE) * HEAD_DIM ** (-0.5))
    scores = jnp.where(allowed[None, None], scores, NEG)
    probabilities = low(jax.nn.softmax(scores, axis=-1))
    attended = jnp.einsum('kgts,skd->tkgd', probabilities, values_in, precision=PRECISE).reshape(rows_count, HEADS * HEAD_DIM)
    attended = low(low_back(attended))
    residual_mid = block_rows + low_back(jnp.dot(attended, output_weight, precision=PRECISE))
    inv_two = lax.rsqrt(lax.optimization_barrier(jnp.mean(residual_mid * residual_mid, -1, keepdims=True)) + EPS)
    moe_in = low(residual_mid * inv_two * norm_gains[1])
    logits = low_back(jnp.dot(block_rows, router_weight, precision=PRECISE))
    expert_ids = jnp.arange(EXPERTS, dtype=jnp.int32)
    route_hot = block_routes[:, :, None] == expert_ids[None, None, :]
    picked = lax.optimization_barrier(jnp.sum(jnp.where(route_hot, logits[:, None, :], 0.0), -1))
    gate_weights = jax.nn.softmax(picked, axis=-1)
    flat_routes = block_routes.reshape(-1).astype(jnp.int32)
    flat_hot = (flat_routes[:, None] == expert_ids[None, :]).astype(jnp.int32)
    slot_index = lax.optimization_barrier(jnp.sum((jnp.cumsum(flat_hot, 0).astype(jnp.int32) - 1) * flat_hot, 1)).astype(jnp.int32)
    destination = (flat_routes * CAP + slot_index).astype(jnp.int32)
    token_of = (jnp.arange(rows_count * TOP, dtype=jnp.int32) // TOP).astype(jnp.int32)
    route_rows = low_back(moe_in[token_of])
    slot_rows = jnp.zeros((EXPERTS * CAP, D), route_rows.dtype).at[destination].set(route_rows).reshape(EXPERTS, CAP, D)
    gate_up = low_back(jnp.einsum('ecd,edf->ecf', slot_rows, expert_in, precision=PRECISE))
    product = low(gelu_tanh(gate_up[..., :FF]) * gate_up[..., FF:])
    expert_rows = low(low_back(jnp.einsum('ecf,efd->ecd', product, expert_out, precision=PRECISE)))
    routed = expert_rows.reshape(EXPERTS * CAP, D)[destination].reshape(rows_count, TOP, D)
    return residual_mid + lax.optimization_barrier(jnp.sum(gate_weights[:, :, None] * routed, 1))

def reference(tokens, cotangent, routes, doc_lengths, query_weight, query_first, query_second, keyvalue_weight, keyvalue_first, keyvalue_second, output_weight, output_first, output_second, router_weight, router_first, router_second, norm_gains, gains_first, gains_second, expert_in, expert_in_first, expert_in_second, expert_out, expert_out_first, expert_out_second):
    devices_count = N_DP * N_EXPERT
    route_blocks = routes.reshape(devices_count, TOK_DEV, TOP)

    def forward(inputs, *weight_args):
        weight_copies = [low(weight_arg) for weight_arg in weight_args]

        def scan_step(carried, block_item):
            block_rows, block_routes, block_lengths = block_item
            return (carried, jax.checkpoint(layer_block)(block_rows, block_routes, block_lengths, *weight_copies))
        unused, outputs = lax.scan(scan_step, jnp.zeros((), jnp.float32), (inputs.reshape(devices_count, TOK_DEV, D), route_blocks, doc_lengths))
        return outputs.reshape(devices_count * TOK_DEV, D)
    weights = (query_weight, keyvalue_weight, output_weight, router_weight, norm_gains, expert_in, expert_out)
    firsts = (query_first, keyvalue_first, output_first, router_first, gains_first, expert_in_first, expert_out_first)
    seconds = (query_second, keyvalue_second, output_second, router_second, gains_second, expert_in_second, expert_out_second)
    block_out, pull_back = jax.vjp(forward, tokens.astype(jnp.float32), *weights)
    gradients = pull_back(cotangent.astype(jnp.float32))
    rates = learning_rates()
    decays = (DECAY, DECAY, DECAY, DECAY, 0.0, DECAY, DECAY)
    updates = [adam_update(weights[index_w], firsts[index_w], seconds[index_w], gradients[index_w + 1], rates[index_w], decays[index_w]) for index_w in range(7)]
    return (block_out.astype(jnp.bfloat16), gradients[0], updates[0][0], updates[0][1], updates[0][2], updates[1][0], updates[1][1], updates[1][2], updates[2][0], updates[2][1], updates[2][2], updates[3][0], updates[3][1], updates[3][2], updates[4][0], updates[4][1], updates[4][2], updates[5][0], updates[5][1], updates[5][2], updates[6][0], updates[6][1], updates[6][2])
```

```python
import functools

import jax
import jax.numpy as jnp
from jax import lax
from jax.experimental import pallas as pl
from jax.experimental.pallas import tpu as pltpu
from jax.sharding import PartitionSpec as P

D = 1536
FF = 768
HEADS = 12
KV_HEADS = 2
HEAD_DIM = 128
TOP = 4
STEP = 10


EPS = 1e-06
NEG = -1e30
BETA_ONE = 0.9
BETA_TWO = 0.999
ADAM_EPS = 1e-08
DECAY = 0.1
ROPE_BASE = 10000.0
RATE_SCALE = 2.5
GAIN_RATE = 0.6


def doc_tables(lengths, rows_count):
    position = jnp.arange(rows_count, dtype=jnp.int32)
    doc_ends = jnp.cumsum(lengths)
    doc_starts = doc_ends - lengths
    doc_index = jnp.sum((position[:, None] >= doc_ends[None, :]).astype(jnp.int32), 1)
    doc_hot = doc_index[:, None] == jnp.arange(lengths.shape[0], dtype=jnp.int32)[None, :]
    start_of = jnp.sum(jnp.where(doc_hot, doc_starts[None, :], 0), 1)
    offset = (position - start_of).astype(jnp.float32)
    frequency = ROPE_BASE ** (-2.0 * jnp.arange(HEAD_DIM // 2, dtype=jnp.float32) / HEAD_DIM)
    angles = offset[:, None] * frequency[None, :]
    allowed = (doc_index[:, None] == doc_index[None, :]) & (position[None, :] <= position[:, None])
    return (jnp.cos(angles), jnp.sin(angles), allowed)


def rotate(values, cos_table, sin_table):
    half_width = values.shape[-1] // 2
    first_half = values[..., :half_width]
    second_half = values[..., half_width:]
    cosine = cos_table[:, None, :]
    sine_part = sin_table[:, None, :]
    return jnp.concatenate(
        [
            first_half * cosine - second_half * sine_part,
            second_half * cosine + first_half * sine_part,
        ],
        -1,
    )


def rotate_back(grads, cos_table, sin_table):
    half_width = grads.shape[-1] // 2
    first_half = grads[..., :half_width]
    second_half = grads[..., half_width:]
    cosine = cos_table[:, None, :]
    sine_part = sin_table[:, None, :]
    return jnp.concatenate(
        [
            first_half * cosine + second_half * sine_part,
            second_half * cosine - first_half * sine_part,
        ],
        -1,
    )


def gelu_tanh(values):
    return jax.nn.gelu(values, approximate=True)


def learning_rates():
    return (
        RATE_SCALE * D ** (-0.5),
        RATE_SCALE * D ** (-0.5),
        RATE_SCALE * (D // 32) ** (-0.5),
        RATE_SCALE * (4 * D) ** (-0.5),
        GAIN_RATE,
        RATE_SCALE * D ** (-0.5),
        RATE_SCALE * (FF // 8) ** (-0.5),
    )


def adam_update(weight, first, second, grad, rate, decay):
    new_first = BETA_ONE * first + (1.0 - BETA_ONE) * grad
    new_second = BETA_TWO * second + (1.0 - BETA_TWO) * grad * grad
    first_hat = new_first / (1.0 - BETA_ONE**STEP)
    second_hat = new_second / (1.0 - BETA_TWO**STEP)
    new_weight = weight - rate * (first_hat / (jnp.sqrt(second_hat) + ADAM_EPS) + decay * weight)
    return (new_first, new_second, new_weight)


def shards(
    tokens,
    cotangent,
    routes,
    doc_lengths,
    query_weight,
    query_first,
    query_second,
    keyvalue_weight,
    keyvalue_first,
    keyvalue_second,
    output_weight,
    output_first,
    output_second,
    router_weight,
    router_first,
    router_second,
    norm_gains,
    gains_first,
    gains_second,
    expert_in,
    expert_in_first,
    expert_in_second,
    expert_out,
    expert_out_first,
    expert_out_second,
):
    rows_count = tokens.shape[0]
    experts = router_weight.shape[1]
    owners = lax.axis_size("expert")
    per_owner = expert_in.shape[0]
    capacity = 3 * rows_count * TOP // (2 * experts)
    groups = HEADS // KV_HEADS
    width_kv = KV_HEADS * HEAD_DIM
    score_scale = HEAD_DIM ** (-0.5)
    query_full, keyvalue_full, output_full, router_full, gains_full = (
        lax.all_gather(query_weight.astype(jnp.bfloat16), ("dp", "expert"), axis=0, tiled=True),
        lax.all_gather(keyvalue_weight.astype(jnp.bfloat16), ("dp", "expert"), axis=0, tiled=True),
        lax.all_gather(output_weight.astype(jnp.bfloat16), ("dp", "expert"), axis=0, tiled=True),
        lax.all_gather(router_weight.astype(jnp.bfloat16), ("dp", "expert"), axis=0, tiled=True),
        lax.all_gather(norm_gains.astype(jnp.bfloat16), ("dp", "expert"), axis=1, tiled=True),
    )
    in_full, out_full = (
        lax.all_gather(expert_in.astype(jnp.bfloat16), "dp", axis=1, tiled=True),
        lax.all_gather(expert_out.astype(jnp.bfloat16), "dp", axis=1, tiled=True),
    )
    gain_attn = gains_full[0].astype(jnp.float32)
    gain_moe = gains_full[1].astype(jnp.float32)
    cos_table, sin_table, allowed = doc_tables(doc_lengths[0], rows_count)
    inputs = tokens.astype(jnp.float32)
    inv_one = lax.rsqrt(jnp.mean(inputs * inputs, -1, keepdims=True) + EPS)
    normed_one = inputs * inv_one
    attn_in = (normed_one * gain_attn).astype(jnp.bfloat16)
    query_raw = jnp.dot(attn_in, query_full, preferred_element_type=jnp.float32)
    keyvalue_raw = jnp.dot(attn_in, keyvalue_full, preferred_element_type=jnp.float32)
    queries = (
        rotate(query_raw.reshape(rows_count, HEADS, HEAD_DIM), cos_table, sin_table)
        .astype(jnp.bfloat16)
        .reshape(rows_count, KV_HEADS, groups, HEAD_DIM)
    )
    keys_rot = rotate(
        keyvalue_raw[:, :width_kv].reshape(rows_count, KV_HEADS, HEAD_DIM), cos_table, sin_table
    ).astype(jnp.bfloat16)
    values_in = (
        keyvalue_raw[:, width_kv:].reshape(rows_count, KV_HEADS, HEAD_DIM).astype(jnp.bfloat16)
    )

    def score_table():
        raw_scores = (
            jnp.einsum("tkgd,skd->kgts", queries, keys_rot, preferred_element_type=jnp.float32)
            * score_scale
        )
        return jnp.where(allowed[None, None], raw_scores, NEG)

    scores = score_table()
    row_max = jnp.max(scores, -1, keepdims=True)
    exponent = jnp.exp(scores - row_max)
    totals = jnp.sum(exponent, -1, keepdims=True)
    probabilities = exponent / totals
    log_sum = row_max + jnp.log(totals)
    attended = jnp.einsum(
        "kgts,skd->tkgd",
        probabilities.astype(jnp.bfloat16),
        values_in,
        preferred_element_type=jnp.float32,
    )
    attended = attended.reshape(rows_count, HEADS * HEAD_DIM).astype(jnp.bfloat16)
    residual_mid = inputs + jnp.dot(attended, output_full, preferred_element_type=jnp.float32)
    inv_two = lax.rsqrt(jnp.mean(residual_mid * residual_mid, -1, keepdims=True) + EPS)
    normed_two = residual_mid * inv_two
    moe_in = (normed_two * gain_moe).astype(jnp.bfloat16)
    logits = jnp.dot(tokens, router_full, preferred_element_type=jnp.float32)
    expert_ids = jnp.arange(experts, dtype=jnp.int32)
    route_hot = routes[:, :, None] == expert_ids[None, None, :]
    picked = jnp.sum(jnp.where(route_hot, logits[:, None, :], 0.0), -1)
    gate_weights = jax.nn.softmax(picked, axis=-1)
    flat_routes = routes.reshape(-1)
    flat_hot = (flat_routes[:, None] == expert_ids[None, :]).astype(jnp.int32)
    slot_index = jnp.sum((jnp.cumsum(flat_hot, 0) - 1) * flat_hot, 1)
    destination = flat_routes * capacity + slot_index
    route_ids = jnp.arange(rows_count * TOP, dtype=jnp.int32)
    source_route = jnp.zeros((experts * capacity,), jnp.int32).at[destination].set(route_ids)
    slot_used = jnp.zeros((experts * capacity,), jnp.bool_).at[destination].set(True)
    source_token = source_route // TOP
    zero_row = jnp.zeros((), jnp.bfloat16)
    send_rows = jnp.where(slot_used[:, None], moe_in[source_token], zero_row).reshape(
        owners, per_owner, capacity, D
    )
    received = lax.all_to_all(send_rows, "expert", split_axis=0, concat_axis=0, tiled=True)
    hidden_pre = jnp.einsum("sicd,idf->sicf", received, in_full, preferred_element_type=jnp.float32)
    gate_part = hidden_pre[..., :FF]
    up_part = hidden_pre[..., FF:]
    activated, gelu_pull = jax.vjp(gelu_tanh, gate_part)
    product = (activated * up_part).astype(jnp.bfloat16)
    expert_rows = jnp.einsum(
        "sicf,ifd->sicd", product, out_full, preferred_element_type=jnp.float32
    ).astype(jnp.bfloat16)
    returned = lax.all_to_all(
        expert_rows, "expert", split_axis=0, concat_axis=0, tiled=True
    ).reshape(experts * capacity, D)
    routed = returned[destination].reshape(rows_count, TOP, D)
    block_out = residual_mid + jnp.sum(gate_weights[:, :, None] * routed, 1)
    mixed_out = block_out.astype(jnp.bfloat16)
    upstream = cotangent.astype(jnp.float32)
    gate_grad = jnp.einsum("tjd,td->tj", routed, cotangent, preferred_element_type=jnp.float32)
    picked_grad = gate_weights * (gate_grad - jnp.sum(gate_weights * gate_grad, -1, keepdims=True))
    logits_grad = jnp.sum(jnp.where(route_hot, picked_grad[:, :, None], 0.0), 1).astype(
        jnp.bfloat16
    )
    rows_grad = (
        (gate_weights[:, :, None] * upstream[:, None, :])
        .astype(jnp.bfloat16)
        .reshape(rows_count * TOP, D)
    )
    send_grad = jnp.where(slot_used[:, None], rows_grad[source_route], zero_row).reshape(
        owners, per_owner, capacity, D
    )
    received_grad = lax.all_to_all(send_grad, "expert", split_axis=0, concat_axis=0, tiled=True)
    product_grad = jnp.einsum(
        "sicd,ifd->sicf", received_grad, out_full, preferred_element_type=jnp.float32
    )
    out_weight_grad = jnp.einsum(
        "sicf,sicd->ifd", product, received_grad, preferred_element_type=jnp.float32
    )
    gate_part_grad = gelu_pull(product_grad * up_part)[0]
    up_part_grad = product_grad * activated
    hidden_grad = jnp.concatenate([gate_part_grad, up_part_grad], -1).astype(jnp.bfloat16)
    in_weight_grad = jnp.einsum(
        "sicd,sicf->idf", received, hidden_grad, preferred_element_type=jnp.float32
    )
    input_rows_grad = jnp.einsum(
        "sicf,idf->sicd", hidden_grad, in_full, preferred_element_type=jnp.float32
    ).astype(jnp.bfloat16)
    returned_grad = lax.all_to_all(
        input_rows_grad, "expert", split_axis=0, concat_axis=0, tiled=True
    ).reshape(experts * capacity, D)
    moe_in_grad = jnp.sum(
        returned_grad[destination].reshape(rows_count, TOP, D).astype(jnp.float32), 1
    )
    gain_two_grad = jnp.sum(moe_in_grad * normed_two, 0)
    scaled_two = moe_in_grad * gain_moe
    mid_grad = upstream + inv_two * (
        scaled_two - normed_two * jnp.mean(scaled_two * normed_two, -1, keepdims=True)
    )
    attn_out_grad = mid_grad.astype(jnp.bfloat16)
    output_weight_grad = jnp.einsum(
        "tc,td->cd", attended, attn_out_grad, preferred_element_type=jnp.float32
    )
    attended_grad = jnp.einsum(
        "td,cd->tc", attn_out_grad, output_full, preferred_element_type=jnp.float32
    )
    attended_grad = attended_grad.astype(jnp.bfloat16).reshape(
        rows_count, KV_HEADS, groups, HEAD_DIM
    )
    probs_again = jnp.exp(score_table() - log_sum)
    prob_grad = jnp.einsum(
        "tkgd,skd->kgts", attended_grad, values_in, preferred_element_type=jnp.float32
    )
    delta_sum = jnp.sum(probs_again * prob_grad, -1, keepdims=True)
    score_grad = (probs_again * (prob_grad - delta_sum)).astype(jnp.bfloat16)
    values_grad = jnp.einsum(
        "kgts,tkgd->skd",
        probs_again.astype(jnp.bfloat16),
        attended_grad,
        preferred_element_type=jnp.float32,
    )
    queries_grad = (
        jnp.einsum("kgts,skd->tkgd", score_grad, keys_rot, preferred_element_type=jnp.float32)
        * score_scale
    )
    keys_grad = (
        jnp.einsum("kgts,tkgd->skd", score_grad, queries, preferred_element_type=jnp.float32)
        * score_scale
    )
    query_raw_grad = rotate_back(
        queries_grad.reshape(rows_count, HEADS, HEAD_DIM), cos_table, sin_table
    )
    query_raw_grad = query_raw_grad.astype(jnp.bfloat16).reshape(rows_count, HEADS * HEAD_DIM)
    key_raw_grad = (
        rotate_back(keys_grad, cos_table, sin_table)
        .astype(jnp.bfloat16)
        .reshape(rows_count, width_kv)
    )
    keyvalue_grad = jnp.concatenate(
        [key_raw_grad, values_grad.astype(jnp.bfloat16).reshape(rows_count, width_kv)], -1
    )
    query_weight_grad = jnp.einsum(
        "tc,tf->cf", attn_in, query_raw_grad, preferred_element_type=jnp.float32
    )
    keyvalue_weight_grad = jnp.einsum(
        "tc,tf->cf", attn_in, keyvalue_grad, preferred_element_type=jnp.float32
    )
    attn_in_grad = jnp.einsum(
        "tf,cf->tc", query_raw_grad, query_full, preferred_element_type=jnp.float32
    )
    attn_in_grad = attn_in_grad + jnp.einsum(
        "tf,cf->tc", keyvalue_grad, keyvalue_full, preferred_element_type=jnp.float32
    )
    gain_one_grad = jnp.sum(attn_in_grad * normed_one, 0)
    scaled_one = attn_in_grad * gain_attn
    tokens_grad = mid_grad + inv_one * (
        scaled_one - normed_one * jnp.mean(scaled_one * normed_one, -1, keepdims=True)
    )
    tokens_grad = tokens_grad + jnp.einsum(
        "te,ce->tc", logits_grad, router_full, preferred_element_type=jnp.float32
    )
    router_weight_grad = jnp.einsum(
        "tc,te->ce", tokens, logits_grad, preferred_element_type=jnp.float32
    )
    gains_grad = jnp.stack([gain_one_grad, gain_two_grad], 0)
    reduced = (
        lax.psum_scatter(query_weight_grad, ("dp", "expert"), scatter_dimension=0, tiled=True),
        lax.psum_scatter(keyvalue_weight_grad, ("dp", "expert"), scatter_dimension=0, tiled=True),
        lax.psum_scatter(output_weight_grad, ("dp", "expert"), scatter_dimension=0, tiled=True),
        lax.psum_scatter(router_weight_grad, ("dp", "expert"), scatter_dimension=0, tiled=True),
        lax.psum_scatter(gains_grad, ("dp", "expert"), scatter_dimension=1, tiled=True),
    )
    expert_sums = (
        lax.psum_scatter(
            in_weight_grad.astype(jnp.bfloat16), "dp", scatter_dimension=1, tiled=True
        ).astype(jnp.float32),
        lax.psum_scatter(
            out_weight_grad.astype(jnp.bfloat16), "dp", scatter_dimension=1, tiled=True
        ).astype(jnp.float32),
    )
    rates = learning_rates()
    query_upd = adam_update(query_weight, query_first, query_second, reduced[0], rates[0], DECAY)
    keyvalue_upd = adam_update(
        keyvalue_weight, keyvalue_first, keyvalue_second, reduced[1], rates[1], DECAY
    )
    output_upd = adam_update(
        output_weight, output_first, output_second, reduced[2], rates[2], DECAY
    )
    router_upd = adam_update(
        router_weight, router_first, router_second, reduced[3], rates[3], DECAY
    )
    gains_upd = adam_update(norm_gains, gains_first, gains_second, reduced[4], rates[4], 0.0)
    in_upd = adam_update(
        expert_in, expert_in_first, expert_in_second, expert_sums[0], rates[5], DECAY
    )
    out_upd = adam_update(
        expert_out, expert_out_first, expert_out_second, expert_sums[1], rates[6], DECAY
    )
    return (
        mixed_out,
        tokens_grad,
        query_upd[0],
        query_upd[1],
        query_upd[2],
        keyvalue_upd[0],
        keyvalue_upd[1],
        keyvalue_upd[2],
        output_upd[0],
        output_upd[1],
        output_upd[2],
        router_upd[0],
        router_upd[1],
        router_upd[2],
        gains_upd[0],
        gains_upd[1],
        gains_upd[2],
        in_upd[0],
        in_upd[1],
        in_upd[2],
        out_upd[0],
        out_upd[1],
        out_upd[2],
    )


def flip(mask):
    return [(i, i ^ mask) for i in range(8)]


ACROSS_X, ACROSS_Y, ACROSS_CORE = flip(2), flip(4), flip(1)
FORWARD = [(i, i ^ (4 if i & 1 else 2)) for i in range(8)]


def after(value, *earlier):
    return lax.optimization_barrier((value, *earlier))[0]


def to_x(value):
    return lax.ppermute(value, "expert", ACROSS_X)


def to_y(value):
    return lax.ppermute(value, "expert", ACROSS_Y)


def to_core(value):
    return lax.ppermute(value, "expert", ACROSS_CORE)


def forward(value):
    return lax.ppermute(value, "expert", FORWARD)


def gather_plane(value, core):
    from_x, from_y = to_x(value), to_y(value)
    from_core = to_core(value)
    from_far = forward(jnp.where(core == 0, from_y, from_x))
    return [
        value,
        from_core,
        from_x,
        to_core(from_x),
        from_y,
        to_core(from_y),
        from_far,
        to_core(from_far),
    ]


def add_low(*terms):
    total = terms[0].astype(jnp.float32)
    for term in terms[1:]:
        total = total + term.astype(jnp.float32)
    return total.astype(jnp.bfloat16)


def scatter_plane(parts, core):
    far = add_low(parts[6], to_core(parts[7]))
    relayed = forward(far)
    by_x = add_low(parts[2], to_core(parts[3]))
    by_y = add_low(parts[4], to_core(parts[5]))
    own = add_low(parts[0], to_core(parts[1]))
    zero = jnp.zeros((), jnp.bfloat16)
    by_x = add_low(by_x, jnp.where(core == 1, relayed, zero))
    by_y = add_low(by_y, jnp.where(core == 0, relayed, zero))
    return own, to_x(by_x), to_y(by_y)


def gather_column(value, ring):
    values = [value]
    for _ in range(len(ring) - 1):
        values.append(lax.ppermute(values[-1], "dp", ring))
    return values


def scatter_column(value, ring, place):
    count = len(ring)
    rows = value.shape[0] // count

    def piece(shard):
        return lax.dynamic_slice_in_dim(value, (shard % count) * rows, rows, 0)

    moving = piece(place + count - 1)
    for step in range(count - 2):
        moving = add_low(lax.ppermute(moving, "dp", ring), piece(place + count - 2 - step))
    return lax.ppermute(moving, "dp", ring).astype(jnp.float32) + piece(place).astype(jnp.float32)


def anywhere():
    return pl.BlockSpec(memory_space=pl.ANY)


def scalars():
    return pl.BlockSpec(memory_space=pltpu.SMEM)


def join_kernel(count, pieces, start_ref, *refs):
    sources, joined, sems = refs[:count], refs[count], refs[count + 1]
    copies = []
    for i in range(count):
        for p in range(pieces):
            rows = sources[i].shape[1]
            at = pl.multiple_of(start_ref[i * pieces + p], 16)
            copies.append(
                pltpu.make_async_copy(
                    sources[i].at[p], joined.at[pl.ds(at, rows)], sems.at[i * pieces + p]
                )
            )
    for copy in copies:
        copy.start()
    for copy in copies:
        copy.wait()


def join_rows(sources, starts, total):
    count, pieces = len(sources), sources[0].shape[0]
    columns, dtype = sources[0].shape[2], sources[0].dtype
    size = total * columns * dtype.itemsize
    return pl.pallas_call(
        functools.partial(join_kernel, count, pieces),
        out_shape=jax.ShapeDtypeStruct((total, columns), dtype),
        in_specs=[scalars()] + [anywhere()] * count,
        out_specs=pl.BlockSpec(memory_space=pltpu.VMEM),
        scratch_shapes=[pltpu.SemaphoreType.DMA((count * pieces,))],
        compiler_params=pltpu.CompilerParams(vmem_limit_bytes=16 << 20),
        cost_estimate=pl.CostEstimate(flops=0, bytes_accessed=2 * size, transcendentals=0),
        name="join_rows",
    )(starts, *sources)


def wide_dot(left, right):
    return lax.dot_general(
        left, right, (((1,), (1,)), ((), ())), preferred_element_type=jnp.float32
    )


def tall_dot(left, right):
    return lax.dot_general(
        left, right, (((0,), (0,)), ((), ())), preferred_element_type=jnp.float32
    )


def load_weight(chunks, place_ref, buffer, sems):
    rows = chunks[0].shape[0]
    copies = [
        pltpu.make_async_copy(
            chunk, buffer.at[pl.ds(pl.multiple_of(place_ref[p] * rows, 64), rows)], sems.at[p]
        )
        for p, chunk in enumerate(chunks)
    ]
    for copy in copies:
        copy.start()
    return copies


LANES = 256


def hidden_kernel(count, tokens_count, place_ref, *refs):
    rows_in, chunks = refs[:count], refs[count : count + 4]
    slopes, products = refs[count + 4 : 2 * count + 4], refs[2 * count + 4 : 3 * count + 4]
    weight, sems = refs[3 * count + 4 :]
    for copy in load_weight(chunks, place_ref, weight, sems):
        copy.wait()
    for rows_ref, slope_ref, product_ref in zip(rows_in, slopes, products):
        for at in range(0, FF, LANES):
            rows = rows_ref[:tokens_count, :]
            gate = jnp.dot(
                rows, weight[:, at : at + LANES], preferred_element_type=jnp.float32
            )
            up = jnp.dot(
                rows, weight[:, FF + at : FF + at + LANES], preferred_element_type=jnp.float32
            )
            square = gate * gate
            bend = jnp.tanh(0.7978845608028654 * gate * (1.0 + 0.044715 * square))
            half = 0.5 + 0.5 * bend
            slope = half + 0.5 * gate * (1.0 - bend * bend) * (
                0.7978845608028654 + 0.10703222440890037 * square
            )
            active = gate * half
            slope_ref[:, at : at + LANES] = (up * slope).astype(jnp.bfloat16)
            slope_ref[:, FF + at : FF + at + LANES] = active.astype(jnp.bfloat16)
            product_ref[:, at : at + LANES] = (active * up).astype(jnp.bfloat16)


def hidden_call(rows_in, chunks, places, tokens_count):
    count = len(rows_in)
    whole = pl.BlockSpec(memory_space=pltpu.VMEM)
    shapes = [jax.ShapeDtypeStruct((tokens_count, 2 * FF), jnp.bfloat16)] * count
    shapes += [jax.ShapeDtypeStruct((tokens_count, FF), jnp.bfloat16)] * count
    flops = count * tokens_count * D * 4 * FF
    outs = pl.pallas_call(
        functools.partial(hidden_kernel, count, tokens_count),
        out_shape=shapes,
        in_specs=[scalars()] + [whole] * count + [anywhere()] * 4,
        out_specs=[whole] * (2 * count),
        scratch_shapes=[
            pltpu.VMEM((D, 2 * FF), jnp.bfloat16),
            pltpu.SemaphoreType.DMA((4,)),
        ],
        compiler_params=pltpu.CompilerParams(vmem_limit_bytes=32 << 20),
        cost_estimate=pl.CostEstimate(
            flops=flops, bytes_accessed=20 << 20, transcendentals=count * tokens_count * FF
        ),
        name="expert_hidden",
    )(places, *rows_in, *chunks)
    return outs[:count], outs[count:]


def spread(row, tokens_count):
    return jnp.transpose(jnp.broadcast_to(row, (128, tokens_count)))


def expert_row(block, expert):
    third = block.shape[1] // 3
    index = lax.broadcasted_iota(jnp.int32, block.shape, 0)
    row = jnp.sum(jnp.where(index == expert, block.astype(jnp.float32), 0.0), 0, keepdims=True)
    return row[:, :third] + row[:, third : 2 * third] + row[:, 2 * third :]


def split_row(row):
    high = row.astype(jnp.bfloat16)
    rest = row - high.astype(jnp.float32)
    middle = rest.astype(jnp.bfloat16)
    low = (rest - middle.astype(jnp.float32)).astype(jnp.bfloat16)
    return jnp.concatenate(
        [high.astype(jnp.float32), middle.astype(jnp.float32), low.astype(jnp.float32)], 1
    )


def pull_kernel(count, tokens_count, place_ref, *refs):
    gates, cots, slopes, products = (refs[i * count : (i + 1) * count] for i in range(4))
    in_chunks, out_chunks = refs[4 * count : 4 * count + 4], refs[4 * count + 4 : 4 * count + 8]
    refs = refs[4 * count + 8 :]
    row_grads, hidden_grads, gated = (refs[i * count : (i + 1) * count] for i in range(3))
    in_weight, out_weight, sems = refs[3 * count :]
    expert = place_ref[4]
    out_copies = load_weight(out_chunks, place_ref, out_weight, sems.at[0])
    in_copies = load_weight(in_chunks, place_ref, in_weight, sems.at[1])
    for copy in out_copies:
        copy.wait()
    for i in range(count):
        weights = spread(expert_row(gates[i][...], expert), tokens_count)
        weights = jnp.concatenate([weights] * (LANES // 128), 1)
        gate_grad = jnp.zeros((tokens_count, 1), jnp.float32)
        for at in range(0, FF, LANES):
            pulled = wide_dot(cots[i][...], out_weight[at : at + LANES, :])
            product = products[i][:, at : at + LANES].astype(jnp.float32)
            gate_grad = gate_grad + jnp.sum(pulled * product, 1, keepdims=True)
            gated[i][:, at : at + LANES] = (product * weights).astype(jnp.bfloat16)
            pulled = pulled * weights
            for base in (at, FF + at):
                slope = slopes[i][:, base : base + LANES].astype(jnp.float32)
                hidden_grads[i][:, base : base + LANES] = (pulled * slope).astype(jnp.bfloat16)
        row = jnp.transpose(jnp.broadcast_to(gate_grad, (tokens_count, 128)))[:1, :]
        parts = jnp.broadcast_to(split_row(row), (16, 3 * tokens_count))
        index = lax.broadcasted_iota(jnp.int32, parts.shape, 0)
        row_grads[i][tokens_count:, :] = jnp.where(index == expert, parts, 0.0).astype(jnp.bfloat16)
    for copy in in_copies:
        copy.wait()
    for i in range(count):
        for at in range(0, D, LANES):
            row_grads[i][:tokens_count, at : at + LANES] = wide_dot(
                hidden_grads[i][...], in_weight[at : at + LANES, :]
            ).astype(jnp.bfloat16)


def pull_call(packed, cots, slopes, products, in_chunks, out_chunks, places, tokens_count):
    count = len(packed)
    whole = pl.BlockSpec(memory_space=pltpu.VMEM)
    tail = pl.BlockSpec((16, D), lambda i: (tokens_count // 16, 0))
    full = lambda rows, columns: pl.BlockSpec((rows, columns), lambda i: (0, 0))
    widths = (D, 2 * FF, FF)
    heights = (tokens_count + 16, tokens_count, tokens_count)
    shapes = [
        jax.ShapeDtypeStruct((rows, columns), jnp.bfloat16)
        for rows, columns in zip(heights, widths)
        for _ in range(count)
    ]
    outs = pl.pallas_call(
        functools.partial(pull_kernel, count, tokens_count),
        grid=(1,),
        out_shape=shapes,
        in_specs=[scalars()]
        + [tail] * count
        + [full(tokens_count, D)] * count
        + [full(tokens_count, 2 * FF)] * count
        + [full(tokens_count, FF)] * count
        + [anywhere()] * 8,
        out_specs=[full(*shape.shape) for shape in shapes],
        scratch_shapes=[
            pltpu.VMEM((D, 2 * FF), jnp.bfloat16),
            pltpu.VMEM((FF, D), jnp.bfloat16),
            pltpu.SemaphoreType.DMA((2, 4)),
        ],
        compiler_params=pltpu.CompilerParams(vmem_limit_bytes=58 << 20),
        cost_estimate=pl.CostEstimate(
            flops=count * tokens_count * D * 6 * FF, bytes_accessed=32 << 20, transcendentals=0
        ),
        name="expert_pull",
    )(places, *packed, *cots, *slopes, *products, *in_chunks, *out_chunks)
    return outs[:count], outs[count : 2 * count], outs[2 * count :]


def product_kernel(count, place_ref, *refs):
    gated, chunks, rows_out = refs[:count], refs[count : count + 4], refs[count + 4 : 2 * count + 4]
    weight, sems = refs[2 * count + 4 :]
    for copy in load_weight(chunks, place_ref, weight, sems):
        copy.wait()
    for i in range(count):
        for at in range(0, D, LANES):
            rows_out[i][:, at : at + LANES] = jnp.dot(
                gated[i][...], weight[:, at : at + LANES], preferred_element_type=jnp.float32
            ).astype(jnp.bfloat16)


def product_call(gated, chunks, places):
    count, rows = len(gated), gated[0].shape[0]
    whole = pl.BlockSpec(memory_space=pltpu.VMEM)
    return pl.pallas_call(
        functools.partial(product_kernel, count),
        out_shape=[jax.ShapeDtypeStruct((rows, D), jnp.bfloat16)] * count,
        in_specs=[scalars()] + [whole] * count + [anywhere()] * 4,
        out_specs=[whole] * count,
        scratch_shapes=[
            pltpu.VMEM((FF, D), jnp.bfloat16),
            pltpu.SemaphoreType.DMA((4,)),
        ],
        compiler_params=pltpu.CompilerParams(vmem_limit_bytes=32 << 20),
        cost_estimate=pl.CostEstimate(
            flops=count * rows * D * 2 * FF, bytes_accessed=12 << 20, transcendentals=0
        ),
        name="expert_rows",
    )(places, *gated, *chunks)


def weight_grad_kernel(count, rows, *refs):
    left, right, grad = refs[:count], refs[count : 2 * count], refs[2 * count]
    total = tall_dot(left[0][:rows, :], right[0][:rows, :])
    for i in range(1, count):
        total = total + tall_dot(left[i][:rows, :], right[i][:rows, :])
    grad[...] = total.astype(grad.dtype)


def weight_grad_call(left, right, rows, tall, name):
    count = len(left)
    height, width = left[0].shape[1], right[0].shape[1]
    return pl.pallas_call(
        functools.partial(weight_grad_kernel, count, rows),
        grid=(height // tall, width // LANES),
        out_shape=jax.ShapeDtypeStruct((height, width), jnp.bfloat16),
        in_specs=[pl.BlockSpec((rows, tall), lambda i, j: (0, i))] * count
        + [pl.BlockSpec((rows, LANES), lambda i, j: (0, j))] * count,
        out_specs=pl.BlockSpec((tall, LANES), lambda i, j: (i, j)),
        compiler_params=pltpu.CompilerParams(vmem_limit_bytes=48 << 20),
        cost_estimate=pl.CostEstimate(
            flops=count * rows * height * width * 2,
            bytes_accessed=count * rows * (height + width) * 2 + height * width * 2,
            transcendentals=0,
        ),
        name=name,
    )(*left, *right)


def plane_shards(
    tokens,
    cotangent,
    routes,
    doc_lengths,
    query_weight,
    query_first,
    query_second,
    keyvalue_weight,
    keyvalue_first,
    keyvalue_second,
    output_weight,
    output_first,
    output_second,
    router_weight,
    router_first,
    router_second,
    norm_gains,
    gains_first,
    gains_second,
    expert_in,
    expert_in_first,
    expert_in_second,
    expert_out,
    expert_out_first,
    expert_out_second,
):
    rows_count = tokens.shape[0]
    experts = router_weight.shape[1]
    columns_dp, owners = lax.axis_size("dp"), lax.axis_size("expert")
    dp_index, expert_index = lax.axis_index("dp"), lax.axis_index("expert")
    core = expert_index & 1
    ring = [(i, (i + 1) % columns_dp) for i in range(columns_dp)]
    shard = query_weight.shape[0]
    groups = HEADS // KV_HEADS
    width_q = HEADS * HEAD_DIM
    width_kv = KV_HEADS * HEAD_DIM
    width_qkv = width_q + 2 * width_kv
    score_scale = HEAD_DIM ** (-0.5)
    low = jnp.bfloat16
    places = (dp_index - jnp.arange(columns_dp, dtype=jnp.int32)) % columns_dp
    starts = (
        (expert_index ^ jnp.arange(owners, dtype=jnp.int32))[:, None] + places[None, :] * owners
    ).reshape(-1) * shard
    places = jnp.concatenate([places, expert_index[None]]).astype(jnp.int32)

    early = jnp.concatenate(
        [
            query_weight.astype(low),
            keyvalue_weight.astype(low),
            router_weight.astype(low),
            norm_gains.T.astype(low),
            jnp.zeros((shard, 128 - experts - 2), low),
        ],
        1,
    )
    early_column = gather_column(early, ring)
    late_column = gather_column(after(output_weight.astype(low), early_column[-1]), ring)
    in_chunks = gather_column(after(expert_in[0].astype(low), late_column[-1]), ring)
    out_chunks = gather_column(after(expert_out[0].astype(low), in_chunks[-1]), ring)
    early_plane = gather_plane(jnp.stack(early_column), core)
    late_plane = gather_plane(after(jnp.stack(late_column), early_plane[6]), core)
    cot_blocks = gather_plane(after(cotangent, late_plane[6]), core)

    early_full = join_rows(early_plane, starts, D)
    query_full = early_full[:, :width_q]
    keyvalue_full = early_full[:, width_q:width_qkv]
    router_full = early_full[:, width_qkv : width_qkv + experts]
    gain_attn = early_full[:, width_qkv + experts].astype(jnp.float32)
    gain_moe = early_full[:, width_qkv + experts + 1].astype(jnp.float32)
    output_full = join_rows(late_plane, starts, D)

    cos_table, sin_table, allowed = doc_tables(doc_lengths[0], rows_count)
    inputs = tokens.astype(jnp.float32)
    inv_one = lax.rsqrt(jnp.mean(inputs * inputs, -1, keepdims=True) + EPS)
    normed_one = inputs * inv_one
    attn_in = (normed_one * gain_attn).astype(low)
    query_raw = jnp.dot(attn_in, query_full, preferred_element_type=jnp.float32)
    keyvalue_raw = jnp.dot(attn_in, keyvalue_full, preferred_element_type=jnp.float32)
    queries = (
        rotate(query_raw.reshape(rows_count, HEADS, HEAD_DIM), cos_table, sin_table)
        .astype(low)
        .reshape(rows_count, KV_HEADS, groups, HEAD_DIM)
    )
    keys_rot = rotate(
        keyvalue_raw[:, :width_kv].reshape(rows_count, KV_HEADS, HEAD_DIM), cos_table, sin_table
    ).astype(low)
    values_in = keyvalue_raw[:, width_kv:].reshape(rows_count, KV_HEADS, HEAD_DIM).astype(low)

    def score_table():
        raw_scores = (
            jnp.einsum("tkgd,skd->kgts", queries, keys_rot, preferred_element_type=jnp.float32)
            * score_scale
        )
        return jnp.where(allowed[None, None], raw_scores, NEG)

    scores = score_table()
    row_max = jnp.max(scores, -1, keepdims=True)
    exponent = jnp.exp(scores - row_max)
    totals = jnp.sum(exponent, -1, keepdims=True)
    probabilities = exponent / totals
    log_sum = row_max + jnp.log(totals)
    attended = jnp.einsum(
        "kgts,skd->tkgd", probabilities.astype(low), values_in, preferred_element_type=jnp.float32
    )
    attended = attended.reshape(rows_count, HEADS * HEAD_DIM).astype(low)
    residual_mid = inputs + jnp.dot(attended, output_full, preferred_element_type=jnp.float32)
    inv_two = lax.rsqrt(jnp.mean(residual_mid * residual_mid, -1, keepdims=True) + EPS)
    normed_two = residual_mid * inv_two
    moe_in = (normed_two * gain_moe).astype(low)

    logits = jnp.dot(tokens, router_full, preferred_element_type=jnp.float32)
    expert_ids = jnp.arange(experts, dtype=jnp.int32)
    routed = jnp.any(routes[:, :, None] == expert_ids[None, None, :], 1)
    peak = jnp.max(jnp.where(routed, logits, NEG), -1, keepdims=True)
    gates = jnp.where(routed, jnp.exp(logits - peak), 0.0)
    gates = gates / jnp.sum(gates, -1, keepdims=True)
    gate_rows = gates.T
    high = lax.reduce_precision(gate_rows, 8, 7)
    middle = lax.reduce_precision(gate_rows - high, 8, 7)
    gate_parts = jnp.concatenate([high, middle, gate_rows - high - middle], 1).astype(low)
    packed = jnp.concatenate([moe_in, gate_parts, jnp.zeros((16 - experts, D), low)], 0)
    packed_blocks = gather_plane(after(packed, cot_blocks[6]), core)

    slopes, products = [None] * 8, [None] * 8
    for k in range(0, 8, 2):
        slopes[k : k + 2], products[k : k + 2] = hidden_call(
            packed_blocks[k : k + 2], in_chunks, places, rows_count
        )
    row_grads, hidden_grads, gated = [None] * 8, [None] * 8, [None] * 8
    for k in (6, 4, 2, 0):
        pair = slice(k, k + 2)
        row_grads[pair], hidden_grads[pair], gated[pair] = pull_call(
            packed_blocks[pair],
            cot_blocks[pair],
            slopes[pair],
            products[pair],
            in_chunks,
            out_chunks,
            places,
            rows_count,
        )
    out_weight_grad = weight_grad_call(gated, cot_blocks, rows_count, FF, "expert_out_grad")
    in_weight_grad = weight_grad_call(
        packed_blocks, hidden_grads, rows_count, FF, "expert_in_grad"
    )
    expert_out_sum = scatter_column(out_weight_grad, ring, dp_index)
    expert_in_sum = scatter_column(after(in_weight_grad, expert_out_sum), ring, dp_index)
    pulled = scatter_plane(row_grads, core)
    pulled = sum([term.astype(jnp.float32) for term in pulled])
    rows_out = [None] * 8
    for k in (6, 4, 2, 0):
        rows_out[k : k + 2] = product_call(gated[k : k + 2], out_chunks, places)
    mixed_terms = scatter_plane(rows_out, core)
    block_out = residual_mid + sum([term.astype(jnp.float32) for term in mixed_terms])
    mixed_out = block_out.astype(low)

    gate_grad = pulled[rows_count : rows_count + experts]
    gate_grad = (
        gate_grad[:, :rows_count]
        + gate_grad[:, rows_count : 2 * rows_count]
        + gate_grad[:, 2 * rows_count :]
    ).T
    logits_grad = gates * (gate_grad - jnp.sum(gates * gate_grad, -1, keepdims=True))
    logits_grad = logits_grad.astype(low)
    moe_in_grad = pulled[:rows_count]
    upstream = cotangent.astype(jnp.float32)
    gain_two_grad = jnp.sum(moe_in_grad * normed_two, 0)
    scaled_two = moe_in_grad * gain_moe
    mid_grad = upstream + inv_two * (
        scaled_two - normed_two * jnp.mean(scaled_two * normed_two, -1, keepdims=True)
    )
    attn_out_grad = mid_grad.astype(low)
    output_weight_grad = jnp.einsum(
        "tc,td->cd", attended, attn_out_grad, preferred_element_type=jnp.float32
    )
    attended_grad = jnp.einsum(
        "td,cd->tc", attn_out_grad, output_full, preferred_element_type=jnp.float32
    )
    attended_grad = attended_grad.astype(low).reshape(rows_count, KV_HEADS, groups, HEAD_DIM)
    probs_again = jnp.exp(score_table() - log_sum)
    prob_grad = jnp.einsum(
        "tkgd,skd->kgts", attended_grad, values_in, preferred_element_type=jnp.float32
    )
    delta_sum = jnp.sum(probs_again * prob_grad, -1, keepdims=True)
    score_grad = (probs_again * (prob_grad - delta_sum)).astype(low)
    values_grad = jnp.einsum(
        "kgts,tkgd->skd", probs_again.astype(low), attended_grad, preferred_element_type=jnp.float32
    )
    queries_grad = (
        jnp.einsum("kgts,skd->tkgd", score_grad, keys_rot, preferred_element_type=jnp.float32)
        * score_scale
    )
    keys_grad = (
        jnp.einsum("kgts,tkgd->skd", score_grad, queries, preferred_element_type=jnp.float32)
        * score_scale
    )
    query_raw_grad = rotate_back(
        queries_grad.reshape(rows_count, HEADS, HEAD_DIM), cos_table, sin_table
    )
    query_raw_grad = query_raw_grad.astype(low).reshape(rows_count, width_q)
    key_raw_grad = rotate_back(keys_grad, cos_table, sin_table).astype(low)
    raw_grad = jnp.concatenate(
        [
            query_raw_grad,
            key_raw_grad.reshape(rows_count, width_kv),
            values_grad.astype(low).reshape(rows_count, width_kv),
        ],
        -1,
    )
    early_weight_grad = jnp.einsum(
        "tc,tf->cf", attn_in, raw_grad, preferred_element_type=jnp.float32
    )
    attn_in_grad = jnp.einsum(
        "tf,cf->tc", raw_grad, early_full[:, :width_qkv], preferred_element_type=jnp.float32
    )
    gain_one_grad = jnp.sum(attn_in_grad * normed_one, 0)
    scaled_one = attn_in_grad * gain_attn
    tokens_grad = mid_grad + inv_one * (
        scaled_one - normed_one * jnp.mean(scaled_one * normed_one, -1, keepdims=True)
    )
    tokens_grad = tokens_grad + jnp.einsum(
        "te,ce->tc", logits_grad, router_full, preferred_element_type=jnp.float32
    )
    router_weight_grad = jnp.einsum(
        "tc,te->ce", tokens, logits_grad, preferred_element_type=jnp.float32
    )

    def reduce_rows(grad):
        parts = grad.astype(low).reshape(columns_dp, owners, shard, grad.shape[1])
        parts = [
            lax.dynamic_index_in_dim(parts, expert_index ^ k, 1, keepdims=False)
            for k in range(owners)
        ]
        return scatter_column(add_low(*scatter_plane(parts, core)), ring, dp_index)[0]

    output_sum = reduce_rows(output_weight_grad)
    early_sum = reduce_rows(
        jnp.concatenate(
            [
                early_weight_grad,
                router_weight_grad,
                gain_one_grad[:, None],
                gain_two_grad[:, None],
                jnp.zeros((D, 128 - experts - 2), jnp.float32),
            ],
            1,
        )
    )
    at = width_qkv
    sums = (
        early_sum[:, :width_q],
        early_sum[:, width_q:at],
        output_sum,
        early_sum[:, at : at + experts],
        early_sum[:, at + experts : at + experts + 2].T,
        expert_in_sum[None],
        expert_out_sum[None],
    )
    weights = (
        (query_weight, query_first, query_second),
        (keyvalue_weight, keyvalue_first, keyvalue_second),
        (output_weight, output_first, output_second),
        (router_weight, router_first, router_second),
        (norm_gains, gains_first, gains_second),
        (expert_in, expert_in_first, expert_in_second),
        (expert_out, expert_out_first, expert_out_second),
    )
    updates = []
    for state, grad, rate, decay in zip(
        weights, sums, learning_rates(), (DECAY, DECAY, DECAY, DECAY, 0.0, DECAY, DECAY)
    ):
        updates.extend(adam_update(*state, grad, rate, decay))
    return (mixed_out, tokens_grad, *updates)


def solution(mesh):
    in_specs = (
        P(("dp", "expert"), None),
        P(("dp", "expert"), None),
        P(("dp", "expert"), None),
        P(("dp", "expert"), None),
        P(("dp", "expert"), None),
        P(("dp", "expert"), None),
        P(("dp", "expert"), None),
        P(("dp", "expert"), None),
        P(("dp", "expert"), None),
        P(("dp", "expert"), None),
        P(("dp", "expert"), None),
        P(("dp", "expert"), None),
        P(("dp", "expert"), None),
        P(("dp", "expert"), None),
        P(("dp", "expert"), None),
        P(("dp", "expert"), None),
        P(None, ("dp", "expert")),
        P(None, ("dp", "expert")),
        P(None, ("dp", "expert")),
        P("expert", "dp", None),
        P("expert", "dp", None),
        P("expert", "dp", None),
        P("expert", "dp", None),
        P("expert", "dp", None),
        P("expert", "dp", None),
    )
    out_specs = (
        P(("dp", "expert"), None),
        P(("dp", "expert"), None),
        P(("dp", "expert"), None),
        P(("dp", "expert"), None),
        P(("dp", "expert"), None),
        P(("dp", "expert"), None),
        P(("dp", "expert"), None),
        P(("dp", "expert"), None),
        P(("dp", "expert"), None),
        P(("dp", "expert"), None),
        P(("dp", "expert"), None),
        P(("dp", "expert"), None),
        P(("dp", "expert"), None),
        P(("dp", "expert"), None),
        P(None, ("dp", "expert")),
        P(None, ("dp", "expert")),
        P(None, ("dp", "expert")),
        P("expert", "dp", None),
        P("expert", "dp", None),
        P("expert", "dp", None),
        P("expert", "dp", None),
        P("expert", "dp", None),
        P("expert", "dp", None),
    )
    body = plane_shards if mesh.shape["expert"] == 8 else shards
    return jax.shard_map(body, mesh=mesh, in_specs=in_specs, out_specs=out_specs, check_vma=False)
```

```python
import functools

import jax
import jax.numpy as jnp
from jax import lax
from jax.experimental import pallas as pl
from jax.experimental.pallas import tpu as pltpu
from jax.sharding import PartitionSpec as P

D = 1536
FF = 768
HEADS = 12
KV_HEADS = 2
HEAD_DIM = 128
TOP = 4
STEP = 10


EPS = 1e-06
NEG = -1e30
BETA_ONE = 0.9
BETA_TWO = 0.999
ADAM_EPS = 1e-08
DECAY = 0.1
ROPE_BASE = 10000.0
RATE_SCALE = 2.5
GAIN_RATE = 0.6


def doc_tables(lengths, rows_count):
    position = jnp.arange(rows_count, dtype=jnp.int32)
    doc_ends = jnp.cumsum(lengths)
    doc_starts = doc_ends - lengths
    doc_index = jnp.sum((position[:, None] >= doc_ends[None, :]).astype(jnp.int32), 1)
    doc_hot = doc_index[:, None] == jnp.arange(lengths.shape[0], dtype=jnp.int32)[None, :]
    start_of = jnp.sum(jnp.where(doc_hot, doc_starts[None, :], 0), 1)
    offset = (position - start_of).astype(jnp.float32)
    frequency = ROPE_BASE ** (-2.0 * jnp.arange(HEAD_DIM // 2, dtype=jnp.float32) / HEAD_DIM)
    angles = offset[:, None] * frequency[None, :]
    allowed = (doc_index[:, None] == doc_index[None, :]) & (position[None, :] <= position[:, None])
    return (jnp.cos(angles), jnp.sin(angles), allowed)


def rotate(values, cos_table, sin_table):
    half_width = values.shape[-1] // 2
    first_half = values[..., :half_width]
    second_half = values[..., half_width:]
    cosine = cos_table[:, None, :]
    sine_part = sin_table[:, None, :]
    return jnp.concatenate(
        [
            first_half * cosine - second_half * sine_part,
            second_half * cosine + first_half * sine_part,
        ],
        -1,
    )


def rotate_back(grads, cos_table, sin_table):
    half_width = grads.shape[-1] // 2
    first_half = grads[..., :half_width]
    second_half = grads[..., half_width:]
    cosine = cos_table[:, None, :]
    sine_part = sin_table[:, None, :]
    return jnp.concatenate(
        [
            first_half * cosine + second_half * sine_part,
            second_half * cosine - first_half * sine_part,
        ],
        -1,
    )


def gelu_tanh(values):
    return jax.nn.gelu(values, approximate=True)


def learning_rates():
    return (
        RATE_SCALE * D ** (-0.5),
        RATE_SCALE * D ** (-0.5),
        RATE_SCALE * (D // 32) ** (-0.5),
        RATE_SCALE * (4 * D) ** (-0.5),
        GAIN_RATE,
        RATE_SCALE * D ** (-0.5),
        RATE_SCALE * (FF // 8) ** (-0.5),
    )


def adam_update(weight, first, second, grad, rate, decay):
    new_first = BETA_ONE * first + (1.0 - BETA_ONE) * grad
    new_second = BETA_TWO * second + (1.0 - BETA_TWO) * grad * grad
    first_hat = new_first / (1.0 - BETA_ONE**STEP)
    second_hat = new_second / (1.0 - BETA_TWO**STEP)
    new_weight = weight - rate * (first_hat / (jnp.sqrt(second_hat) + ADAM_EPS) + decay * weight)
    return (new_first, new_second, new_weight)


def shards(
    tokens,
    cotangent,
    routes,
    doc_lengths,
    query_weight,
    query_first,
    query_second,
    keyvalue_weight,
    keyvalue_first,
    keyvalue_second,
    output_weight,
    output_first,
    output_second,
    router_weight,
    router_first,
    router_second,
    norm_gains,
    gains_first,
    gains_second,
    expert_in,
    expert_in_first,
    expert_in_second,
    expert_out,
    expert_out_first,
    expert_out_second,
):
    rows_count = tokens.shape[0]
    experts = router_weight.shape[1]
    owners = lax.axis_size("expert")
    per_owner = expert_in.shape[0]
    capacity = 3 * rows_count * TOP // (2 * experts)
    groups = HEADS // KV_HEADS
    width_kv = KV_HEADS * HEAD_DIM
    score_scale = HEAD_DIM ** (-0.5)
    query_full, keyvalue_full, output_full, router_full, gains_full = (
        lax.all_gather(query_weight.astype(jnp.bfloat16), ("dp", "expert"), axis=0, tiled=True),
        lax.all_gather(keyvalue_weight.astype(jnp.bfloat16), ("dp", "expert"), axis=0, tiled=True),
        lax.all_gather(output_weight.astype(jnp.bfloat16), ("dp", "expert"), axis=0, tiled=True),
        lax.all_gather(router_weight.astype(jnp.bfloat16), ("dp", "expert"), axis=0, tiled=True),
        lax.all_gather(norm_gains.astype(jnp.bfloat16), ("dp", "expert"), axis=1, tiled=True),
    )
    in_full, out_full = (
        lax.all_gather(expert_in.astype(jnp.bfloat16), "dp", axis=1, tiled=True),
        lax.all_gather(expert_out.astype(jnp.bfloat16), "dp", axis=1, tiled=True),
    )
    gain_attn = gains_full[0].astype(jnp.float32)
    gain_moe = gains_full[1].astype(jnp.float32)
    cos_table, sin_table, allowed = doc_tables(doc_lengths[0], rows_count)
    inputs = tokens.astype(jnp.float32)
    inv_one = lax.rsqrt(jnp.mean(inputs * inputs, -1, keepdims=True) + EPS)
    normed_one = inputs * inv_one
    attn_in = (normed_one * gain_attn).astype(jnp.bfloat16)
    query_raw = jnp.dot(attn_in, query_full, preferred_element_type=jnp.float32)
    keyvalue_raw = jnp.dot(attn_in, keyvalue_full, preferred_element_type=jnp.float32)
    queries = (
        rotate(query_raw.reshape(rows_count, HEADS, HEAD_DIM), cos_table, sin_table)
        .astype(jnp.bfloat16)
        .reshape(rows_count, KV_HEADS, groups, HEAD_DIM)
    )
    keys_rot = rotate(
        keyvalue_raw[:, :width_kv].reshape(rows_count, KV_HEADS, HEAD_DIM), cos_table, sin_table
    ).astype(jnp.bfloat16)
    values_in = (
        keyvalue_raw[:, width_kv:].reshape(rows_count, KV_HEADS, HEAD_DIM).astype(jnp.bfloat16)
    )

    def score_table():
        raw_scores = (
            jnp.einsum("tkgd,skd->kgts", queries, keys_rot, preferred_element_type=jnp.float32)
            * score_scale
        )
        return jnp.where(allowed[None, None], raw_scores, NEG)

    scores = score_table()
    row_max = jnp.max(scores, -1, keepdims=True)
    exponent = jnp.exp(scores - row_max)
    totals = jnp.sum(exponent, -1, keepdims=True)
    probabilities = exponent / totals
    log_sum = row_max + jnp.log(totals)
    attended = jnp.einsum(
        "kgts,skd->tkgd",
        probabilities.astype(jnp.bfloat16),
        values_in,
        preferred_element_type=jnp.float32,
    )
    attended = attended.reshape(rows_count, HEADS * HEAD_DIM).astype(jnp.bfloat16)
    residual_mid = inputs + jnp.dot(attended, output_full, preferred_element_type=jnp.float32)
    inv_two = lax.rsqrt(jnp.mean(residual_mid * residual_mid, -1, keepdims=True) + EPS)
    normed_two = residual_mid * inv_two
    moe_in = (normed_two * gain_moe).astype(jnp.bfloat16)
    logits = jnp.dot(tokens, router_full, preferred_element_type=jnp.float32)
    expert_ids = jnp.arange(experts, dtype=jnp.int32)
    route_hot = routes[:, :, None] == expert_ids[None, None, :]
    picked = jnp.sum(jnp.where(route_hot, logits[:, None, :], 0.0), -1)
    gate_weights = jax.nn.softmax(picked, axis=-1)
    flat_routes = routes.reshape(-1)
    flat_hot = (flat_routes[:, None] == expert_ids[None, :]).astype(jnp.int32)
    slot_index = jnp.sum((jnp.cumsum(flat_hot, 0) - 1) * flat_hot, 1)
    destination = flat_routes * capacity + slot_index
    route_ids = jnp.arange(rows_count * TOP, dtype=jnp.int32)
    source_route = jnp.zeros((experts * capacity,), jnp.int32).at[destination].set(route_ids)
    slot_used = jnp.zeros((experts * capacity,), jnp.bool_).at[destination].set(True)
    source_token = source_route // TOP
    zero_row = jnp.zeros((), jnp.bfloat16)
    send_rows = jnp.where(slot_used[:, None], moe_in[source_token], zero_row).reshape(
        owners, per_owner, capacity, D
    )
    received = lax.all_to_all(send_rows, "expert", split_axis=0, concat_axis=0, tiled=True)
    hidden_pre = jnp.einsum("sicd,idf->sicf", received, in_full, preferred_element_type=jnp.float32)
    gate_part = hidden_pre[..., :FF]
    up_part = hidden_pre[..., FF:]
    activated, gelu_pull = jax.vjp(gelu_tanh, gate_part)
    product = (activated * up_part).astype(jnp.bfloat16)
    expert_rows = jnp.einsum(
        "sicf,ifd->sicd", product, out_full, preferred_element_type=jnp.float32
    ).astype(jnp.bfloat16)
    returned = lax.all_to_all(
        expert_rows, "expert", split_axis=0, concat_axis=0, tiled=True
    ).reshape(experts * capacity, D)
    routed = returned[destination].reshape(rows_count, TOP, D)
    block_out = residual_mid + jnp.sum(gate_weights[:, :, None] * routed, 1)
    mixed_out = block_out.astype(jnp.bfloat16)
    upstream = cotangent.astype(jnp.float32)
    gate_grad = jnp.einsum("tjd,td->tj", routed, cotangent, preferred_element_type=jnp.float32)
    picked_grad = gate_weights * (gate_grad - jnp.sum(gate_weights * gate_grad, -1, keepdims=True))
    logits_grad = jnp.sum(jnp.where(route_hot, picked_grad[:, :, None], 0.0), 1).astype(
        jnp.bfloat16
    )
    rows_grad = (
        (gate_weights[:, :, None] * upstream[:, None, :])
        .astype(jnp.bfloat16)
        .reshape(rows_count * TOP, D)
    )
    send_grad = jnp.where(slot_used[:, None], rows_grad[source_route], zero_row).reshape(
        owners, per_owner, capacity, D
    )
    received_grad = lax.all_to_all(send_grad, "expert", split_axis=0, concat_axis=0, tiled=True)
    product_grad = jnp.einsum(
        "sicd,ifd->sicf", received_grad, out_full, preferred_element_type=jnp.float32
    )
    out_weight_grad = jnp.einsum(
        "sicf,sicd->ifd", product, received_grad, preferred_element_type=jnp.float32
    )
    gate_part_grad = gelu_pull(product_grad * up_part)[0]
    up_part_grad = product_grad * activated
    hidden_grad = jnp.concatenate([gate_part_grad, up_part_grad], -1).astype(jnp.bfloat16)
    in_weight_grad = jnp.einsum(
        "sicd,sicf->idf", received, hidden_grad, preferred_element_type=jnp.float32
    )
    input_rows_grad = jnp.einsum(
        "sicf,idf->sicd", hidden_grad, in_full, preferred_element_type=jnp.float32
    ).astype(jnp.bfloat16)
    returned_grad = lax.all_to_all(
        input_rows_grad, "expert", split_axis=0, concat_axis=0, tiled=True
    ).reshape(experts * capacity, D)
    moe_in_grad = jnp.sum(
        returned_grad[destination].reshape(rows_count, TOP, D).astype(jnp.float32), 1
    )
    gain_two_grad = jnp.sum(moe_in_grad * normed_two, 0)
    scaled_two = moe_in_grad * gain_moe
    mid_grad = upstream + inv_two * (
        scaled_two - normed_two * jnp.mean(scaled_two * normed_two, -1, keepdims=True)
    )
    attn_out_grad = mid_grad.astype(jnp.bfloat16)
    output_weight_grad = jnp.einsum(
        "tc,td->cd", attended, attn_out_grad, preferred_element_type=jnp.float32
    )
    attended_grad = jnp.einsum(
        "td,cd->tc", attn_out_grad, output_full, preferred_element_type=jnp.float32
    )
    attended_grad = attended_grad.astype(jnp.bfloat16).reshape(
        rows_count, KV_HEADS, groups, HEAD_DIM
    )
    probs_again = jnp.exp(score_table() - log_sum)
    prob_grad = jnp.einsum(
        "tkgd,skd->kgts", attended_grad, values_in, preferred_element_type=jnp.float32
    )
    delta_sum = jnp.sum(probs_again * prob_grad, -1, keepdims=True)
    score_grad = (probs_again * (prob_grad - delta_sum)).astype(jnp.bfloat16)
    values_grad = jnp.einsum(
        "kgts,tkgd->skd",
        probs_again.astype(jnp.bfloat16),
        attended_grad,
        preferred_element_type=jnp.float32,
    )
    queries_grad = (
        jnp.einsum("kgts,skd->tkgd", score_grad, keys_rot, preferred_element_type=jnp.float32)
        * score_scale
    )
    keys_grad = (
        jnp.einsum("kgts,tkgd->skd", score_grad, queries, preferred_element_type=jnp.float32)
        * score_scale
    )
    query_raw_grad = rotate_back(
        queries_grad.reshape(rows_count, HEADS, HEAD_DIM), cos_table, sin_table
    )
    query_raw_grad = query_raw_grad.astype(jnp.bfloat16).reshape(rows_count, HEADS * HEAD_DIM)
    key_raw_grad = (
        rotate_back(keys_grad, cos_table, sin_table)
        .astype(jnp.bfloat16)
        .reshape(rows_count, width_kv)
    )
    keyvalue_grad = jnp.concatenate(
        [key_raw_grad, values_grad.astype(jnp.bfloat16).reshape(rows_count, width_kv)], -1
    )
    query_weight_grad = jnp.einsum(
        "tc,tf->cf", attn_in, query_raw_grad, preferred_element_type=jnp.float32
    )
    keyvalue_weight_grad = jnp.einsum(
        "tc,tf->cf", attn_in, keyvalue_grad, preferred_element_type=jnp.float32
    )
    attn_in_grad = jnp.einsum(
        "tf,cf->tc", query_raw_grad, query_full, preferred_element_type=jnp.float32
    )
    attn_in_grad = attn_in_grad + jnp.einsum(
        "tf,cf->tc", keyvalue_grad, keyvalue_full, preferred_element_type=jnp.float32
    )
    gain_one_grad = jnp.sum(attn_in_grad * normed_one, 0)
    scaled_one = attn_in_grad * gain_attn
    tokens_grad = mid_grad + inv_one * (
        scaled_one - normed_one * jnp.mean(scaled_one * normed_one, -1, keepdims=True)
    )
    tokens_grad = tokens_grad + jnp.einsum(
        "te,ce->tc", logits_grad, router_full, preferred_element_type=jnp.float32
    )
    router_weight_grad = jnp.einsum(
        "tc,te->ce", tokens, logits_grad, preferred_element_type=jnp.float32
    )
    gains_grad = jnp.stack([gain_one_grad, gain_two_grad], 0)
    reduced = (
        lax.psum_scatter(query_weight_grad, ("dp", "expert"), scatter_dimension=0, tiled=True),
        lax.psum_scatter(keyvalue_weight_grad, ("dp", "expert"), scatter_dimension=0, tiled=True),
        lax.psum_scatter(output_weight_grad, ("dp", "expert"), scatter_dimension=0, tiled=True),
        lax.psum_scatter(router_weight_grad, ("dp", "expert"), scatter_dimension=0, tiled=True),
        lax.psum_scatter(gains_grad, ("dp", "expert"), scatter_dimension=1, tiled=True),
    )
    expert_sums = (
        lax.psum_scatter(
            in_weight_grad.astype(jnp.bfloat16), "dp", scatter_dimension=1, tiled=True
        ).astype(jnp.float32),
        lax.psum_scatter(
            out_weight_grad.astype(jnp.bfloat16), "dp", scatter_dimension=1, tiled=True
        ).astype(jnp.float32),
    )
    rates = learning_rates()
    query_upd = adam_update(query_weight, query_first, query_second, reduced[0], rates[0], DECAY)
    keyvalue_upd = adam_update(
        keyvalue_weight, keyvalue_first, keyvalue_second, reduced[1], rates[1], DECAY
    )
    output_upd = adam_update(
        output_weight, output_first, output_second, reduced[2], rates[2], DECAY
    )
    router_upd = adam_update(
        router_weight, router_first, router_second, reduced[3], rates[3], DECAY
    )
    gains_upd = adam_update(norm_gains, gains_first, gains_second, reduced[4], rates[4], 0.0)
    in_upd = adam_update(
        expert_in, expert_in_first, expert_in_second, expert_sums[0], rates[5], DECAY
    )
    out_upd = adam_update(
        expert_out, expert_out_first, expert_out_second, expert_sums[1], rates[6], DECAY
    )
    return (
        mixed_out,
        tokens_grad,
        query_upd[0],
        query_upd[1],
        query_upd[2],
        keyvalue_upd[0],
        keyvalue_upd[1],
        keyvalue_upd[2],
        output_upd[0],
        output_upd[1],
        output_upd[2],
        router_upd[0],
        router_upd[1],
        router_upd[2],
        gains_upd[0],
        gains_upd[1],
        gains_upd[2],
        in_upd[0],
        in_upd[1],
        in_upd[2],
        out_upd[0],
        out_upd[1],
        out_upd[2],
    )


def flip(mask):
    return [(i, i ^ mask) for i in range(8)]


ACROSS_X, ACROSS_Y, ACROSS_CORE = flip(2), flip(4), flip(1)
FORWARD = [(i, i ^ (4 if i & 1 else 2)) for i in range(8)]


def after(value, *earlier):
    return lax.optimization_barrier((value, *earlier))[0]


def hold(*values):
    return lax.optimization_barrier(values)


def to_x(value):
    return lax.ppermute(value, "expert", ACROSS_X)


def to_y(value):
    return lax.ppermute(value, "expert", ACROSS_Y)


def to_core(value):
    return lax.ppermute(value, "expert", ACROSS_CORE)


def forward(value):
    return lax.ppermute(value, "expert", FORWARD)


def gather_plane(value, core):
    from_x, from_y = to_x(value), to_y(value)
    from_core = to_core(value)
    from_far = forward(jnp.where(core == 0, from_y, from_x))
    return [
        value,
        from_core,
        from_x,
        to_core(from_x),
        from_y,
        to_core(from_y),
        from_far,
        to_core(from_far),
    ]


def add_low(*terms):
    total = terms[0].astype(jnp.float32)
    for term in terms[1:]:
        total = total + term.astype(jnp.float32)
    return total.astype(jnp.bfloat16)


def add_low_wide(*terms):
    return sum([term.astype(jnp.float32) for term in terms])


def scatter_plane(parts, core):
    far = add_low(parts[6], to_core(parts[7]))
    relayed = forward(far)
    by_x = add_low(parts[2], to_core(parts[3]))
    by_y = add_low(parts[4], to_core(parts[5]))
    own = add_low(parts[0], to_core(parts[1]))
    zero = jnp.zeros((), jnp.bfloat16)
    by_x = add_low(by_x, jnp.where(core == 1, relayed, zero))
    by_y = add_low(by_y, jnp.where(core == 0, relayed, zero))
    return own, to_x(by_x), to_y(by_y)


def gather_column(value, ring):
    values = [value]
    for _ in range(len(ring) - 1):
        values.append(lax.ppermute(values[-1], "dp", ring))
    return values


def scatter_column(value, ring, place):
    count = len(ring)
    rows = value.shape[0] // count

    def piece(shard):
        return lax.dynamic_slice_in_dim(value, (shard % count) * rows, rows, 0)

    moving = piece(place + count - 1)
    for step in range(count - 2):
        moving = add_low(lax.ppermute(moving, "dp", ring), piece(place + count - 2 - step))
    return lax.ppermute(moving, "dp", ring).astype(jnp.float32) + piece(place).astype(jnp.float32)


def scatter_pieces(pieces, ring):
    moving = pieces[1]
    for piece in pieces[2:]:
        moving = add_low(lax.ppermute(moving, "dp", ring), piece)
    return lax.ppermute(moving, "dp", ring).astype(jnp.float32) + pieces[0].astype(jnp.float32)


def anywhere():
    return pl.BlockSpec(memory_space=pl.ANY)


def scalars():
    return pl.BlockSpec(memory_space=pltpu.SMEM)


def whole():
    return pl.BlockSpec(memory_space=pltpu.VMEM)


def small_cost():
    return pl.CostEstimate(flops=1024, bytes_accessed=1024, transcendentals=0)


def load_rows(blocks, start_ref, joined, sems, column=0):
    width = joined.shape[1]
    pieces, rows = blocks[0].shape[0], blocks[0].shape[1]
    copies = []
    for i, block in enumerate(blocks):
        for p in range(pieces):
            at = pl.multiple_of(start_ref[i * pieces + p], 16)
            copies.append(
                pltpu.make_async_copy(
                    block.at[p, :, pl.ds(column, width)],
                    joined.at[pl.ds(at, rows)],
                    sems.at[i * pieces + p],
                )
            )
    for copy in copies:
        copy.start()
    return copies


def wide_dot(left, right):
    return lax.dot_general(
        left, right, (((1,), (1,)), ((), ())), preferred_element_type=jnp.float32
    )


def tall_dot(left, right):
    return lax.dot_general(
        left, right, (((0,), (0,)), ((), ())), preferred_element_type=jnp.float32
    )


def load_weight(chunks, place_ref, buffer, sems, start=True):
    total = sum([chunk.shape[0] for chunk in chunks[::4]])
    copies, offset = [], 0
    for j, chunk in enumerate(chunks):
        rows = chunk.shape[0]
        at = pl.multiple_of(place_ref[j % 4] * total + offset, 16)
        copies.append(pltpu.make_async_copy(chunk, buffer.at[pl.ds(at, rows)], sems.at[j]))
        if j % 4 == 3:
            offset += rows
    for copy in copies if start else []:
        copy.start()
    return copies


LANES = 256
WIDE = 512


def turned(values, cosine, sine):
    return values * cosine + pltpu.roll(values, HEAD_DIM // 2, 1) * sine


def fill_bias(bias, first_ref):
    row = lax.broadcasted_iota(jnp.int32, bias.shape, 0)
    column = lax.broadcasted_iota(jnp.int32, bias.shape, 1)
    bias[...] = jnp.where((column <= row) & (column >= first_ref[...]), 0.0, NEG)


def attend_kernel(
    planes, start_ref, tokens_ref, first_ref, cosine_ref, sine_ref, *refs
):
    blocks, refs = refs[:planes], refs[planes:]
    attn_in_ref, heads_ref, attended_ref, log_ref, small_ref, weight, bias, sems = refs
    rows_count = tokens_ref.shape[0]
    copies = load_rows(blocks, start_ref, weight, sems)
    fill_bias(bias, first_ref)
    inputs = tokens_ref[...].astype(jnp.float32)
    inverse = lax.rsqrt(jnp.mean(inputs * inputs, -1, keepdims=True) + EPS)
    normed = inputs * inverse
    for copy in copies:
        copy.wait()
    width_q, width_kv = HEADS * HEAD_DIM, KV_HEADS * HEAD_DIM
    width = width_q + 2 * width_kv
    small = jnp.transpose(weight[:, width:].astype(jnp.float32))
    small_ref[...] = small[:16, :]
    experts = small_ref.shape[0] - 8
    attn_in_ref[...] = (normed * small[experts : experts + 1, :]).astype(jnp.bfloat16)
    for at in range(0, width, LANES):
        raw = jnp.dot(
            attn_in_ref[...], weight[:, at : at + LANES], preferred_element_type=jnp.float32
        )
        for column in range(0, LANES, HEAD_DIM):
            values = raw[:, column : column + HEAD_DIM]
            if at + column < width_q + width_kv:
                values = turned(values, cosine_ref[...], sine_ref[...])
            heads_ref[:, at + column : at + column + HEAD_DIM] = values.astype(jnp.bfloat16)
    half = rows_count // 2
    for block in range(2):
        rows, reach = pl.ds(block * half, half), (block + 1) * half
        logs = jnp.zeros((half, 128), jnp.float32)
        lane = lax.broadcasted_iota(jnp.int32, logs.shape, 1)
        for head in range(HEADS):
            key_at = width_q + head // (HEADS // KV_HEADS) * HEAD_DIM
            value_at = key_at + width_kv
            scores = wide_dot(
                heads_ref[rows, head * HEAD_DIM : (head + 1) * HEAD_DIM],
                heads_ref[:reach, key_at : key_at + HEAD_DIM],
            )
            scores = scores * HEAD_DIM ** (-0.5) + bias[rows, :reach]
            peak = jnp.max(scores, -1, keepdims=True)
            exponent = jnp.exp(scores - peak)
            total = jnp.sum(exponent, -1, keepdims=True)
            mixed = jnp.dot(
                exponent.astype(jnp.bfloat16),
                heads_ref[:reach, value_at : value_at + HEAD_DIM],
                preferred_element_type=jnp.float32,
            )
            attended_ref[rows, head * HEAD_DIM : (head + 1) * HEAD_DIM] = (
                mixed * (1.0 / total)
            ).astype(jnp.bfloat16)
            logs = jnp.where(lane == head, peak + jnp.log(total), logs)
        log_ref[rows, :] = logs


def attend_call(starts, tokens, first, cosine, sine, blocks, width_early):
    rows_count = tokens.shape[0]
    width = (HEADS + 2 * KV_HEADS) * HEAD_DIM
    low = jnp.bfloat16
    return pl.pallas_call(
        functools.partial(attend_kernel, len(blocks)),
        out_shape=[
            jax.ShapeDtypeStruct((rows_count, D), low),
            jax.ShapeDtypeStruct((rows_count, width), low),
            jax.ShapeDtypeStruct((rows_count, HEADS * HEAD_DIM), low),
            jax.ShapeDtypeStruct((rows_count, 128), jnp.float32),
            jax.ShapeDtypeStruct((16, D), jnp.float32),
        ],
        in_specs=[scalars()] + [whole()] * 4 + [anywhere()] * len(blocks),
        out_specs=[whole()] * 5,
        scratch_shapes=[
            pltpu.VMEM((D, width_early), low),
            pltpu.VMEM((rows_count, rows_count), jnp.float32),
            pltpu.SemaphoreType.DMA((len(blocks) * blocks[0].shape[0],)),
        ],
        compiler_params=pltpu.CompilerParams(vmem_limit_bytes=62 << 20),
        cost_estimate=small_cost(),
        name="attend",
    )(starts, tokens, first, cosine, sine, *blocks)


def middle_kernel(planes, column, start_ref, tokens_ref, attended_ref, routes_ref, small_ref, *refs):
    blocks, refs = refs[:planes], refs[planes:]
    residual_ref, packed_ref, gates_ref, weight, sems = refs
    step = pl.program_id(0)
    tile = tokens_ref.shape[0]
    rows_count = packed_ref.shape[0] - 16
    experts = gates_ref.shape[0]

    @pl.when(step == 0)
    def _():
        for copy in load_rows(blocks, start_ref, weight, sems, column):
            copy.wait()

    for at in range(0, D, LANES):
        residual_ref[:, at : at + LANES] = tokens_ref[:, at : at + LANES].astype(
            jnp.float32
        ) + jnp.dot(
            attended_ref[...], weight[:, at : at + LANES], preferred_element_type=jnp.float32
        )
    residual = residual_ref[...]
    inverse = lax.rsqrt(jnp.mean(residual * residual, -1, keepdims=True) + EPS)
    rows = pl.ds(pl.multiple_of(step * tile, tile), tile)
    packed_ref[rows, :] = (
        residual * inverse * small_ref[experts + 1 : experts + 2, :]
    ).astype(jnp.bfloat16)
    logits = wide_dot(small_ref[...].astype(jnp.bfloat16), tokens_ref[...])[:experts, :]
    expert = lax.broadcasted_iota(jnp.int32, logits.shape, 0)
    routed = expert == routes_ref[:1, :]
    for choice in range(1, TOP):
        routed = routed | (expert == routes_ref[choice : choice + 1, :])
    logits = jnp.where(routed, logits, NEG)
    exponent = jnp.exp(logits - jnp.max(logits, 0, keepdims=True))
    exponent = jnp.where(routed, exponent, 0.0)
    gates = exponent / jnp.sum(exponent, 0, keepdims=True)
    gates_ref[...] = gates
    high = gates.astype(jnp.bfloat16)
    rest = gates - high.astype(jnp.float32)
    middle = rest.astype(jnp.bfloat16)
    rest = rest - middle.astype(jnp.float32)
    for part, values in enumerate((high.astype(jnp.float32), middle.astype(jnp.float32), rest)):
        lanes = pl.ds(pl.multiple_of(part * rows_count + step * tile, tile), tile)
        packed_ref[rows_count:, lanes] = jnp.concatenate(
            [values, jnp.zeros((16 - experts, tile), jnp.float32)], 0
        ).astype(jnp.bfloat16)


def middle_call(starts, tokens, attended, routes, small, blocks, experts, column):
    rows_count = tokens.shape[0]
    tile = rows_count // 2
    low = jnp.bfloat16
    tiled = pl.BlockSpec((tile, D), lambda i: (i, 0))
    lanes = lambda rows: pl.BlockSpec((rows, tile), lambda i: (0, i))
    return pl.pallas_call(
        functools.partial(middle_kernel, len(blocks), column),
        grid=(2,),
        out_shape=[
            jax.ShapeDtypeStruct((rows_count, D), jnp.float32),
            jax.ShapeDtypeStruct((rows_count + 16, D), low),
            jax.ShapeDtypeStruct((experts, rows_count), jnp.float32),
        ],
        in_specs=[
            scalars(),
            tiled,
            tiled,
            lanes(routes.shape[0]),
            pl.BlockSpec((16, D), lambda i: (0, 0)),
        ]
        + [anywhere()] * len(blocks),
        out_specs=[
            tiled,
            pl.BlockSpec((rows_count + 16, D), lambda i: (0, 0)),
            lanes(experts),
        ],
        scratch_shapes=[
            pltpu.VMEM((D, D), low),
            pltpu.SemaphoreType.DMA((len(blocks) * blocks[0].shape[0],)),
        ],
        compiler_params=pltpu.CompilerParams(vmem_limit_bytes=62 << 20),
        cost_estimate=small_cost(),
        name="middle",
    )(starts, tokens, attended, routes, small, *blocks)


def middle_back_kernel(planes, column, start_ref, *refs):
    terms, tails, refs = refs[:4], refs[4:8], refs[8:]
    residual_ref, small_ref, cot_ref, gates_ref, refs = *refs[:4], refs[4:]
    blocks, refs = refs[:planes], refs[planes:]
    mid_ref, low_ref, attended_grad_ref, logits_grad_ref, gain_ref, weight, sems = refs
    step = pl.program_id(0)
    experts = gates_ref.shape[0]
    rows_count = gates_ref.shape[1]

    @pl.when(step == 0)
    def _():
        copies = load_rows(blocks, start_ref, weight, sems, column)
        gates = gates_ref[...]
        parts = sum([tail[:experts, :].astype(jnp.float32) for tail in tails])
        grad = (
            parts[:, :rows_count]
            + parts[:, rows_count : 2 * rows_count]
            + parts[:, 2 * rows_count :]
        )
        grad = gates * (grad - jnp.sum(gates * grad, 0, keepdims=True))
        logits_grad_ref[...] = jnp.concatenate(
            [grad, jnp.zeros((16 - experts, rows_count), jnp.float32)], 0
        ).astype(jnp.bfloat16)
        gain_ref[...] = jnp.zeros_like(gain_ref)
        for copy in copies:
            copy.wait()

    grad = sum([term[...].astype(jnp.float32) for term in terms])
    residual = residual_ref[...]
    inverse = lax.rsqrt(jnp.mean(residual * residual, -1, keepdims=True) + EPS)
    normed = residual * inverse
    product = grad * normed
    gain_ref[...] += jnp.sum(product, 0, keepdims=True)
    gain = small_ref[experts + 1 : experts + 2, :]
    mean = jnp.mean(product * gain, -1, keepdims=True)
    mid = cot_ref[...].astype(jnp.float32) + inverse * (grad * gain - normed * mean)
    mid_ref[...] = mid
    low_ref[...] = mid.astype(jnp.bfloat16)
    for at in range(0, D, LANES):
        attended_grad_ref[:, at : at + LANES] = wide_dot(
            low_ref[...], weight[at : at + LANES, :]
        ).astype(jnp.bfloat16)


def middle_back_call(starts, terms, residual, small, cotangent, gates, blocks, column):
    rows_count = residual.shape[0]
    tile = rows_count // 2
    low = jnp.bfloat16
    tiled = pl.BlockSpec((tile, D), lambda i: (i, 0))
    fixed = lambda rows, columns: pl.BlockSpec((rows, columns), lambda i: (0, 0))
    tail = pl.BlockSpec((16, D), lambda i: (rows_count // 16, 0))
    return pl.pallas_call(
        functools.partial(middle_back_kernel, len(blocks), column),
        grid=(2,),
        out_shape=[
            jax.ShapeDtypeStruct((rows_count, D), jnp.float32),
            jax.ShapeDtypeStruct((rows_count, D), low),
            jax.ShapeDtypeStruct((rows_count, D), low),
            jax.ShapeDtypeStruct((16, rows_count), low),
            jax.ShapeDtypeStruct((1, D), jnp.float32),
        ],
        in_specs=[scalars()]
        + [tiled] * 4
        + [tail] * 4
        + [tiled, fixed(16, D), tiled, fixed(*gates.shape)]
        + [anywhere()] * len(blocks),
        out_specs=[tiled, tiled, tiled, fixed(16, rows_count), fixed(1, D)],
        scratch_shapes=[
            pltpu.VMEM((D, D), low),
            pltpu.SemaphoreType.DMA((len(blocks) * blocks[0].shape[0],)),
        ],
        compiler_params=pltpu.CompilerParams(vmem_limit_bytes=62 << 20),
        cost_estimate=small_cost(),
        name="middle_back",
    )(starts, *terms, *terms, residual, small, cotangent, gates, *blocks)


def attend_back_kernel(heads_ref, grad_ref, log_ref, first_ref, cosine_ref, sine_ref, raw_ref, bias):
    rows_count = heads_ref.shape[0]
    width_q, width_kv = HEADS * HEAD_DIM, KV_HEADS * HEAD_DIM
    half = rows_count // 2
    scale = HEAD_DIM ** (-0.5)
    fill_bias(bias, first_ref)
    cosine, sine = cosine_ref[...], -sine_ref[...]
    for key_head in range(KV_HEADS):
        key_at = width_q + key_head * HEAD_DIM
        value_at = key_at + width_kv
        key_grads, value_grads = [], []
        for block in range(2):
            rows, reach = slice(block * half, (block + 1) * half), (block + 1) * half
            keys = heads_ref[:reach, key_at : key_at + HEAD_DIM]
            values = heads_ref[:reach, value_at : value_at + HEAD_DIM]
            key_grad = jnp.zeros((reach, HEAD_DIM), jnp.float32)
            value_grad = jnp.zeros((reach, HEAD_DIM), jnp.float32)
            for head in range(key_head * HEADS // KV_HEADS, (key_head + 1) * HEADS // KV_HEADS):
                columns = slice(head * HEAD_DIM, (head + 1) * HEAD_DIM)
                queries, grads = heads_ref[rows, columns], grad_ref[rows, columns]
                scores = wide_dot(queries, keys) * scale + bias[rows, :reach]
                chances = jnp.exp(scores - log_ref[rows, head : head + 1])
                pulled = wide_dot(grads, values)
                shift = jnp.sum(chances * pulled, -1, keepdims=True)
                score_grad = (chances * (pulled - shift)).astype(jnp.bfloat16)
                value_grad = value_grad + tall_dot(chances.astype(jnp.bfloat16), grads)
                key_grad = key_grad + tall_dot(score_grad, queries)
                query_grad = (
                    jnp.dot(score_grad, keys, preferred_element_type=jnp.float32) * scale
                )
                raw_ref[rows, columns] = turned(
                    query_grad, cosine[rows, :], sine[rows, :]
                ).astype(jnp.bfloat16)
            key_grads.append(key_grad)
            value_grads.append(value_grad)
        key_grad = jnp.concatenate([key_grads[0] + key_grads[1][:half], key_grads[1][half:]], 0)
        value_grad = jnp.concatenate(
            [value_grads[0] + value_grads[1][:half], value_grads[1][half:]], 0
        )
        raw_ref[:, key_at : key_at + HEAD_DIM] = turned(key_grad * scale, cosine, sine).astype(
            jnp.bfloat16
        )
        raw_ref[:, value_at : value_at + HEAD_DIM] = value_grad.astype(jnp.bfloat16)


def attend_back_call(heads, grads, logs, first, cosine, sine):
    rows_count = heads.shape[0]
    return pl.pallas_call(
        attend_back_kernel,
        out_shape=jax.ShapeDtypeStruct(heads.shape, jnp.bfloat16),
        in_specs=[whole()] * 6,
        out_specs=whole(),
        scratch_shapes=[pltpu.VMEM((rows_count, rows_count), jnp.float32)],
        compiler_params=pltpu.CompilerParams(vmem_limit_bytes=62 << 20),
        cost_estimate=small_cost(),
        name="attend_back",
    )(heads, grads, logs, first, cosine, sine)


def shard_grad_kernel(start_ref, left_ref, right_ref, *refs):
    parts, grad, sems = refs[:-2], refs[-2], refs[-1]
    owners, width = len(parts), right_ref.shape[1]
    pieces, rows = parts[0].shape[0], parts[0].shape[1]
    tall = owners * rows
    copies = []
    for p in range(pieces):
        for at in range(0, width, WIDE):
            grad[p * tall : (p + 1) * tall, at : at + WIDE] = tall_dot(
                left_ref[:, p * tall : (p + 1) * tall], right_ref[:, at : at + WIDE]
            ).astype(jnp.bfloat16)
        to = lax.rem(start_ref[0] + pieces - p, pieces)
        for i, part in enumerate(parts):
            at = pl.multiple_of(p * tall + start_ref[1 + i] * rows, 16)
            copy = pltpu.make_async_copy(
                grad.at[pl.ds(at, rows)], part.at[to], sems.at[p * owners + i]
            )
            copy.start()
            copies.append(copy)
    for copy in copies:
        copy.wait()


def shard_grad_call(spots, left, right, pieces, owners):
    width, height = right.shape[1], left.shape[1]
    rows = height // (pieces * owners)
    return pl.pallas_call(
        shard_grad_kernel,
        out_shape=[jax.ShapeDtypeStruct((pieces, rows, width), jnp.bfloat16)] * owners,
        in_specs=[scalars(), whole(), whole()],
        out_specs=[anywhere()] * owners,
        scratch_shapes=[
            pltpu.VMEM((height, width), jnp.bfloat16),
            pltpu.SemaphoreType.DMA((pieces * owners,)),
        ],
        compiler_params=pltpu.CompilerParams(vmem_limit_bytes=62 << 20),
        cost_estimate=small_cost(),
        name="shard_grad",
    )(spots, left, right)


def entry_back_kernel(planes, start_ref, *refs):
    raw_ref, tokens_ref, mid_ref, small_ref, logits_grad_ref, gain_two_ref, refs = (
        *refs[:6],
        refs[6:],
    )
    blocks, refs = refs[:planes], refs[planes:]
    grad_ref, small_grad_ref, weight, sems = refs
    step = pl.program_id(0)
    width = raw_ref.shape[1]
    experts = small_ref.shape[0] - 8
    tile = tokens_ref.shape[0]

    @pl.when(step == 0)
    def _():
        for copy in load_rows(blocks, start_ref, weight, sems):
            copy.wait()
        small_grad_ref[...] = jnp.zeros_like(small_grad_ref)
        small_grad_ref[experts + 1 : experts + 2, :] = gain_two_ref[...]

    for at in range(0, D, LANES):
        grad_ref[:, at : at + LANES] = wide_dot(raw_ref[...], weight[at : at + LANES, :width])
    inputs = tokens_ref[...].astype(jnp.float32)
    inverse = lax.rsqrt(jnp.mean(inputs * inputs, -1, keepdims=True) + EPS)
    normed = inputs * inverse
    grad = grad_ref[...]
    gain = small_ref[experts : experts + 1, :]
    product = grad * normed
    small_grad_ref[experts : experts + 1, :] += jnp.sum(product, 0, keepdims=True)
    small_grad_ref[:experts, :] += jnp.dot(
        logits_grad_ref[...], tokens_ref[...], preferred_element_type=jnp.float32
    )[:experts, :]
    mean = jnp.mean(product * gain, -1, keepdims=True)
    row = lax.broadcasted_iota(jnp.int32, (16, 1), 0)
    router = jnp.where(row < experts, small_ref[...], 0.0).astype(jnp.bfloat16)
    grad_ref[...] = (
        mid_ref[...]
        + inverse * (grad * gain - normed * mean)
        + tall_dot(logits_grad_ref[...], router)
    )


def entry_back_call(
    starts, raw_grad, tokens, mid_grad, small, logits_grad, gain_two, blocks, width_early
):
    rows_count = tokens.shape[0]
    tile = rows_count // 2
    tiled = lambda columns: pl.BlockSpec((tile, columns), lambda i: (i, 0))
    fixed = lambda rows, columns: pl.BlockSpec((rows, columns), lambda i: (0, 0))
    return pl.pallas_call(
        functools.partial(entry_back_kernel, len(blocks)),
        grid=(2,),
        out_shape=[
            jax.ShapeDtypeStruct((rows_count, D), jnp.float32),
            jax.ShapeDtypeStruct((16, D), jnp.float32),
        ],
        in_specs=[
            scalars(),
            tiled(raw_grad.shape[1]),
            tiled(D),
            tiled(D),
            fixed(16, D),
            pl.BlockSpec((16, tile), lambda i: (0, i)),
            fixed(1, D),
        ]
        + [anywhere()] * len(blocks),
        out_specs=[tiled(D), fixed(16, D)],
        scratch_shapes=[
            pltpu.VMEM((D, width_early), jnp.bfloat16),
            pltpu.SemaphoreType.DMA((len(blocks) * blocks[0].shape[0],)),
        ],
        compiler_params=pltpu.CompilerParams(vmem_limit_bytes=62 << 20),
        cost_estimate=small_cost(),
        name="entry_back",
    )(starts, raw_grad, tokens, mid_grad, small, logits_grad, gain_two, *blocks)


def pipeline(loads, stores, body, count, later=()):
    coming = {}

    def fetch(i):
        coming[i] = loads(i, i % 2)
        for copy in coming[i]:
            copy.start()

    leaving = {}
    fetch(0)
    for copy in later:
        copy.start()
    for i in range(count):
        if i + 1 < count:
            fetch(i + 1)
        for copy in coming.pop(i):
            copy.wait()
        for copy in leaving.pop(i - 2, []):
            copy.wait()
        body(i, i % 2)
        leaving[i] = stores(i, i % 2)
        for copy in leaving[i]:
            copy.start()
    for i in sorted(leaving):
        for copy in leaving[i]:
            copy.wait()


def copies_of(pairs, sems):
    return [
        pltpu.make_async_copy(source, target, sems.at[j])
        for j, (source, target) in enumerate(pairs)
    ]


def hidden_kernel(count, pieces, tokens_count, place_ref, *refs):
    rows_in, chunks, refs = refs[:count], refs[count : count + pieces], refs[count + pieces :]
    outs, refs = refs[: 3 * count], refs[3 * count :]
    weight, rows, slope, product, gated, sems, in_sems, out_sems = refs
    weight_copies = load_weight(chunks, place_ref, weight, sems)

    def loads(i, slot):
        return copies_of([(rows_in[i], rows.at[slot])], in_sems.at[slot])

    def stores(i, slot):
        buffers = (slope, product, gated)
        return copies_of(
            [(buffer.at[slot], outs[j * count + i]) for j, buffer in enumerate(buffers)],
            out_sems.at[slot],
        )

    def body(i, slot):
        if i == 0:
            for copy in weight_copies:
                copy.wait()
        weights = spread(expert_row(rows[slot, tokens_count:, :], place_ref[4]), tokens_count)
        weights = jnp.concatenate([weights] * (LANES // 128), 1)
        for at in range(0, FF, LANES):
            gate = jnp.dot(
                rows[slot, :tokens_count, :],
                weight[:, at : at + LANES],
                preferred_element_type=jnp.float32,
            )
            up = jnp.dot(
                rows[slot, :tokens_count, :],
                weight[:, FF + at : FF + at + LANES],
                preferred_element_type=jnp.float32,
            )
            square = gate * gate
            bend = jnp.tanh(0.7978845608028654 * gate * (1.0 + 0.044715 * square))
            half = 0.5 + 0.5 * bend
            steep = half + 0.5 * gate * (1.0 - bend * bend) * (
                0.7978845608028654 + 0.10703222440890037 * square
            )
            active = gate * half
            both = (active * up).astype(jnp.bfloat16)
            slope[slot, :, at : at + LANES] = (up * steep).astype(jnp.bfloat16)
            slope[slot, :, FF + at : FF + at + LANES] = active.astype(jnp.bfloat16)
            product[slot, :, at : at + LANES] = both
            gated[slot, :, at : at + LANES] = (both.astype(jnp.float32) * weights).astype(
                jnp.bfloat16
            )

    pipeline(loads, stores, body, count)


def hidden_call(rows_in, chunks, places, tokens_count):
    count = len(rows_in)
    low = jnp.bfloat16
    widths = [2 * FF, FF, FF]
    outs = pl.pallas_call(
        functools.partial(hidden_kernel, count, len(chunks), tokens_count),
        out_shape=[
            jax.ShapeDtypeStruct((tokens_count, width), low)
            for width in widths
            for _ in range(count)
        ],
        in_specs=[scalars()] + [anywhere()] * (count + len(chunks)),
        out_specs=[anywhere()] * (3 * count),
        scratch_shapes=[
            pltpu.VMEM((D, 2 * FF), low),
            pltpu.VMEM((2, *rows_in[0].shape), low),
            *[pltpu.VMEM((2, tokens_count, width), low) for width in widths],
            pltpu.SemaphoreType.DMA((len(chunks),)),
            pltpu.SemaphoreType.DMA((2, 1)),
            pltpu.SemaphoreType.DMA((2, 3)),
        ],
        compiler_params=pltpu.CompilerParams(vmem_limit_bytes=62 << 20),
        cost_estimate=small_cost(),
        name="expert_hidden",
    )(places, *rows_in, *chunks)
    return outs[:count], outs[count : 2 * count], outs[2 * count :]


def spread(row, tokens_count):
    return jnp.transpose(jnp.broadcast_to(row, (128, tokens_count)))


def expert_row(block, expert):
    third = block.shape[1] // 3
    index = lax.broadcasted_iota(jnp.int32, block.shape, 0)
    row = jnp.sum(jnp.where(index == expert, block.astype(jnp.float32), 0.0), 0, keepdims=True)
    return row[:, :third] + row[:, third : 2 * third] + row[:, 2 * third :]


def split_row(row):
    high = row.astype(jnp.bfloat16)
    rest = row - high.astype(jnp.float32)
    middle = rest.astype(jnp.bfloat16)
    low = (rest - middle.astype(jnp.float32)).astype(jnp.bfloat16)
    return jnp.concatenate(
        [high.astype(jnp.float32), middle.astype(jnp.float32), low.astype(jnp.float32)], 1
    )


def pull_kernel(count, pieces, tokens_count, place_ref, *refs):
    packed, cots, slopes, products = (refs[i * count : (i + 1) * count] for i in range(4))
    refs = refs[4 * count :]
    in_chunks, out_chunks, refs = refs[: pieces[0]], refs[pieces[0] : sum(pieces)], refs[sum(pieces) :]
    row_grads, hidden_grads, refs = refs[:count], refs[count : 2 * count], refs[2 * count :]
    in_weight, out_weight, tail, cot, slope, product, grad, hidden, *sems = refs
    expert = place_ref[4]
    in_copies, out_copies = [], []

    def loads(i, slot):
        copies = copies_of(
            [
                (packed[i].at[pl.ds(tokens_count, 16)], tail.at[slot]),
                (cots[i], cot.at[slot]),
                (slopes[i], slope.at[slot]),
                (products[i], product.at[slot]),
            ],
            sems[2].at[slot],
        )
        return copies

    def stores(i, slot):
        return copies_of(
            [(grad.at[slot], row_grads[i]), (hidden.at[slot], hidden_grads[i])], sems[3].at[slot]
        )

    def body(i, slot):
        if i == 0:
            for copy in out_copies:
                copy.wait()
        weights = spread(expert_row(tail[slot], expert), tokens_count)
        weights = jnp.concatenate([weights] * (LANES // 128), 1)
        gate_grad = jnp.zeros((tokens_count, 1), jnp.float32)
        for at in range(0, FF, LANES):
            pulled = wide_dot(cot[slot], out_weight[at : at + LANES, :])
            both = product[slot, :, at : at + LANES].astype(jnp.float32)
            gate_grad = gate_grad + jnp.sum(pulled * both, 1, keepdims=True)
            pulled = pulled * weights
            for base in (at, FF + at):
                hidden[slot, :, base : base + LANES] = (
                    pulled * slope[slot, :, base : base + LANES].astype(jnp.float32)
                ).astype(jnp.bfloat16)
        row = jnp.transpose(jnp.broadcast_to(gate_grad, (tokens_count, 128)))[:1, :]
        parts = jnp.broadcast_to(split_row(row), (16, 3 * tokens_count))
        index = lax.broadcasted_iota(jnp.int32, parts.shape, 0)
        grad[slot, tokens_count:, :] = jnp.where(index == expert, parts, 0.0).astype(jnp.bfloat16)
        if i == 0:
            for copy in in_copies:
                copy.wait()
        for at in range(0, D, LANES):
            grad[slot, :tokens_count, at : at + LANES] = wide_dot(
                hidden[slot], in_weight[at : at + LANES, :]
            ).astype(jnp.bfloat16)

    out_copies += load_weight(out_chunks, place_ref, out_weight, sems[1])
    in_copies += load_weight(in_chunks, place_ref, in_weight, sems[0], False)
    pipeline(loads, stores, body, count, in_copies)


def pull_call(packed, cots, slopes, products, in_chunks, out_chunks, places, tokens_count):
    count = len(packed)
    low = jnp.bfloat16
    out_shapes = [(tokens_count + 16, D), (tokens_count, 2 * FF)]
    outs = pl.pallas_call(
        functools.partial(
            pull_kernel, count, (len(in_chunks), len(out_chunks)), tokens_count
        ),
        out_shape=[jax.ShapeDtypeStruct(shape, low) for shape in out_shapes for _ in range(count)],
        in_specs=[scalars()] + [anywhere()] * (4 * count + len(in_chunks) + len(out_chunks)),
        out_specs=[anywhere()] * (2 * count),
        scratch_shapes=[
            pltpu.VMEM((D, 2 * FF), low),
            pltpu.VMEM((FF, D), low),
            pltpu.VMEM((2, 16, D), low),
            pltpu.VMEM((2, tokens_count, D), low),
            pltpu.VMEM((2, tokens_count, 2 * FF), low),
            pltpu.VMEM((2, tokens_count, FF), low),
            pltpu.VMEM((2, tokens_count + 16, D), low),
            pltpu.VMEM((2, tokens_count, 2 * FF), low),
            pltpu.SemaphoreType.DMA((len(in_chunks),)),
            pltpu.SemaphoreType.DMA((len(out_chunks),)),
            pltpu.SemaphoreType.DMA((2, 4)),
            pltpu.SemaphoreType.DMA((2, 2)),
        ],
        compiler_params=pltpu.CompilerParams(vmem_limit_bytes=62 << 20),
        cost_estimate=small_cost(),
        name="expert_pull",
    )(places, *packed, *cots, *slopes, *products, *in_chunks, *out_chunks)
    return outs[:count], outs[count:]


def product_kernel(count, place_ref, *refs):
    gated, chunks, refs = refs[:count], refs[count : count + 4], refs[count + 4 :]
    rows_out, (weight, left, total, *sems) = refs[:count], refs[count:]
    weight_copies = load_weight(chunks, place_ref, weight, sems[0])

    def loads(i, slot):
        return copies_of([(gated[i], left.at[slot])], sems[1].at[slot])

    def stores(i, slot):
        return copies_of([(total.at[slot], rows_out[i])], sems[2].at[slot])

    def body(i, slot):
        if i == 0:
            for copy in weight_copies:
                copy.wait()
        for at in range(0, D, LANES):
            total[slot, :, at : at + LANES] = jnp.dot(
                left[slot], weight[:, at : at + LANES], preferred_element_type=jnp.float32
            ).astype(jnp.bfloat16)

    pipeline(loads, stores, body, count)


def product_call(gated, chunks, places):
    count, rows = len(gated), gated[0].shape[0]
    return pl.pallas_call(
        functools.partial(product_kernel, count),
        out_shape=[jax.ShapeDtypeStruct((rows, D), jnp.bfloat16)] * count,
        in_specs=[scalars()] + [anywhere()] * (count + 4),
        out_specs=[anywhere()] * count,
        scratch_shapes=[
            pltpu.VMEM((FF, D), jnp.bfloat16),
            pltpu.VMEM((2, rows, FF), jnp.bfloat16),
            pltpu.VMEM((2, rows, D), jnp.bfloat16),
            pltpu.SemaphoreType.DMA((4,)),
            pltpu.SemaphoreType.DMA((2, 1)),
            pltpu.SemaphoreType.DMA((2, 1)),
        ],
        compiler_params=pltpu.CompilerParams(vmem_limit_bytes=62 << 20),
        cost_estimate=small_cost(),
        name="expert_rows",
    )(places, *gated, *chunks)


def weight_grad_kernel(count, rows, *refs):
    left, right, grad = refs[:count], refs[count : 2 * count], refs[2 * count]
    total = tall_dot(left[0][:rows, :], right[0][:rows, :])
    for i in range(1, count):
        total = total + tall_dot(left[i][:rows, :], right[i][:rows, :])
    grad[...] = total.astype(grad.dtype)


def weight_grad_call(left, right, rows, tall, name):
    count = len(left)
    height, width = left[0].shape[1], right[0].shape[1]
    return pl.pallas_call(
        functools.partial(weight_grad_kernel, count, rows),
        grid=(height // tall, width // WIDE),
        out_shape=jax.ShapeDtypeStruct((height, width), jnp.bfloat16),
        in_specs=[pl.BlockSpec((rows, tall), lambda i, j: (0, i))] * count
        + [pl.BlockSpec((rows, WIDE), lambda i, j: (0, j))] * count,
        out_specs=pl.BlockSpec((tall, WIDE), lambda i, j: (i, j)),
        compiler_params=pltpu.CompilerParams(vmem_limit_bytes=62 << 20),
        cost_estimate=small_cost(),
        name=name,
    )(*left, *right)


def plane_shards(
    tokens,
    cotangent,
    routes,
    doc_lengths,
    query_weight,
    query_first,
    query_second,
    keyvalue_weight,
    keyvalue_first,
    keyvalue_second,
    output_weight,
    output_first,
    output_second,
    router_weight,
    router_first,
    router_second,
    norm_gains,
    gains_first,
    gains_second,
    expert_in,
    expert_in_first,
    expert_in_second,
    expert_out,
    expert_out_first,
    expert_out_second,
):
    rows_count = tokens.shape[0]
    experts = router_weight.shape[1]
    columns_dp, owners = lax.axis_size("dp"), lax.axis_size("expert")
    dp_index, expert_index = lax.axis_index("dp"), lax.axis_index("expert")
    core = expert_index & 1
    ring = [(i, (i + 1) % columns_dp) for i in range(columns_dp)]
    shard = query_weight.shape[0]
    width_q = HEADS * HEAD_DIM
    width_qkv = (HEADS + 2 * KV_HEADS) * HEAD_DIM
    low = jnp.bfloat16
    places = (dp_index - jnp.arange(columns_dp, dtype=jnp.int32)) % columns_dp
    starts = (
        (expert_index ^ jnp.arange(owners, dtype=jnp.int32))[:, None] + places[None, :] * owners
    ).reshape(-1) * shard
    places = jnp.concatenate([places, expert_index[None]]).astype(jnp.int32)
    spots = jnp.concatenate([dp_index[None], expert_index ^ jnp.arange(owners)]).astype(jnp.int32)

    position = jnp.arange(rows_count, dtype=jnp.int32)
    ends = jnp.cumsum(doc_lengths[0])
    first = jnp.max(jnp.where(position[:, None] >= ends[None, :], ends[None, :], 0), 1)
    offset = (position - first).astype(jnp.float32)
    frequency = ROPE_BASE ** (-2.0 * jnp.arange(HEAD_DIM // 2, dtype=jnp.float32) / HEAD_DIM)
    angles = offset[:, None] * frequency[None, :]
    cosine = jnp.tile(jnp.cos(angles), (1, 2))
    sine = jnp.concatenate([-jnp.sin(angles), jnp.sin(angles)], 1)
    first = first[:, None]

    width_early = width_qkv + 128

    def cross(block):
        return to_x(block), to_y(block)

    def onward(from_x, from_y):
        return jnp.where(core == 0, from_y, from_x)

    sent = jnp.concatenate(
        [
            query_weight.astype(low),
            keyvalue_weight.astype(low),
            router_weight.astype(low),
            norm_gains.T.astype(low),
            jnp.zeros((shard, 128 - experts - 2), low),
            output_weight.astype(low),
        ],
        1,
    )

    def around(value):
        return lax.ppermute(value, "dp", ring)

    cot_x, cot_y = cross(cotangent)
    in_low, out_low = expert_in[0].astype(low), expert_out[0].astype(low)
    column = [sent, around(sent)]
    column.append(around(column[1]))
    column[2], in_low, out_low, cosine, sine, first, routes_t = hold(
        column[2], in_low, out_low, cosine, sine, first, routes.T
    )
    column.append(around(column[2]))
    joint = jnp.stack(column)
    cut = in_low.shape[0] * 5 // 8
    in_near, in_rest = [in_low[:cut]], [in_low[cut:]]
    cot_x, cot_y, joint, in_near[0], in_rest[0] = hold(
        cot_x, cot_y, joint, in_near[0], in_rest[0]
    )

    joint_x, joint_y = cross(joint)
    joint_core, cot_core = to_core(joint), to_core(cotangent)
    in_near.append(around(in_near[0]))
    in_rest.append(around(in_rest[0]))
    joint_x, joint_y, joint_core, cot_core, in_near[1], in_rest[1] = hold(
        joint_x, joint_y, joint_core, cot_core, in_near[1], in_rest[1]
    )

    joint_far = forward(onward(joint_x, joint_y))
    joint_x2, joint_y2 = to_core(joint_x), to_core(joint_y)
    cot_x2, cot_y2 = to_core(cot_x), to_core(cot_y)
    in_near.append(around(in_near[1]))
    joint_far, joint_x2, joint_y2, cot_x2, cot_y2, in_near[2] = hold(
        joint_far, joint_x2, joint_y2, cot_x2, cot_y2, in_near[2]
    )
    plane = [joint, joint_core, joint_x, joint_x2, joint_y, joint_y2, joint_far]
    plane.append(to_core(joint_far))

    plane[7], cot_x = hold(plane[7], cot_x)
    cot_far = forward(onward(cot_x, cot_y))
    in_near.append(around(in_near[2]))
    attn_in, heads, attended, logs, small = attend_call(
        starts, tokens, first, cosine, sine, plane, width_early
    )
    attended, cot_far, in_near[3], in_rest[1] = hold(attended, cot_far, in_near[3], in_rest[1])
    in_rest.append(around(in_rest[1]))
    residual_mid, packed, gates = middle_call(
        starts, tokens, attended, routes_t, small, plane, experts, width_early
    )
    packed, in_rest[2], out_low, cot_far = hold(packed, in_rest[2], out_low, cot_far)

    packed_x, packed_y = cross(packed)
    packed_core, cot_far2 = to_core(packed), to_core(cot_far)
    in_rest.append(around(in_rest[2]))
    out_chunks = [out_low, around(out_low)]
    packed_x, packed_y, packed_core, cot_far2, in_rest[3], out_chunks[1] = hold(
        packed_x, packed_y, packed_core, cot_far2, in_rest[3], out_chunks[1]
    )
    cot_blocks = [cotangent, cot_core, cot_x, cot_x2, cot_y, cot_y2, cot_far, cot_far2]
    in_chunks = in_near + in_rest
    slopes, products, gated = [None] * 8, [None] * 8, [None] * 8

    def hidden(k, *blocks):
        outs = hidden_call(blocks, in_chunks, places, rows_count)
        to = slice(k, k + len(blocks))
        slopes[to], products[to], gated[to] = outs

    packed_x2, packed_y2 = to_core(packed_x), to_core(packed_y)
    packed_x, packed_x2, packed_y, packed_y2 = hold(packed_x, packed_x2, packed_y, packed_y2)
    packed_far = forward(onward(packed_x, packed_y))
    out_chunks.append(around(out_chunks[1]))
    hidden(0, packed, packed_core, packed_x, packed_x2)
    packed_far, gated[0], out_chunks[2] = hold(packed_far, gated[0], out_chunks[2])
    packed_far2 = to_core(packed_far)
    packed_far, packed_far2, out_chunks[2] = hold(packed_far, packed_far2, out_chunks[2])
    out_chunks.append(around(out_chunks[2]))
    hidden(4, packed_y, packed_y2, packed_far, packed_far2)
    packed_blocks = [packed, packed_core, packed_x, packed_x2]
    packed_blocks += [packed_y, packed_y2, packed_far, packed_far2]

    def column_piece(value, back):
        rows = value.shape[0] // columns_dp
        return lax.dynamic_slice_in_dim(value, places[back] * rows, rows, 0)

    out_grad = weight_grad_call(gated, cot_blocks, rows_count, FF, "expert_out_grad")
    out_grad, out_chunks[3] = hold(out_grad, out_chunks[3])
    moving = column_piece(out_grad, 1)
    row_grads, hidden_grads = [None] * 8, [None] * 8

    def pull(order, *earlier):
        def pick(values):
            return [values[k] for k in order]

        first_cot = after(cot_blocks[order[0]], *earlier)
        outs = pull_call(
            pick(packed_blocks),
            [first_cot] + pick(cot_blocks)[1:],
            pick(slopes),
            pick(products),
            in_chunks,
            out_chunks,
            places,
            rows_count,
        )
        for k, row_grad, hidden_grad in zip(order, *outs):
            row_grads[k], hidden_grads[k] = row_grad, hidden_grad

    moved = around(moving)
    pull((7, 6), moving)
    moved, row_grads[6], row_grads[7] = hold(moved, row_grads[6], row_grads[7])
    far = add_low(row_grads[6], to_core(row_grads[7]))
    moving = add_low(moved, column_piece(out_grad, 2))
    far, moving = hold(far, moving)
    relayed = forward(far)
    moved = around(moving)
    pull((0, 1, 3, 2, 5, 4), far, moving)
    relayed, moved, row_grads[:6] = hold(relayed, moved, row_grads[:6])
    zero = jnp.zeros((), low)
    back_x = to_core(row_grads[3])
    back_y = to_core(row_grads[5])
    by_x = add_low(row_grads[2], back_x, jnp.where(core == 1, relayed, zero))
    by_y = add_low(row_grads[4], back_y, jnp.where(core == 0, relayed, zero))
    moving = add_low(moved, column_piece(out_grad, 3))
    by_x, by_y, moving = hold(by_x, by_y, moving)

    from_x, from_y = cross(by_x)[0], cross(by_y)[1]
    moved = around(moving)
    rows_out = [None] * 8

    def rows_of(order, *earlier):
        first_gated = after(gated[order[0]], *earlier)
        outs = product_call(
            [first_gated] + [gated[k] for k in order[1:]], out_chunks, places
        )
        for k, rows in zip(order, outs):
            rows_out[k] = rows

    rows_of((7, 6), by_x, by_y, moving)
    hidden_grads[0], rows_out[6] = hold(hidden_grads[0], rows_out[6])
    in_grad = weight_grad_call(packed_blocks, hidden_grads, rows_count, FF, "expert_in_grad")
    moving = column_piece(in_grad, 1)
    from_x, from_y, moved, moving, row_grads[1] = hold(
        from_x, from_y, moved, moving, row_grads[1]
    )
    expert_out_sum = moved.astype(jnp.float32) + column_piece(out_grad, 0).astype(jnp.float32)
    back_own, rows_back = to_core(row_grads[1]), to_core(rows_out[7])
    rows_far = add_low(rows_out[6], rows_back)
    back_own, rows_far, moving = hold(back_own, rows_far, moving)

    rows_relayed = forward(rows_far)
    moved = around(moving)
    mid_grad, mid_low, attended_grad, logits_grad, gain_two = middle_back_call(
        starts, [after(row_grads[0], rows_far, moving), back_own, from_x, from_y], residual_mid,
        small, cotangent, gates, plane, width_early,
    )
    output_parts = shard_grad_call(spots, attended, mid_low, columns_dp, owners)
    rows_of((5, 4, 3, 2, 1, 0), output_parts[0])
    rows_relayed, moved, rows_out[:6], output_parts = hold(
        rows_relayed, moved, rows_out[:6], output_parts
    )
    rows_x = add_low(
        rows_out[2], to_core(rows_out[3]), jnp.where(core == 1, rows_relayed, zero)
    )
    rows_y = add_low(
        rows_out[4], to_core(rows_out[5]), jnp.where(core == 0, rows_relayed, zero)
    )
    output_back = [to_core(output_parts[k]) for k in (1, 3, 5, 7)]
    output_far = add_low(output_parts[6], output_back[3])
    moving = add_low(moved, column_piece(in_grad, 2))
    rows_x, rows_y, output_far, moving, output_back = hold(
        rows_x, rows_y, output_far, moving, output_back
    )

    rows_from_x, rows_from_y = to_x(rows_x), to_y(rows_y)
    output_relayed = forward(output_far)
    moved = around(moving)
    raw_grad = attend_back_call(
        heads, after(attended_grad, rows_x, output_far, moving), logs, first, cosine, sine
    )
    early_parts = shard_grad_call(spots, attn_in, raw_grad, columns_dp, owners)
    rows_from_x, rows_from_y, output_relayed, moved, early_parts, rows_out[0] = hold(
        rows_from_x, rows_from_y, output_relayed, moved, early_parts, rows_out[0]
    )
    early_back = [to_core(early_parts[k]) for k in (1, 3, 5, 7)]
    early_far = add_low(early_parts[6], early_back[3])
    output_x = add_low(
        output_parts[2], output_back[1], jnp.where(core == 1, output_relayed, zero)
    )
    output_y = add_low(
        output_parts[4], output_back[2], jnp.where(core == 0, output_relayed, zero)
    )
    moving = add_low(moved, column_piece(in_grad, 3))
    early_far, output_x, output_y, moving, early_back = hold(
        early_far, output_x, output_y, moving, early_back
    )

    early_relayed = forward(early_far)
    output_terms = [output_parts[0], output_back[0], to_x(output_x), to_y(output_y)]
    tokens_grad, small_grad = entry_back_call(
        starts, after(raw_grad, early_far, output_x), tokens, mid_grad, small, logits_grad,
        gain_two, plane, width_early,
    )
    early_relayed, output_terms, small_grad = hold(early_relayed, output_terms, small_grad)
    early_x = add_low(early_parts[2], early_back[1], jnp.where(core == 1, early_relayed, zero))
    early_y = add_low(early_parts[4], early_back[2], jnp.where(core == 0, early_relayed, zero))
    small_sum = small_grad + to_core(small_grad)
    early_x, early_y, small_sum, output_terms = hold(early_x, early_y, small_sum, output_terms)
    early_terms = [early_parts[0], early_back[0], to_x(early_x), to_y(early_y)]
    moved = around(moving)
    small_x = small_sum + to_x(small_sum)
    small_sum = small_x + to_y(small_x)
    output_total = add_low(*output_terms)
    block_out = residual_mid + add_low_wide(
        rows_out[0], to_core(rows_out[1]), rows_from_x, rows_from_y
    )
    mixed_out = block_out.astype(low)
    early_terms, output_total, moved, small_sum = hold(
        early_terms, output_total, moved, small_sum
    )
    total = jnp.concatenate([add_low(*early_terms), output_total], 2)
    summed = scatter_pieces([total[p] for p in range(columns_dp)], ring)
    small_total = small_sum
    small_moving = small_sum
    for _ in range(columns_dp - 1):
        small_moving = around(small_moving)
        small_total = small_total + small_moving
    small_own = lax.dynamic_slice_in_dim(
        small_total.T, (dp_index * owners + expert_index) * shard, shard, 0
    )
    expert_in_sum = moved.astype(jnp.float32) + column_piece(in_grad, 0).astype(jnp.float32)
    at = width_qkv
    sums = (
        summed[:, :width_q],
        summed[:, width_q:at],
        summed[:, at:],
        small_own[:, :experts],
        small_own[:, experts : experts + 2].T,
        expert_in_sum[None],
        expert_out_sum[None],
    )
    weights = (
        (query_weight, query_first, query_second),
        (keyvalue_weight, keyvalue_first, keyvalue_second),
        (output_weight, output_first, output_second),
        (router_weight, router_first, router_second),
        (norm_gains, gains_first, gains_second),
        (expert_in, expert_in_first, expert_in_second),
        (expert_out, expert_out_first, expert_out_second),
    )
    updates = []
    for state, grad, rate, decay in zip(
        weights, sums, learning_rates(), (DECAY, DECAY, DECAY, DECAY, 0.0, DECAY, DECAY)
    ):
        updates.extend(adam_update(*state, grad, rate, decay))
    return (mixed_out, tokens_grad, *updates)


def solution(mesh):
    in_specs = (
        P(("dp", "expert"), None),
        P(("dp", "expert"), None),
        P(("dp", "expert"), None),
        P(("dp", "expert"), None),
        P(("dp", "expert"), None),
        P(("dp", "expert"), None),
        P(("dp", "expert"), None),
        P(("dp", "expert"), None),
        P(("dp", "expert"), None),
        P(("dp", "expert"), None),
        P(("dp", "expert"), None),
        P(("dp", "expert"), None),
        P(("dp", "expert"), None),
        P(("dp", "expert"), None),
        P(("dp", "expert"), None),
        P(("dp", "expert"), None),
        P(None, ("dp", "expert")),
        P(None, ("dp", "expert")),
        P(None, ("dp", "expert")),
        P("expert", "dp", None),
        P("expert", "dp", None),
        P("expert", "dp", None),
        P("expert", "dp", None),
        P("expert", "dp", None),
        P("expert", "dp", None),
    )
    out_specs = (
        P(("dp", "expert"), None),
        P(("dp", "expert"), None),
        P(("dp", "expert"), None),
        P(("dp", "expert"), None),
        P(("dp", "expert"), None),
        P(("dp", "expert"), None),
        P(("dp", "expert"), None),
        P(("dp", "expert"), None),
        P(("dp", "expert"), None),
        P(("dp", "expert"), None),
        P(("dp", "expert"), None),
        P(("dp", "expert"), None),
        P(("dp", "expert"), None),
        P(("dp", "expert"), None),
        P(None, ("dp", "expert")),
        P(None, ("dp", "expert")),
        P(None, ("dp", "expert")),
        P("expert", "dp", None),
        P("expert", "dp", None),
        P("expert", "dp", None),
        P("expert", "dp", None),
        P("expert", "dp", None),
        P("expert", "dp", None),
    )
    def body(tokens, *rest):
        one_plane = mesh.shape["expert"] == 8 and rest[12].shape[1] == 8
        fits = one_plane and 3 * tokens.shape[0] == D
        return (plane_shards if fits else shards)(tokens, *rest)

    return jax.shard_map(body, mesh=mesh, in_specs=in_specs, out_specs=out_specs, check_vma=False)
```

```python
import functools

import jax
import jax.numpy as jnp
from jax import lax
from jax.experimental import pallas as pl
from jax.experimental.pallas import tpu as pltpu
from jax.sharding import PartitionSpec as P

D = 1536
FF = 768
HEADS = 12
KV_HEADS = 2
HEAD_DIM = 128
TOP = 4
STEP = 10


EPS = 1e-06
NEG = -1e30
BETA_ONE = 0.9
BETA_TWO = 0.999
ADAM_EPS = 1e-08
DECAY = 0.1
ROPE_BASE = 10000.0
RATE_SCALE = 2.5
GAIN_RATE = 0.6


def doc_tables(lengths, rows_count):
    position = jnp.arange(rows_count, dtype=jnp.int32)
    doc_ends = jnp.cumsum(lengths)
    doc_starts = doc_ends - lengths
    doc_index = jnp.sum((position[:, None] >= doc_ends[None, :]).astype(jnp.int32), 1)
    doc_hot = doc_index[:, None] == jnp.arange(lengths.shape[0], dtype=jnp.int32)[None, :]
    start_of = jnp.sum(jnp.where(doc_hot, doc_starts[None, :], 0), 1)
    offset = (position - start_of).astype(jnp.float32)
    frequency = ROPE_BASE ** (-2.0 * jnp.arange(HEAD_DIM // 2, dtype=jnp.float32) / HEAD_DIM)
    angles = offset[:, None] * frequency[None, :]
    allowed = (doc_index[:, None] == doc_index[None, :]) & (position[None, :] <= position[:, None])
    return (jnp.cos(angles), jnp.sin(angles), allowed)


def rotate(values, cos_table, sin_table):
    half_width = values.shape[-1] // 2
    first_half = values[..., :half_width]
    second_half = values[..., half_width:]
    cosine = cos_table[:, None, :]
    sine_part = sin_table[:, None, :]
    return jnp.concatenate(
        [
            first_half * cosine - second_half * sine_part,
            second_half * cosine + first_half * sine_part,
        ],
        -1,
    )


def rotate_back(grads, cos_table, sin_table):
    half_width = grads.shape[-1] // 2
    first_half = grads[..., :half_width]
    second_half = grads[..., half_width:]
    cosine = cos_table[:, None, :]
    sine_part = sin_table[:, None, :]
    return jnp.concatenate(
        [
            first_half * cosine + second_half * sine_part,
            second_half * cosine - first_half * sine_part,
        ],
        -1,
    )


def gelu_tanh(values):
    return jax.nn.gelu(values, approximate=True)


def learning_rates():
    return (
        RATE_SCALE * D ** (-0.5),
        RATE_SCALE * D ** (-0.5),
        RATE_SCALE * (D // 32) ** (-0.5),
        RATE_SCALE * (4 * D) ** (-0.5),
        GAIN_RATE,
        RATE_SCALE * D ** (-0.5),
        RATE_SCALE * (FF // 8) ** (-0.5),
    )


def adam_update(weight, first, second, grad, rate, decay):
    new_first = BETA_ONE * first + (1.0 - BETA_ONE) * grad
    new_second = BETA_TWO * second + (1.0 - BETA_TWO) * grad * grad
    first_hat = new_first / (1.0 - BETA_ONE**STEP)
    second_hat = new_second / (1.0 - BETA_TWO**STEP)
    new_weight = weight - rate * (first_hat / (jnp.sqrt(second_hat) + ADAM_EPS) + decay * weight)
    return (new_first, new_second, new_weight)


def shards(
    tokens,
    cotangent,
    routes,
    doc_lengths,
    query_weight,
    query_first,
    query_second,
    keyvalue_weight,
    keyvalue_first,
    keyvalue_second,
    output_weight,
    output_first,
    output_second,
    router_weight,
    router_first,
    router_second,
    norm_gains,
    gains_first,
    gains_second,
    expert_in,
    expert_in_first,
    expert_in_second,
    expert_out,
    expert_out_first,
    expert_out_second,
):
    rows_count = tokens.shape[0]
    experts = router_weight.shape[1]
    owners = lax.axis_size("expert")
    per_owner = expert_in.shape[0]
    capacity = 3 * rows_count * TOP // (2 * experts)
    groups = HEADS // KV_HEADS
    width_kv = KV_HEADS * HEAD_DIM
    score_scale = HEAD_DIM ** (-0.5)
    query_full, keyvalue_full, output_full, router_full, gains_full = (
        lax.all_gather(query_weight.astype(jnp.bfloat16), ("dp", "expert"), axis=0, tiled=True),
        lax.all_gather(keyvalue_weight.astype(jnp.bfloat16), ("dp", "expert"), axis=0, tiled=True),
        lax.all_gather(output_weight.astype(jnp.bfloat16), ("dp", "expert"), axis=0, tiled=True),
        lax.all_gather(router_weight.astype(jnp.bfloat16), ("dp", "expert"), axis=0, tiled=True),
        lax.all_gather(norm_gains.astype(jnp.bfloat16), ("dp", "expert"), axis=1, tiled=True),
    )
    in_full, out_full = (
        lax.all_gather(expert_in.astype(jnp.bfloat16), "dp", axis=1, tiled=True),
        lax.all_gather(expert_out.astype(jnp.bfloat16), "dp", axis=1, tiled=True),
    )
    gain_attn = gains_full[0].astype(jnp.float32)
    gain_moe = gains_full[1].astype(jnp.float32)
    cos_table, sin_table, allowed = doc_tables(doc_lengths[0], rows_count)
    inputs = tokens.astype(jnp.float32)
    inv_one = lax.rsqrt(jnp.mean(inputs * inputs, -1, keepdims=True) + EPS)
    normed_one = inputs * inv_one
    attn_in = (normed_one * gain_attn).astype(jnp.bfloat16)
    query_raw = jnp.dot(attn_in, query_full, preferred_element_type=jnp.float32)
    keyvalue_raw = jnp.dot(attn_in, keyvalue_full, preferred_element_type=jnp.float32)
    queries = (
        rotate(query_raw.reshape(rows_count, HEADS, HEAD_DIM), cos_table, sin_table)
        .astype(jnp.bfloat16)
        .reshape(rows_count, KV_HEADS, groups, HEAD_DIM)
    )
    keys_rot = rotate(
        keyvalue_raw[:, :width_kv].reshape(rows_count, KV_HEADS, HEAD_DIM), cos_table, sin_table
    ).astype(jnp.bfloat16)
    values_in = (
        keyvalue_raw[:, width_kv:].reshape(rows_count, KV_HEADS, HEAD_DIM).astype(jnp.bfloat16)
    )

    def score_table():
        raw_scores = (
            jnp.einsum("tkgd,skd->kgts", queries, keys_rot, preferred_element_type=jnp.float32)
            * score_scale
        )
        return jnp.where(allowed[None, None], raw_scores, NEG)

    scores = score_table()
    row_max = jnp.max(scores, -1, keepdims=True)
    exponent = jnp.exp(scores - row_max)
    totals = jnp.sum(exponent, -1, keepdims=True)
    probabilities = exponent / totals
    log_sum = row_max + jnp.log(totals)
    attended = jnp.einsum(
        "kgts,skd->tkgd",
        probabilities.astype(jnp.bfloat16),
        values_in,
        preferred_element_type=jnp.float32,
    )
    attended = attended.reshape(rows_count, HEADS * HEAD_DIM).astype(jnp.bfloat16)
    residual_mid = inputs + jnp.dot(attended, output_full, preferred_element_type=jnp.float32)
    inv_two = lax.rsqrt(jnp.mean(residual_mid * residual_mid, -1, keepdims=True) + EPS)
    normed_two = residual_mid * inv_two
    moe_in = (normed_two * gain_moe).astype(jnp.bfloat16)
    logits = jnp.dot(tokens, router_full, preferred_element_type=jnp.float32)
    expert_ids = jnp.arange(experts, dtype=jnp.int32)
    route_hot = routes[:, :, None] == expert_ids[None, None, :]
    picked = jnp.sum(jnp.where(route_hot, logits[:, None, :], 0.0), -1)
    gate_weights = jax.nn.softmax(picked, axis=-1)
    flat_routes = routes.reshape(-1)
    flat_hot = (flat_routes[:, None] == expert_ids[None, :]).astype(jnp.int32)
    slot_index = jnp.sum((jnp.cumsum(flat_hot, 0) - 1) * flat_hot, 1)
    destination = flat_routes * capacity + slot_index
    route_ids = jnp.arange(rows_count * TOP, dtype=jnp.int32)
    source_route = jnp.zeros((experts * capacity,), jnp.int32).at[destination].set(route_ids)
    slot_used = jnp.zeros((experts * capacity,), jnp.bool_).at[destination].set(True)
    source_token = source_route // TOP
    zero_row = jnp.zeros((), jnp.bfloat16)
    send_rows = jnp.where(slot_used[:, None], moe_in[source_token], zero_row).reshape(
        owners, per_owner, capacity, D
    )
    received = lax.all_to_all(send_rows, "expert", split_axis=0, concat_axis=0, tiled=True)
    hidden_pre = jnp.einsum("sicd,idf->sicf", received, in_full, preferred_element_type=jnp.float32)
    gate_part = hidden_pre[..., :FF]
    up_part = hidden_pre[..., FF:]
    activated, gelu_pull = jax.vjp(gelu_tanh, gate_part)
    product = (activated * up_part).astype(jnp.bfloat16)
    expert_rows = jnp.einsum(
        "sicf,ifd->sicd", product, out_full, preferred_element_type=jnp.float32
    ).astype(jnp.bfloat16)
    returned = lax.all_to_all(
        expert_rows, "expert", split_axis=0, concat_axis=0, tiled=True
    ).reshape(experts * capacity, D)
    routed = returned[destination].reshape(rows_count, TOP, D)
    block_out = residual_mid + jnp.sum(gate_weights[:, :, None] * routed, 1)
    mixed_out = block_out.astype(jnp.bfloat16)
    upstream = cotangent.astype(jnp.float32)
    gate_grad = jnp.einsum("tjd,td->tj", routed, cotangent, preferred_element_type=jnp.float32)
    picked_grad = gate_weights * (gate_grad - jnp.sum(gate_weights * gate_grad, -1, keepdims=True))
    logits_grad = jnp.sum(jnp.where(route_hot, picked_grad[:, :, None], 0.0), 1).astype(
        jnp.bfloat16
    )
    rows_grad = (
        (gate_weights[:, :, None] * upstream[:, None, :])
        .astype(jnp.bfloat16)
        .reshape(rows_count * TOP, D)
    )
    send_grad = jnp.where(slot_used[:, None], rows_grad[source_route], zero_row).reshape(
        owners, per_owner, capacity, D
    )
    received_grad = lax.all_to_all(send_grad, "expert", split_axis=0, concat_axis=0, tiled=True)
    product_grad = jnp.einsum(
        "sicd,ifd->sicf", received_grad, out_full, preferred_element_type=jnp.float32
    )
    out_weight_grad = jnp.einsum(
        "sicf,sicd->ifd", product, received_grad, preferred_element_type=jnp.float32
    )
    gate_part_grad = gelu_pull(product_grad * up_part)[0]
    up_part_grad = product_grad * activated
    hidden_grad = jnp.concatenate([gate_part_grad, up_part_grad], -1).astype(jnp.bfloat16)
    in_weight_grad = jnp.einsum(
        "sicd,sicf->idf", received, hidden_grad, preferred_element_type=jnp.float32
    )
    input_rows_grad = jnp.einsum(
        "sicf,idf->sicd", hidden_grad, in_full, preferred_element_type=jnp.float32
    ).astype(jnp.bfloat16)
    returned_grad = lax.all_to_all(
        input_rows_grad, "expert", split_axis=0, concat_axis=0, tiled=True
    ).reshape(experts * capacity, D)
    moe_in_grad = jnp.sum(
        returned_grad[destination].reshape(rows_count, TOP, D).astype(jnp.float32), 1
    )
    gain_two_grad = jnp.sum(moe_in_grad * normed_two, 0)
    scaled_two = moe_in_grad * gain_moe
    mid_grad = upstream + inv_two * (
        scaled_two - normed_two * jnp.mean(scaled_two * normed_two, -1, keepdims=True)
    )
    attn_out_grad = mid_grad.astype(jnp.bfloat16)
    output_weight_grad = jnp.einsum(
        "tc,td->cd", attended, attn_out_grad, preferred_element_type=jnp.float32
    )
    attended_grad = jnp.einsum(
        "td,cd->tc", attn_out_grad, output_full, preferred_element_type=jnp.float32
    )
    attended_grad = attended_grad.astype(jnp.bfloat16).reshape(
        rows_count, KV_HEADS, groups, HEAD_DIM
    )
    probs_again = jnp.exp(score_table() - log_sum)
    prob_grad = jnp.einsum(
        "tkgd,skd->kgts", attended_grad, values_in, preferred_element_type=jnp.float32
    )
    delta_sum = jnp.sum(probs_again * prob_grad, -1, keepdims=True)
    score_grad = (probs_again * (prob_grad - delta_sum)).astype(jnp.bfloat16)
    values_grad = jnp.einsum(
        "kgts,tkgd->skd",
        probs_again.astype(jnp.bfloat16),
        attended_grad,
        preferred_element_type=jnp.float32,
    )
    queries_grad = (
        jnp.einsum("kgts,skd->tkgd", score_grad, keys_rot, preferred_element_type=jnp.float32)
        * score_scale
    )
    keys_grad = (
        jnp.einsum("kgts,tkgd->skd", score_grad, queries, preferred_element_type=jnp.float32)
        * score_scale
    )
    query_raw_grad = rotate_back(
        queries_grad.reshape(rows_count, HEADS, HEAD_DIM), cos_table, sin_table
    )
    query_raw_grad = query_raw_grad.astype(jnp.bfloat16).reshape(rows_count, HEADS * HEAD_DIM)
    key_raw_grad = (
        rotate_back(keys_grad, cos_table, sin_table)
        .astype(jnp.bfloat16)
        .reshape(rows_count, width_kv)
    )
    keyvalue_grad = jnp.concatenate(
        [key_raw_grad, values_grad.astype(jnp.bfloat16).reshape(rows_count, width_kv)], -1
    )
    query_weight_grad = jnp.einsum(
        "tc,tf->cf", attn_in, query_raw_grad, preferred_element_type=jnp.float32
    )
    keyvalue_weight_grad = jnp.einsum(
        "tc,tf->cf", attn_in, keyvalue_grad, preferred_element_type=jnp.float32
    )
    attn_in_grad = jnp.einsum(
        "tf,cf->tc", query_raw_grad, query_full, preferred_element_type=jnp.float32
    )
    attn_in_grad = attn_in_grad + jnp.einsum(
        "tf,cf->tc", keyvalue_grad, keyvalue_full, preferred_element_type=jnp.float32
    )
    gain_one_grad = jnp.sum(attn_in_grad * normed_one, 0)
    scaled_one = attn_in_grad * gain_attn
    tokens_grad = mid_grad + inv_one * (
        scaled_one - normed_one * jnp.mean(scaled_one * normed_one, -1, keepdims=True)
    )
    tokens_grad = tokens_grad + jnp.einsum(
        "te,ce->tc", logits_grad, router_full, preferred_element_type=jnp.float32
    )
    router_weight_grad = jnp.einsum(
        "tc,te->ce", tokens, logits_grad, preferred_element_type=jnp.float32
    )
    gains_grad = jnp.stack([gain_one_grad, gain_two_grad], 0)
    reduced = (
        lax.psum_scatter(query_weight_grad, ("dp", "expert"), scatter_dimension=0, tiled=True),
        lax.psum_scatter(keyvalue_weight_grad, ("dp", "expert"), scatter_dimension=0, tiled=True),
        lax.psum_scatter(output_weight_grad, ("dp", "expert"), scatter_dimension=0, tiled=True),
        lax.psum_scatter(router_weight_grad, ("dp", "expert"), scatter_dimension=0, tiled=True),
        lax.psum_scatter(gains_grad, ("dp", "expert"), scatter_dimension=1, tiled=True),
    )
    expert_sums = (
        lax.psum_scatter(
            in_weight_grad.astype(jnp.bfloat16), "dp", scatter_dimension=1, tiled=True
        ).astype(jnp.float32),
        lax.psum_scatter(
            out_weight_grad.astype(jnp.bfloat16), "dp", scatter_dimension=1, tiled=True
        ).astype(jnp.float32),
    )
    rates = learning_rates()
    query_upd = adam_update(query_weight, query_first, query_second, reduced[0], rates[0], DECAY)
    keyvalue_upd = adam_update(
        keyvalue_weight, keyvalue_first, keyvalue_second, reduced[1], rates[1], DECAY
    )
    output_upd = adam_update(
        output_weight, output_first, output_second, reduced[2], rates[2], DECAY
    )
    router_upd = adam_update(
        router_weight, router_first, router_second, reduced[3], rates[3], DECAY
    )
    gains_upd = adam_update(norm_gains, gains_first, gains_second, reduced[4], rates[4], 0.0)
    in_upd = adam_update(
        expert_in, expert_in_first, expert_in_second, expert_sums[0], rates[5], DECAY
    )
    out_upd = adam_update(
        expert_out, expert_out_first, expert_out_second, expert_sums[1], rates[6], DECAY
    )
    return (
        mixed_out,
        tokens_grad,
        query_upd[0],
        query_upd[1],
        query_upd[2],
        keyvalue_upd[0],
        keyvalue_upd[1],
        keyvalue_upd[2],
        output_upd[0],
        output_upd[1],
        output_upd[2],
        router_upd[0],
        router_upd[1],
        router_upd[2],
        gains_upd[0],
        gains_upd[1],
        gains_upd[2],
        in_upd[0],
        in_upd[1],
        in_upd[2],
        out_upd[0],
        out_upd[1],
        out_upd[2],
    )


def flip(mask):
    return [(i, i ^ mask) for i in range(8)]


ACROSS_X, ACROSS_Y, ACROSS_CORE = flip(2), flip(4), flip(1)
FORWARD = [(i, i ^ (4 if i & 1 else 2)) for i in range(8)]


def after(value, *earlier):
    return lax.optimization_barrier((value, *earlier))[0]


def hold(*values):
    return lax.optimization_barrier(values)


def to_x(value):
    return lax.ppermute(value, "expert", ACROSS_X)


def to_y(value):
    return lax.ppermute(value, "expert", ACROSS_Y)


def to_core(value):
    return lax.ppermute(value, "expert", ACROSS_CORE)


def to_far(value):
    return lax.ppermute(value, "expert", flip(6))


def forward(value):
    return lax.ppermute(value, "expert", FORWARD)


def gather_plane(value, core):
    from_x, from_y = to_x(value), to_y(value)
    from_core = to_core(value)
    from_far = forward(jnp.where(core == 0, from_y, from_x))
    return [
        value,
        from_core,
        from_x,
        to_core(from_x),
        from_y,
        to_core(from_y),
        from_far,
        to_core(from_far),
    ]


def add_low(*terms):
    total = terms[0].astype(jnp.float32)
    for term in terms[1:]:
        total = total + term.astype(jnp.float32)
    return total.astype(jnp.bfloat16)


def add_low_wide(*terms):
    return sum([term.astype(jnp.float32) for term in terms])


def scatter_plane(parts, core):
    far = add_low(parts[6], to_core(parts[7]))
    relayed = forward(far)
    by_x = add_low(parts[2], to_core(parts[3]))
    by_y = add_low(parts[4], to_core(parts[5]))
    own = add_low(parts[0], to_core(parts[1]))
    zero = jnp.zeros((), jnp.bfloat16)
    by_x = add_low(by_x, jnp.where(core == 1, relayed, zero))
    by_y = add_low(by_y, jnp.where(core == 0, relayed, zero))
    return own, to_x(by_x), to_y(by_y)


def gather_column(value, ring):
    values = [value]
    for _ in range(len(ring) - 1):
        values.append(lax.ppermute(values[-1], "dp", ring))
    return values


def scatter_column(value, ring, place):
    count = len(ring)
    rows = value.shape[0] // count

    def piece(shard):
        return lax.dynamic_slice_in_dim(value, (shard % count) * rows, rows, 0)

    moving = piece(place + count - 1)
    for step in range(count - 2):
        moving = add_low(lax.ppermute(moving, "dp", ring), piece(place + count - 2 - step))
    return lax.ppermute(moving, "dp", ring).astype(jnp.float32) + piece(place).astype(jnp.float32)


def scatter_pieces(pieces, ring):
    moving = pieces[1]
    for piece in pieces[2:]:
        moving = add_low(lax.ppermute(moving, "dp", ring), piece)
    return lax.ppermute(moving, "dp", ring).astype(jnp.float32) + pieces[0].astype(jnp.float32)


def anywhere():
    return pl.BlockSpec(memory_space=pl.ANY)


def scalars():
    return pl.BlockSpec(memory_space=pltpu.SMEM)


def whole():
    return pl.BlockSpec(memory_space=pltpu.VMEM)


def small_cost():
    return pl.CostEstimate(flops=1024, bytes_accessed=1024, transcendentals=0)


def load_rows(blocks, start_ref, joined, sems, column=0, start=True):
    width = joined.shape[1]
    pieces, rows = blocks[0].shape[0], blocks[0].shape[1]
    copies = []
    for i, block in enumerate(blocks):
        for p in range(pieces):
            at = pl.multiple_of(start_ref[i * pieces + p], 16)
            copies.append(
                pltpu.make_async_copy(
                    block.at[p, :, pl.ds(column, width)],
                    joined.at[pl.ds(at, rows)],
                    sems.at[i * pieces + p],
                )
            )
    for copy in copies if start else []:
        copy.start()
    return copies


def wide_dot(left, right):
    return lax.dot_general(
        left, right, (((1,), (1,)), ((), ())), preferred_element_type=jnp.float32
    )


def tall_dot(left, right):
    return lax.dot_general(
        left, right, (((0,), (0,)), ((), ())), preferred_element_type=jnp.float32
    )


def load_weight(chunks, place_ref, buffer, sems, start=True):
    total = sum([chunk.shape[0] for chunk in chunks[::4]])
    copies, offset = [], 0
    for j, chunk in enumerate(chunks):
        rows = chunk.shape[0]
        at = pl.multiple_of(place_ref[j % 4] * total + offset, 16)
        copies.append(pltpu.make_async_copy(chunk, buffer.at[pl.ds(at, rows)], sems.at[j]))
        if j % 4 == 3:
            offset += rows
    for copy in copies if start else []:
        copy.start()
    return copies


LANES = 256
WIDE = 512


def turned(values, cosine, sine):
    return values * cosine + pltpu.roll(values, HEAD_DIM // 2, 1) * sine


def fill_bias(bias, first_ref):
    row = lax.broadcasted_iota(jnp.int32, bias.shape, 0)
    column = lax.broadcasted_iota(jnp.int32, bias.shape, 1)
    bias[...] = jnp.where((column <= row) & (column >= first_ref[...]), 0.0, NEG)


def attend_kernel(
    planes, start_ref, tokens_ref, first_ref, cosine_ref, sine_ref, *refs
):
    blocks, refs = refs[:planes], refs[planes:]
    attn_in_ref, heads_ref, attended_ref, log_ref, small_ref, weight, bias, sems = refs
    rows_count = tokens_ref.shape[0]
    copies = load_rows(blocks, start_ref, weight, sems)
    fill_bias(bias, first_ref)
    inputs = tokens_ref[...].astype(jnp.float32)
    inverse = lax.rsqrt(jnp.mean(inputs * inputs, -1, keepdims=True) + EPS)
    normed = inputs * inverse
    for copy in copies:
        copy.wait()
    width_q, width_kv = HEADS * HEAD_DIM, KV_HEADS * HEAD_DIM
    width = width_q + 2 * width_kv
    small = jnp.transpose(weight[:, width:].astype(jnp.float32))
    small_ref[...] = small[:16, :]
    experts = small_ref.shape[0] - 8
    attn_in_ref[...] = (normed * small[experts : experts + 1, :]).astype(jnp.bfloat16)
    for at in range(0, width, LANES):
        raw = jnp.dot(
            attn_in_ref[...], weight[:, at : at + LANES], preferred_element_type=jnp.float32
        )
        for column in range(0, LANES, HEAD_DIM):
            values = raw[:, column : column + HEAD_DIM]
            if at + column < width_q + width_kv:
                values = turned(values, cosine_ref[...], sine_ref[...])
            heads_ref[:, at + column : at + column + HEAD_DIM] = values.astype(jnp.bfloat16)
    half = rows_count // 2
    for block in range(2):
        rows, reach = pl.ds(block * half, half), (block + 1) * half
        logs = jnp.zeros((half, 128), jnp.float32)
        lane = lax.broadcasted_iota(jnp.int32, logs.shape, 1)
        for head in range(HEADS):
            key_at = width_q + head // (HEADS // KV_HEADS) * HEAD_DIM
            value_at = key_at + width_kv
            scores = wide_dot(
                heads_ref[rows, head * HEAD_DIM : (head + 1) * HEAD_DIM],
                heads_ref[:reach, key_at : key_at + HEAD_DIM],
            )
            scores = scores * HEAD_DIM ** (-0.5) + bias[rows, :reach]
            peak = jnp.max(scores, -1, keepdims=True)
            exponent = jnp.exp(scores - peak)
            total = jnp.sum(exponent, -1, keepdims=True)
            mixed = jnp.dot(
                exponent.astype(jnp.bfloat16),
                heads_ref[:reach, value_at : value_at + HEAD_DIM],
                preferred_element_type=jnp.float32,
            )
            attended_ref[rows, head * HEAD_DIM : (head + 1) * HEAD_DIM] = (
                mixed * (1.0 / total)
            ).astype(jnp.bfloat16)
            logs = jnp.where(lane == head, peak + jnp.log(total), logs)
        log_ref[rows, :] = logs


def attend_call(starts, tokens, first, cosine, sine, blocks, width_early):
    rows_count = tokens.shape[0]
    width = (HEADS + 2 * KV_HEADS) * HEAD_DIM
    low = jnp.bfloat16
    return pl.pallas_call(
        functools.partial(attend_kernel, len(blocks)),
        out_shape=[
            jax.ShapeDtypeStruct((rows_count, D), low),
            jax.ShapeDtypeStruct((rows_count, width), low),
            jax.ShapeDtypeStruct((rows_count, HEADS * HEAD_DIM), low),
            jax.ShapeDtypeStruct((rows_count, 128), jnp.float32),
            jax.ShapeDtypeStruct((16, D), jnp.float32),
        ],
        in_specs=[scalars()] + [whole()] * 4 + [anywhere()] * len(blocks),
        out_specs=[whole()] * 5,
        scratch_shapes=[
            pltpu.VMEM((D, width_early), low),
            pltpu.VMEM((rows_count, rows_count), jnp.float32),
            pltpu.SemaphoreType.DMA((len(blocks) * blocks[0].shape[0],)),
        ],
        compiler_params=pltpu.CompilerParams(vmem_limit_bytes=62 << 20),
        cost_estimate=small_cost(),
        name="attend",
    )(starts, tokens, first, cosine, sine, *blocks)


def middle_kernel(planes, column, start_ref, tokens_ref, attended_ref, routes_ref, small_ref, *refs):
    blocks, refs = refs[:planes], refs[planes:]
    residual_ref, packed_ref, gates_ref, weight, sems = refs
    step = pl.program_id(0)
    tile = tokens_ref.shape[0]
    rows_count = packed_ref.shape[0] - 16
    experts = gates_ref.shape[0]

    @pl.when(step == 0)
    def _():
        for copy in load_rows(blocks, start_ref, weight, sems, column):
            copy.wait()

    for at in range(0, D, LANES):
        residual_ref[:, at : at + LANES] = tokens_ref[:, at : at + LANES].astype(
            jnp.float32
        ) + jnp.dot(
            attended_ref[...], weight[:, at : at + LANES], preferred_element_type=jnp.float32
        )
    residual = residual_ref[...]
    inverse = lax.rsqrt(jnp.mean(residual * residual, -1, keepdims=True) + EPS)
    rows = pl.ds(pl.multiple_of(step * tile, tile), tile)
    packed_ref[rows, :] = (
        residual * inverse * small_ref[experts + 1 : experts + 2, :]
    ).astype(jnp.bfloat16)
    logits = wide_dot(small_ref[...].astype(jnp.bfloat16), tokens_ref[...])[:experts, :]
    expert = lax.broadcasted_iota(jnp.int32, logits.shape, 0)
    routed = expert == routes_ref[:1, :]
    for choice in range(1, TOP):
        routed = routed | (expert == routes_ref[choice : choice + 1, :])
    logits = jnp.where(routed, logits, NEG)
    exponent = jnp.exp(logits - jnp.max(logits, 0, keepdims=True))
    exponent = jnp.where(routed, exponent, 0.0)
    gates = exponent / jnp.sum(exponent, 0, keepdims=True)
    gates_ref[...] = gates
    high = gates.astype(jnp.bfloat16)
    rest = gates - high.astype(jnp.float32)
    middle = rest.astype(jnp.bfloat16)
    rest = rest - middle.astype(jnp.float32)
    for part, values in enumerate((high.astype(jnp.float32), middle.astype(jnp.float32), rest)):
        lanes = pl.ds(pl.multiple_of(part * rows_count + step * tile, tile), tile)
        packed_ref[rows_count:, lanes] = jnp.concatenate(
            [values, jnp.zeros((16 - experts, tile), jnp.float32)], 0
        ).astype(jnp.bfloat16)


def middle_call(starts, tokens, attended, routes, small, blocks, experts, column):
    rows_count = tokens.shape[0]
    tile = rows_count // 2
    low = jnp.bfloat16
    tiled = pl.BlockSpec((tile, D), lambda i: (i, 0))
    lanes = lambda rows: pl.BlockSpec((rows, tile), lambda i: (0, i))
    return pl.pallas_call(
        functools.partial(middle_kernel, len(blocks), column),
        grid=(2,),
        out_shape=[
            jax.ShapeDtypeStruct((rows_count, D), jnp.float32),
            jax.ShapeDtypeStruct((rows_count + 16, D), low),
            jax.ShapeDtypeStruct((experts, rows_count), jnp.float32),
        ],
        in_specs=[
            scalars(),
            tiled,
            tiled,
            lanes(routes.shape[0]),
            pl.BlockSpec((16, D), lambda i: (0, 0)),
        ]
        + [anywhere()] * len(blocks),
        out_specs=[
            tiled,
            pl.BlockSpec((rows_count + 16, D), lambda i: (0, 0)),
            lanes(experts),
        ],
        scratch_shapes=[
            pltpu.VMEM((D, D), low),
            pltpu.SemaphoreType.DMA((len(blocks) * blocks[0].shape[0],)),
        ],
        compiler_params=pltpu.CompilerParams(vmem_limit_bytes=62 << 20),
        cost_estimate=small_cost(),
        name="middle",
    )(starts, tokens, attended, routes, small, *blocks)


def middle_back_kernel(planes, column, start_ref, *refs):
    terms, tails, refs = refs[:4], refs[4:8], refs[8:]
    residual_ref, small_ref, cot_ref, tokens_ref, gates_ref, refs = *refs[:5], refs[5:]
    blocks, refs = refs[:planes], refs[planes:]
    mid_ref, low_ref, attended_grad_ref, logits_grad_ref, small_grad_ref, weight, sems = refs
    step = pl.program_id(0)
    experts = gates_ref.shape[0]
    rows_count = gates_ref.shape[1]

    @pl.when(step == 0)
    def _():
        copies = load_rows(blocks, start_ref, weight, sems, column)
        del copies
        gates = gates_ref[...]
        parts = sum([tail[:experts, :].astype(jnp.float32) for tail in tails])
        grad = (
            parts[:, :rows_count]
            + parts[:, rows_count : 2 * rows_count]
            + parts[:, 2 * rows_count :]
        )
        grad = gates * (grad - jnp.sum(gates * grad, 0, keepdims=True))
        logits_grad_ref[...] = jnp.concatenate(
            [grad, jnp.zeros((16 - experts, rows_count), jnp.float32)], 0
        ).astype(jnp.bfloat16)
        small_grad_ref[...] = jnp.zeros_like(small_grad_ref)

    grad = sum([term[...].astype(jnp.float32) for term in terms])
    residual = residual_ref[...]
    inverse = lax.rsqrt(jnp.mean(residual * residual, -1, keepdims=True) + EPS)
    normed = residual * inverse
    product = grad * normed
    small_grad_ref[experts : experts + 1, :] += jnp.sum(product, 0, keepdims=True)
    tile = tokens_ref.shape[0]
    lanes = pl.ds(pl.multiple_of(step * tile, tile), tile)
    small_grad_ref[:experts, :] += jnp.dot(
        logits_grad_ref[:, lanes], tokens_ref[...], preferred_element_type=jnp.float32
    )[:experts, :]
    gain = small_ref[experts + 1 : experts + 2, :]
    mean = jnp.mean(product * gain, -1, keepdims=True)
    mid = cot_ref[...].astype(jnp.float32) + inverse * (grad * gain - normed * mean)
    mid_ref[...] = mid
    low_ref[...] = mid.astype(jnp.bfloat16)

    @pl.when(step == 0)
    def _():
        for copy in load_rows(blocks, start_ref, weight, sems, column, False):
            copy.wait()

    for at in range(0, D, LANES):
        attended_grad_ref[:, at : at + LANES] = wide_dot(
            low_ref[...], weight[at : at + LANES, :]
        ).astype(jnp.bfloat16)


def middle_back_call(
    starts, terms, residual, small, cotangent, tokens, gates, blocks, column
):
    rows_count = residual.shape[0]
    tile = rows_count // 2
    low = jnp.bfloat16
    tiled = pl.BlockSpec((tile, D), lambda i: (i, 0))
    fixed = lambda rows, columns: pl.BlockSpec((rows, columns), lambda i: (0, 0))
    tail = pl.BlockSpec((16, D), lambda i: (rows_count // 16, 0))
    return pl.pallas_call(
        functools.partial(middle_back_kernel, len(blocks), column),
        grid=(2,),
        out_shape=[
            jax.ShapeDtypeStruct((rows_count, D), jnp.float32),
            jax.ShapeDtypeStruct((rows_count, D), low),
            jax.ShapeDtypeStruct((rows_count, D), low),
            jax.ShapeDtypeStruct((16, rows_count), low),
            jax.ShapeDtypeStruct((16, D), jnp.float32),
        ],
        in_specs=[scalars()]
        + [tiled] * 4
        + [tail] * 4
        + [tiled, fixed(16, D), tiled, tiled, fixed(*gates.shape)]
        + [anywhere()] * len(blocks),
        out_specs=[tiled, tiled, tiled, fixed(16, rows_count), fixed(16, D)],
        scratch_shapes=[
            pltpu.VMEM((D, D), low),
            pltpu.SemaphoreType.DMA((len(blocks) * blocks[0].shape[0],)),
        ],
        compiler_params=pltpu.CompilerParams(vmem_limit_bytes=62 << 20),
        cost_estimate=small_cost(),
        name="middle_back",
    )(starts, *terms, *terms, residual, small, cotangent, tokens, gates, *blocks)


def attend_back_kernel(heads_ref, grad_ref, log_ref, first_ref, cosine_ref, sine_ref, raw_ref, bias):
    rows_count = heads_ref.shape[0]
    width_q, width_kv = HEADS * HEAD_DIM, KV_HEADS * HEAD_DIM
    half = rows_count // 2
    scale = HEAD_DIM ** (-0.5)
    fill_bias(bias, first_ref)
    cosine, sine = cosine_ref[...], -sine_ref[...]
    for key_head in range(KV_HEADS):
        key_at = width_q + key_head * HEAD_DIM
        value_at = key_at + width_kv
        key_grads, value_grads = [], []
        for block in range(2):
            rows, reach = slice(block * half, (block + 1) * half), (block + 1) * half
            keys = heads_ref[:reach, key_at : key_at + HEAD_DIM]
            values = heads_ref[:reach, value_at : value_at + HEAD_DIM]
            key_grad = jnp.zeros((reach, HEAD_DIM), jnp.float32)
            value_grad = jnp.zeros((reach, HEAD_DIM), jnp.float32)
            for head in range(key_head * HEADS // KV_HEADS, (key_head + 1) * HEADS // KV_HEADS):
                columns = slice(head * HEAD_DIM, (head + 1) * HEAD_DIM)
                queries, grads = heads_ref[rows, columns], grad_ref[rows, columns]
                scores = wide_dot(queries, keys) * scale + bias[rows, :reach]
                chances = jnp.exp(scores - log_ref[rows, head : head + 1])
                pulled = wide_dot(grads, values)
                shift = jnp.sum(chances * pulled, -1, keepdims=True)
                score_grad = (chances * (pulled - shift)).astype(jnp.bfloat16)
                value_grad = value_grad + tall_dot(chances.astype(jnp.bfloat16), grads)
                key_grad = key_grad + tall_dot(score_grad, queries)
                query_grad = (
                    jnp.dot(score_grad, keys, preferred_element_type=jnp.float32) * scale
                )
                raw_ref[rows, columns] = turned(
                    query_grad, cosine[rows, :], sine[rows, :]
                ).astype(jnp.bfloat16)
            key_grads.append(key_grad)
            value_grads.append(value_grad)
        key_grad = jnp.concatenate([key_grads[0] + key_grads[1][:half], key_grads[1][half:]], 0)
        value_grad = jnp.concatenate(
            [value_grads[0] + value_grads[1][:half], value_grads[1][half:]], 0
        )
        raw_ref[:, key_at : key_at + HEAD_DIM] = turned(key_grad * scale, cosine, sine).astype(
            jnp.bfloat16
        )
        raw_ref[:, value_at : value_at + HEAD_DIM] = value_grad.astype(jnp.bfloat16)


def attend_back_call(heads, grads, logs, first, cosine, sine):
    rows_count = heads.shape[0]
    return pl.pallas_call(
        attend_back_kernel,
        out_shape=jax.ShapeDtypeStruct(heads.shape, jnp.bfloat16),
        in_specs=[whole()] * 6,
        out_specs=whole(),
        scratch_shapes=[pltpu.VMEM((rows_count, rows_count), jnp.float32)],
        compiler_params=pltpu.CompilerParams(vmem_limit_bytes=62 << 20),
        cost_estimate=small_cost(),
        name="attend_back",
    )(heads, grads, logs, first, cosine, sine)


def shard_grad_kernel(extra, start_ref, left_ref, right_ref, *refs):
    parts, grad, sems = refs[extra:-2], refs[-2], refs[-1]
    width = right_ref.shape[1]
    pairs, pieces, rows = parts[0].shape[:3]
    owners = 2 * pairs
    tall = owners * rows
    copies = []
    if extra:
        small = refs[0][...]
        small = jnp.concatenate([small, jnp.zeros((128 - small.shape[0], D), jnp.float32)], 0)
        grad[:, width:] = jnp.transpose(small).astype(jnp.bfloat16)
    for p in range(pieces):
        for at in range(0, width, WIDE):
            grad[p * tall : (p + 1) * tall, at : at + WIDE] = tall_dot(
                left_ref[:, p * tall : (p + 1) * tall], right_ref[:, at : at + WIDE]
            ).astype(jnp.bfloat16)
        to = lax.rem(start_ref[0] + pieces - p, pieces)
        for i in range(owners):
            at = pl.multiple_of(p * tall + start_ref[1 + i] * rows, 16)
            copy = pltpu.make_async_copy(
                grad.at[pl.ds(at, rows)], parts[i % 2].at[i // 2, to], sems.at[p * owners + i]
            )
            copy.start()
            copies.append(copy)
    for copy in copies:
        copy.wait()


def shard_grad_call(spots, left, right, pieces, owners, small=None):
    extra = [] if small is None else [small]
    width, height = right.shape[1] + 128 * len(extra), left.shape[1]
    rows = height // (pieces * owners)
    return pl.pallas_call(
        functools.partial(shard_grad_kernel, len(extra)),
        out_shape=[jax.ShapeDtypeStruct((owners // 2, pieces, rows, width), jnp.bfloat16)] * 2,
        in_specs=[scalars()] + [whole()] * (2 + len(extra)),
        out_specs=[anywhere()] * 2,
        scratch_shapes=[
            pltpu.VMEM((height, width), jnp.bfloat16),
            pltpu.SemaphoreType.DMA((pieces * owners,)),
        ],
        compiler_params=pltpu.CompilerParams(vmem_limit_bytes=62 << 20),
        cost_estimate=small_cost(),
        name="shard_grad",
    )(spots, left, right, *extra)


def entry_back_kernel(planes, start_ref, *refs):
    raw_ref, tokens_ref, mid_ref, small_ref, logits_grad_ref, refs = *refs[:5], refs[5:]
    blocks, refs = refs[:planes], refs[planes:]
    grad_ref, weight, sems = refs
    step = pl.program_id(0)
    width = raw_ref.shape[1]
    experts = small_ref.shape[0] - 8
    tile = tokens_ref.shape[0]

    @pl.when(step == 0)
    def _():
        for copy in load_rows(blocks, start_ref, weight, sems):
            copy.wait()

    for at in range(0, D, LANES):
        grad_ref[:, at : at + LANES] = wide_dot(raw_ref[...], weight[at : at + LANES, :width])
    inputs = tokens_ref[...].astype(jnp.float32)
    inverse = lax.rsqrt(jnp.mean(inputs * inputs, -1, keepdims=True) + EPS)
    normed = inputs * inverse
    grad = grad_ref[...]
    gain = small_ref[experts : experts + 1, :]
    mean = jnp.mean(grad * normed * gain, -1, keepdims=True)
    row = lax.broadcasted_iota(jnp.int32, (16, 1), 0)
    router = jnp.where(row < experts, small_ref[...], 0.0).astype(jnp.bfloat16)
    grad_ref[...] = (
        mid_ref[...]
        + inverse * (grad * gain - normed * mean)
        + tall_dot(logits_grad_ref[...], router)
    )


def entry_back_call(
    starts, raw_grad, tokens, mid_grad, small, logits_grad, blocks, width_early
):
    rows_count = tokens.shape[0]
    tile = rows_count // 2
    tiled = lambda columns: pl.BlockSpec((tile, columns), lambda i: (i, 0))
    fixed = lambda rows, columns: pl.BlockSpec((rows, columns), lambda i: (0, 0))
    return pl.pallas_call(
        functools.partial(entry_back_kernel, len(blocks)),
        grid=(2,),
        out_shape=jax.ShapeDtypeStruct((rows_count, D), jnp.float32),
        in_specs=[
            scalars(),
            tiled(raw_grad.shape[1]),
            tiled(D),
            tiled(D),
            fixed(16, D),
            pl.BlockSpec((16, tile), lambda i: (0, i)),
        ]
        + [anywhere()] * len(blocks),
        out_specs=tiled(D),
        scratch_shapes=[
            pltpu.VMEM((D, width_early), jnp.bfloat16),
            pltpu.SemaphoreType.DMA((len(blocks) * blocks[0].shape[0],)),
        ],
        compiler_params=pltpu.CompilerParams(vmem_limit_bytes=62 << 20),
        cost_estimate=small_cost(),
        name="entry_back",
    )(starts, raw_grad, tokens, mid_grad, small, logits_grad, *blocks)


def pipeline(loads, stores, body, count, later=()):
    coming = {}

    def fetch(i):
        coming[i] = loads(i, i % 2)
        for copy in coming[i]:
            copy.start()

    leaving = {}
    fetch(0)
    for copy in later:
        copy.start()
    for i in range(count):
        if i + 1 < count:
            fetch(i + 1)
        for copy in coming.pop(i):
            copy.wait()
        for copy in leaving.pop(i - 2, []):
            copy.wait()
        body(i, i % 2)
        leaving[i] = stores(i, i % 2)
        for copy in leaving[i]:
            copy.start()
    for i in sorted(leaving):
        for copy in leaving[i]:
            copy.wait()


def copies_of(pairs, sems):
    return [
        pltpu.make_async_copy(source, target, sems.at[j])
        for j, (source, target) in enumerate(pairs)
    ]


def hidden_kernel(count, pieces, tokens_count, place_ref, *refs):
    rows_in, chunks, refs = refs[:count], refs[count : count + pieces], refs[count + pieces :]
    outs, refs = refs[: 3 * count], refs[3 * count :]
    weight, rows, slope, product, gated, sems, in_sems, out_sems = refs
    weight_copies = load_weight(chunks, place_ref, weight, sems)

    def loads(i, slot):
        return copies_of([(rows_in[i], rows.at[slot])], in_sems.at[slot])

    def stores(i, slot):
        buffers = (slope, product, gated)
        return copies_of(
            [(buffer.at[slot], outs[j * count + i]) for j, buffer in enumerate(buffers)],
            out_sems.at[slot],
        )

    def body(i, slot):
        if i == 0:
            for copy in weight_copies:
                copy.wait()
        weights = spread(expert_row(rows[slot, tokens_count:, :], place_ref[4]), tokens_count)
        weights = jnp.concatenate([weights] * (LANES // 128), 1)
        for at in range(0, FF, LANES):
            gate = jnp.dot(
                rows[slot, :tokens_count, :],
                weight[:, at : at + LANES],
                preferred_element_type=jnp.float32,
            )
            up = jnp.dot(
                rows[slot, :tokens_count, :],
                weight[:, FF + at : FF + at + LANES],
                preferred_element_type=jnp.float32,
            )
            square = gate * gate
            bend = jnp.tanh(0.7978845608028654 * gate * (1.0 + 0.044715 * square))
            half = 0.5 + 0.5 * bend
            steep = half + 0.5 * gate * (1.0 - bend * bend) * (
                0.7978845608028654 + 0.10703222440890037 * square
            )
            active = gate * half
            both = (active * up).astype(jnp.bfloat16)
            slope[slot, :, at : at + LANES] = (up * steep).astype(jnp.bfloat16)
            slope[slot, :, FF + at : FF + at + LANES] = active.astype(jnp.bfloat16)
            product[slot, :, at : at + LANES] = both
            gated[slot, :, at : at + LANES] = (both.astype(jnp.float32) * weights).astype(
                jnp.bfloat16
            )

    pipeline(loads, stores, body, count)


def hidden_call(rows_in, chunks, places, tokens_count):
    count = len(rows_in)
    low = jnp.bfloat16
    widths = [2 * FF, FF, FF]
    outs = pl.pallas_call(
        functools.partial(hidden_kernel, count, len(chunks), tokens_count),
        out_shape=[
            jax.ShapeDtypeStruct((tokens_count, width), low)
            for width in widths
            for _ in range(count)
        ],
        in_specs=[scalars()] + [anywhere()] * (count + len(chunks)),
        out_specs=[anywhere()] * (3 * count),
        scratch_shapes=[
            pltpu.VMEM((D, 2 * FF), low),
            pltpu.VMEM((2, *rows_in[0].shape), low),
            *[pltpu.VMEM((2, tokens_count, width), low) for width in widths],
            pltpu.SemaphoreType.DMA((len(chunks),)),
            pltpu.SemaphoreType.DMA((2, 1)),
            pltpu.SemaphoreType.DMA((2, 3)),
        ],
        compiler_params=pltpu.CompilerParams(vmem_limit_bytes=62 << 20),
        cost_estimate=small_cost(),
        name="expert_hidden",
    )(places, *rows_in, *chunks)
    return outs[:count], outs[count : 2 * count], outs[2 * count :]


def spread(row, tokens_count):
    return jnp.transpose(jnp.broadcast_to(row, (128, tokens_count)))


def expert_row(block, expert):
    third = block.shape[1] // 3
    index = lax.broadcasted_iota(jnp.int32, block.shape, 0)
    row = jnp.sum(jnp.where(index == expert, block.astype(jnp.float32), 0.0), 0, keepdims=True)
    return row[:, :third] + row[:, third : 2 * third] + row[:, 2 * third :]


def split_row(row):
    high = row.astype(jnp.bfloat16)
    rest = row - high.astype(jnp.float32)
    middle = rest.astype(jnp.bfloat16)
    low = (rest - middle.astype(jnp.float32)).astype(jnp.bfloat16)
    return jnp.concatenate(
        [high.astype(jnp.float32), middle.astype(jnp.float32), low.astype(jnp.float32)], 1
    )


def pull_kernel(count, pieces, tokens_count, place_ref, *refs):
    packed, cots, slopes, products = (refs[i * count : (i + 1) * count] for i in range(4))
    refs = refs[4 * count :]
    in_chunks, out_chunks, refs = refs[: pieces[0]], refs[pieces[0] : sum(pieces)], refs[sum(pieces) :]
    row_grads, hidden_grads, refs = refs[:count], refs[count : 2 * count], refs[2 * count :]
    in_weight, out_weight, tail, cot, slope, product, grad, hidden, *sems = refs
    expert = place_ref[4]
    in_copies, out_copies = [], []

    def loads(i, slot):
        copies = copies_of(
            [
                (packed[i].at[pl.ds(tokens_count, 16)], tail.at[slot]),
                (cots[i], cot.at[slot]),
                (slopes[i], slope.at[slot]),
                (products[i], product.at[slot]),
            ],
            sems[2].at[slot],
        )
        return copies

    def stores(i, slot):
        return copies_of(
            [(grad.at[slot], row_grads[i]), (hidden.at[slot], hidden_grads[i])], sems[3].at[slot]
        )

    def body(i, slot):
        if i == 0:
            for copy in out_copies:
                copy.wait()
        weights = spread(expert_row(tail[slot], expert), tokens_count)
        weights = jnp.concatenate([weights] * (LANES // 128), 1)
        gate_grad = jnp.zeros((tokens_count, 1), jnp.float32)
        for at in range(0, FF, LANES):
            pulled = wide_dot(cot[slot], out_weight[at : at + LANES, :])
            both = product[slot, :, at : at + LANES].astype(jnp.float32)
            gate_grad = gate_grad + jnp.sum(pulled * both, 1, keepdims=True)
            pulled = pulled * weights
            for base in (at, FF + at):
                hidden[slot, :, base : base + LANES] = (
                    pulled * slope[slot, :, base : base + LANES].astype(jnp.float32)
                ).astype(jnp.bfloat16)
        row = jnp.transpose(jnp.broadcast_to(gate_grad, (tokens_count, 128)))[:1, :]
        parts = jnp.broadcast_to(split_row(row), (16, 3 * tokens_count))
        index = lax.broadcasted_iota(jnp.int32, parts.shape, 0)
        grad[slot, tokens_count:, :] = jnp.where(index == expert, parts, 0.0).astype(jnp.bfloat16)
        if i == 0:
            for copy in in_copies:
                copy.wait()
        for at in range(0, D, LANES):
            grad[slot, :tokens_count, at : at + LANES] = wide_dot(
                hidden[slot], in_weight[at : at + LANES, :]
            ).astype(jnp.bfloat16)

    out_copies += load_weight(out_chunks, place_ref, out_weight, sems[1])
    in_copies += load_weight(in_chunks, place_ref, in_weight, sems[0], False)
    pipeline(loads, stores, body, count, in_copies)


def pull_call(packed, cots, slopes, products, in_chunks, out_chunks, places, tokens_count):
    count = len(packed)
    low = jnp.bfloat16
    out_shapes = [(tokens_count + 16, D), (tokens_count, 2 * FF)]
    outs = pl.pallas_call(
        functools.partial(
            pull_kernel, count, (len(in_chunks), len(out_chunks)), tokens_count
        ),
        out_shape=[jax.ShapeDtypeStruct(shape, low) for shape in out_shapes for _ in range(count)],
        in_specs=[scalars()] + [anywhere()] * (4 * count + len(in_chunks) + len(out_chunks)),
        out_specs=[anywhere()] * (2 * count),
        scratch_shapes=[
            pltpu.VMEM((D, 2 * FF), low),
            pltpu.VMEM((FF, D), low),
            pltpu.VMEM((2, 16, D), low),
            pltpu.VMEM((2, tokens_count, D), low),
            pltpu.VMEM((2, tokens_count, 2 * FF), low),
            pltpu.VMEM((2, tokens_count, FF), low),
            pltpu.VMEM((2, tokens_count + 16, D), low),
            pltpu.VMEM((2, tokens_count, 2 * FF), low),
            pltpu.SemaphoreType.DMA((len(in_chunks),)),
            pltpu.SemaphoreType.DMA((len(out_chunks),)),
            pltpu.SemaphoreType.DMA((2, 4)),
            pltpu.SemaphoreType.DMA((2, 2)),
        ],
        compiler_params=pltpu.CompilerParams(vmem_limit_bytes=62 << 20),
        cost_estimate=small_cost(),
        name="expert_pull",
    )(places, *packed, *cots, *slopes, *products, *in_chunks, *out_chunks)
    return outs[:count], outs[count:]


def product_kernel(count, place_ref, *refs):
    gated, chunks, refs = refs[:count], refs[count : count + 4], refs[count + 4 :]
    rows_out, (weight, left, total, *sems) = refs[:count], refs[count:]
    weight_copies = load_weight(chunks, place_ref, weight, sems[0])

    def loads(i, slot):
        return copies_of([(gated[i], left.at[slot])], sems[1].at[slot])

    def stores(i, slot):
        return copies_of([(total.at[slot], rows_out[i])], sems[2].at[slot])

    def body(i, slot):
        if i == 0:
            for copy in weight_copies:
                copy.wait()
        for at in range(0, D, LANES):
            total[slot, :, at : at + LANES] = jnp.dot(
                left[slot], weight[:, at : at + LANES], preferred_element_type=jnp.float32
            ).astype(jnp.bfloat16)

    pipeline(loads, stores, body, count)


def product_call(gated, chunks, places):
    count, rows = len(gated), gated[0].shape[0]
    return pl.pallas_call(
        functools.partial(product_kernel, count),
        out_shape=[jax.ShapeDtypeStruct((rows, D), jnp.bfloat16)] * count,
        in_specs=[scalars()] + [anywhere()] * (count + 4),
        out_specs=[anywhere()] * count,
        scratch_shapes=[
            pltpu.VMEM((FF, D), jnp.bfloat16),
            pltpu.VMEM((2, rows, FF), jnp.bfloat16),
            pltpu.VMEM((2, rows, D), jnp.bfloat16),
            pltpu.SemaphoreType.DMA((4,)),
            pltpu.SemaphoreType.DMA((2, 1)),
            pltpu.SemaphoreType.DMA((2, 1)),
        ],
        compiler_params=pltpu.CompilerParams(vmem_limit_bytes=62 << 20),
        cost_estimate=small_cost(),
        name="expert_rows",
    )(places, *gated, *chunks)


def weight_grad_kernel(count, rows, *refs):
    left, right, grad = refs[:count], refs[count : 2 * count], refs[2 * count]
    total = tall_dot(left[0][:rows, :], right[0][:rows, :])
    for i in range(1, count):
        total = total + tall_dot(left[i][:rows, :], right[i][:rows, :])
    grad[...] = total.astype(grad.dtype)


def weight_grad_call(left, right, rows, tall, name):
    count = len(left)
    height, width = left[0].shape[1], right[0].shape[1]
    return pl.pallas_call(
        functools.partial(weight_grad_kernel, count, rows),
        grid=(height // tall, width // WIDE),
        out_shape=jax.ShapeDtypeStruct((height, width), jnp.bfloat16),
        in_specs=[pl.BlockSpec((rows, tall), lambda i, j: (0, i))] * count
        + [pl.BlockSpec((rows, WIDE), lambda i, j: (0, j))] * count,
        out_specs=pl.BlockSpec((tall, WIDE), lambda i, j: (i, j)),
        compiler_params=pltpu.CompilerParams(vmem_limit_bytes=62 << 20),
        cost_estimate=small_cost(),
        name=name,
    )(*left, *right)


def plane_shards(
    tokens,
    cotangent,
    routes,
    doc_lengths,
    query_weight,
    query_first,
    query_second,
    keyvalue_weight,
    keyvalue_first,
    keyvalue_second,
    output_weight,
    output_first,
    output_second,
    router_weight,
    router_first,
    router_second,
    norm_gains,
    gains_first,
    gains_second,
    expert_in,
    expert_in_first,
    expert_in_second,
    expert_out,
    expert_out_first,
    expert_out_second,
):
    rows_count = tokens.shape[0]
    experts = router_weight.shape[1]
    columns_dp, owners = lax.axis_size("dp"), lax.axis_size("expert")
    dp_index, expert_index = lax.axis_index("dp"), lax.axis_index("expert")
    core = expert_index & 1
    ring = [(i, (i + 1) % columns_dp) for i in range(columns_dp)]
    shard = query_weight.shape[0]
    width_q = HEADS * HEAD_DIM
    width_qkv = (HEADS + 2 * KV_HEADS) * HEAD_DIM
    low = jnp.bfloat16
    places = (dp_index - jnp.arange(columns_dp, dtype=jnp.int32)) % columns_dp
    starts = (
        (expert_index ^ jnp.arange(owners, dtype=jnp.int32))[:, None] + places[None, :] * owners
    ).reshape(-1) * shard
    places = jnp.concatenate([places, expert_index[None]]).astype(jnp.int32)
    spots = jnp.concatenate([dp_index[None], expert_index ^ jnp.arange(owners)]).astype(jnp.int32)

    position = jnp.arange(rows_count, dtype=jnp.int32)
    ends = jnp.cumsum(doc_lengths[0])
    first = jnp.max(jnp.where(position[:, None] >= ends[None, :], ends[None, :], 0), 1)
    offset = (position - first).astype(jnp.float32)
    frequency = ROPE_BASE ** (-2.0 * jnp.arange(HEAD_DIM // 2, dtype=jnp.float32) / HEAD_DIM)
    angles = offset[:, None] * frequency[None, :]
    cosine = jnp.tile(jnp.cos(angles), (1, 2))
    sine = jnp.concatenate([-jnp.sin(angles), jnp.sin(angles)], 1)
    first = first[:, None]

    width_early = width_qkv + 128

    def cross(block):
        return to_x(block), to_y(block)

    def onward(from_x, from_y):
        return jnp.where(core == 0, from_y, from_x)

    sent = jnp.concatenate(
        [
            query_weight.astype(low),
            keyvalue_weight.astype(low),
            router_weight.astype(low),
            norm_gains.T.astype(low),
            jnp.zeros((shard, 128 - experts - 2), low),
            output_weight.astype(low),
        ],
        1,
    )

    def around(value):
        return lax.ppermute(value, "dp", ring)

    cot_x, cot_y = cross(cotangent)
    in_low, out_low = expert_in[0].astype(low), expert_out[0].astype(low)
    column = [sent, around(sent)]
    column.append(around(column[1]))
    column[2], in_low, out_low, cosine, sine, first, routes_t = hold(
        column[2], in_low, out_low, cosine, sine, first, routes.T
    )
    column.append(around(column[2]))
    joint = jnp.stack(column)
    cut = in_low.shape[0] * 5 // 8
    cot_x, cot_y, joint, in_low, out_low = hold(cot_x, cot_y, joint, in_low, out_low)
    in_near, in_rest, out_chunks = [in_low[:cut]], [in_low[cut:]], [out_low]

    joint_x, joint_y = cross(joint)
    joint_core = to_core(joint)
    in_near.append(around(in_near[0]))
    in_rest.append(around(in_rest[0]))
    joint_x, joint_y, joint_core, in_near, in_rest, cot_x, cot_y = hold(
        joint_x, joint_y, joint_core, in_near, in_rest, cot_x, cot_y
    )
    joint_far = forward(onward(joint_x, joint_y))
    joint_x2, joint_y2 = to_core(joint_x), to_core(joint_y)
    cot_x2 = to_core(cot_x)
    in_near.append(around(in_near[1]))
    outward = onward(cot_x, cot_y)
    joint_far, joint_x2, joint_y2, in_near, in_rest, cot_x2, cot_y, outward = hold(
        joint_far, joint_x2, joint_y2, in_near, in_rest, cot_x2, cot_y, outward
    )
    joint_far2 = to_core(joint_far)
    joint_far2, outward, cot_y, in_near, in_rest = hold(
        joint_far2, outward, cot_y, in_near, in_rest
    )
    plane = [joint, joint_core, joint_x, joint_x2, joint_y, joint_y2, joint_far, joint_far2]

    cot_far = forward(outward)
    cot_core, cot_y2 = to_core(cotangent), to_core(cot_y)
    in_near.append(around(in_near[2]))
    in_rest.append(around(in_rest[1]))
    attn_in, heads, attended, logs, small = attend_call(
        starts, tokens, first, cosine, sine, plane, width_early
    )
    residual_mid, packed, gates = middle_call(
        starts, tokens, attended, routes_t, small, plane, experts, width_early
    )
    packed, cot_far, cot_core, cot_y2, in_near, in_rest, out_chunks = hold(
        packed, cot_far, cot_core, cot_y2, in_near, in_rest, out_chunks
    )

    packed_x, packed_y = cross(packed)
    packed_core = to_core(packed)
    in_rest.append(around(in_rest[2]))
    in_chunks = in_near + in_rest
    out_chunks.append(around(after(out_chunks[0], in_rest[3])))
    slopes, products, gated = [None] * 8, [None] * 8, [None] * 8
    packed_blocks = [packed, packed_core] + [None] * 6

    def hidden(order, *earlier):
        blocks = [packed_blocks[k] for k in order]
        blocks[0] = after(blocks[0], *earlier)
        for k, *outs in zip(order, *hidden_call(blocks, in_chunks, places, rows_count)):
            slopes[k], products[k], gated[k] = outs

    hidden((0, 1))
    packed_x, packed_y, gated[0], out_chunks, cot_far = hold(
        packed_x, packed_y, gated[0], out_chunks, cot_far
    )
    outward = onward(packed_x, packed_y)
    outward, packed_x, packed_y = hold(outward, packed_x, packed_y)
    packed_x2, packed_y2 = to_core(packed_x), to_core(packed_y)
    packed_far = forward(outward)
    cot_far2 = to_core(cot_far)
    out_chunks.append(around(out_chunks[1]))
    cot_blocks = [cotangent, cot_core, cot_x, cot_x2, cot_y, cot_y2, cot_far, cot_far2]
    packed_blocks[2:6] = [packed_x, packed_x2, packed_y, packed_y2]
    hidden((2, 4))
    hidden((3, 5), gated[2])
    packed_far, out_chunks, gated[3] = hold(packed_far, out_chunks, gated[3])
    packed_far2 = to_core(packed_far)
    packed_blocks[6:] = hold(packed_far, packed_far2)
    out_chunks.append(around(after(out_chunks[2], packed_far2)))
    hidden((6, 7))
    out_grad = weight_grad_call(gated, cot_blocks, rows_count, FF, "expert_out_grad")
    out_grad, out_chunks = hold(out_grad, out_chunks)

    def column_piece(value, back):
        rows = value.shape[0] // columns_dp
        return lax.dynamic_slice_in_dim(value, places[back] * rows, rows, 0)

    moving = column_piece(out_grad, 1)
    row_grads, hidden_grads, rows_out = [None] * 8, [None] * 8, [None] * 8

    def pick(values, order):
        return [values[k] for k in order]

    def pull(order, *earlier):
        first_cot = after(cot_blocks[order[0]], *earlier)
        outs = pull_call(
            pick(packed_blocks, order),
            [first_cot] + pick(cot_blocks, order[1:]),
            pick(slopes, order),
            pick(products, order),
            in_chunks,
            out_chunks,
            places,
            rows_count,
        )
        for k, row_grad, hidden_grad in zip(order, *outs):
            row_grads[k], hidden_grads[k] = row_grad, hidden_grad

    def rows_of(order, *earlier):
        first_gated = after(gated[order[0]], *earlier)
        outs = product_call([first_gated] + pick(gated, order[1:]), out_chunks, places)
        for k, rows in zip(order, outs):
            rows_out[k] = rows

    zero = jnp.zeros((), low)

    def by_core(value, wanted):
        return jnp.where(core == wanted, value, zero)

    rows_of((7, 6), moving)
    rows_out[6], rows_out[7], moving = hold(rows_out[6], rows_out[7], moving)
    moved = around(moving)
    rows_back = to_core(rows_out[7])
    pull((7, 6), rows_out[6])
    moved, rows_back, row_grads[6], row_grads[7] = hold(
        moved, rows_back, row_grads[6], row_grads[7]
    )
    far_back = to_core(row_grads[7])
    rows_far = add_low(rows_out[6], rows_back)
    moving = add_low(moved, column_piece(out_grad, 2))
    far_back, rows_far, moving = hold(far_back, rows_far, moving)
    far = add_low(row_grads[6], far_back)
    far, rows_far, moving = hold(far, rows_far, moving)
    relayed, rows_relayed = forward(far), forward(rows_far)
    moved = around(moving)
    pull((0, 1, 3, 2, 5, 4), far, rows_far, moving)
    relayed, moved, row_grads[:6] = hold(relayed, moved, row_grads[:6])
    back_x, back_y = to_core(row_grads[3]), to_core(row_grads[5])
    back_own = to_core(row_grads[1])
    rows_of((5, 4, 3, 2, 1, 0), row_grads[0])
    moving = add_low(moved, column_piece(out_grad, 3))
    back_x, back_y, back_own, rows_out[:6], moving = hold(
        back_x, back_y, back_own, rows_out[:6], moving
    )
    by_x = add_low(row_grads[2], back_x, by_core(relayed, 1))
    by_y = add_low(row_grads[4], back_y, by_core(relayed, 0))
    by_x, by_y, moving, hidden_grads[0], rows_out[:6], rows_relayed = hold(
        by_x, by_y, moving, hidden_grads[0], rows_out[:6], rows_relayed
    )

    from_x, from_y = to_x(by_x), to_y(by_y)
    moved = around(moving)
    rows_backs = [to_core(rows_out[k]) for k in (3, 5)]
    in_grad = weight_grad_call(packed_blocks, hidden_grads, rows_count, FF, "expert_in_grad")
    rows_x = add_low(rows_out[2], rows_backs[0], by_core(rows_relayed, 1))
    rows_y = add_low(rows_out[4], rows_backs[1], by_core(rows_relayed, 0))
    cut = in_low.shape[0] * 5 // 8

    def in_pieces(back):
        piece = column_piece(in_grad, back)
        return piece[:cut], piece[cut:]

    near, rest = in_pieces(1)
    from_x, from_y, moved, near, rest, rows_out[:2], rows_x, rows_y = hold(
        from_x, from_y, moved, near, rest, rows_out[:2], rows_x, rows_y
    )
    expert_out_sum = moved.astype(jnp.float32) + column_piece(out_grad, 0).astype(jnp.float32)

    rows_from_x, rows_from_y = to_x(rows_x), to_y(rows_y)
    rows_back = to_core(rows_out[1])
    near_moved, rest_moved = around(near), around(rest)
    mid_grad, mid_low, attended_grad, logits_grad, small_grad = middle_back_call(
        starts, [after(row_grads[0], rows_x), back_own, from_x, from_y], residual_mid,
        small, cotangent, tokens, gates, plane, width_early,
    )
    raw_grad = attend_back_call(heads, attended_grad, logs, first, cosine, sine)
    early_even, early_odd = shard_grad_call(spots, attn_in, raw_grad, columns_dp, owners)
    early_even, early_odd, mid_low, rows_back, near_moved, rest_moved = hold(
        early_even, early_odd, mid_low, rows_back, near_moved, rest_moved
    )
    rest = add_low(rest_moved, in_pieces(2)[1])
    rest, early_odd, rows_from_x, rows_from_y = hold(rest, early_odd, rows_from_x, rows_from_y)
    early_back = to_core(early_odd)
    rest_moved = around(rest)
    near = add_low(near_moved, in_pieces(2)[0])
    output_even, output_odd = shard_grad_call(
        spots, attended, mid_low, columns_dp, owners, small_grad
    )
    early_back, output_even, output_odd, near, rest_moved = hold(
        early_back, output_even, output_odd, near, rest_moved
    )
    near_moved = around(near)
    early_far = add_low(early_even[3], early_back[3])
    early_far, output_odd, output_even = hold(early_far, output_odd, output_even)

    early_relayed = forward(early_far)
    output_back = to_core(output_odd)
    tokens_grad = entry_back_call(
        starts, after(raw_grad, early_far), tokens, mid_grad, small, logits_grad,
        plane, width_early,
    )
    early_pairs = add_low(early_even[:3], early_back[:3])
    rest = add_low(rest_moved, in_pieces(3)[1])
    early_relayed, output_back, tokens_grad, early_pairs, near_moved, rest = hold(
        early_relayed, output_back, tokens_grad, early_pairs, near_moved, rest
    )
    early_x = add_low(early_pairs[1], by_core(early_relayed, 1))
    early_y = add_low(early_pairs[2], by_core(early_relayed, 0))
    output_far = add_low(output_even[3], output_back[3])
    near = add_low(near_moved, in_pieces(3)[0])
    early_x, early_y, output_far, near, expert_out_sum, rows_back = hold(
        early_x, early_y, output_far, near, expert_out_sum, rows_back
    )
    early_x, early_y, output_relayed = to_x(early_x), to_y(early_y), forward(output_far)
    near_moved, rest_moved = around(near), around(rest)
    output_pairs = add_low(output_even[:3], output_back[:3])
    block_out = residual_mid + add_low_wide(rows_out[0], rows_back, rows_from_x, rows_from_y)
    mixed_out = block_out.astype(low)
    early_x, early_y, output_relayed, output_pairs, near_moved, rest_moved = hold(
        early_x, early_y, output_relayed, output_pairs, near_moved, rest_moved
    )
    early_total = add_low(early_pairs[0], early_x, early_y)
    output_x = add_low(output_pairs[1], by_core(output_relayed, 1))
    output_y = add_low(output_pairs[2], by_core(output_relayed, 0))
    early_total, output_x, output_y = hold(early_total, output_x, output_y)

    def spread_pieces(total):
        return [total[0]] + [
            lax.ppermute(total[p], "dp", [(i, (i - p) % columns_dp) for i in range(columns_dp)])
            for p in range(1, columns_dp)
        ]

    early_pieces = spread_pieces(early_total)
    output_x, output_y = to_x(output_x), to_y(output_y)
    expert_in_sum = jnp.concatenate([near_moved, rest_moved]).astype(
        jnp.float32
    ) + column_piece(in_grad, 0).astype(jnp.float32)
    early_pieces, output_x, output_y = hold(early_pieces, output_x, output_y)
    output_total = add_low(output_pairs[0], output_x, output_y)
    output_pieces = spread_pieces(output_total)
    output_sum = add_low_wide(*output_pieces)
    summed = add_low_wide(*early_pieces)
    used = sent[:, :width_qkv].astype(jnp.float32)
    gain_one = sent[:, width_qkv + experts].astype(jnp.float32)
    gain_one_sum = jnp.sum(used * summed, 1) / gain_one
    at = width_qkv
    sums = (
        summed[:, :width_q],
        summed[:, width_q:at],
        output_sum[:, :D],
        output_sum[:, D : D + experts],
        jnp.stack([gain_one_sum, output_sum[:, D + experts]]),
        expert_in_sum[None],
        expert_out_sum[None],
    )
    (
        (query_weight, query_first, query_second),
        (keyvalue_weight, keyvalue_first, keyvalue_second),
        (output_weight, output_first, output_second),
        (router_weight, router_first, router_second),
        (norm_gains, gains_first, gains_second),
        _,
    ) = hold(
        (query_weight, query_first, query_second),
        (keyvalue_weight, keyvalue_first, keyvalue_second),
        (output_weight, output_first, output_second),
        (router_weight, router_first, router_second),
        (norm_gains, gains_first, gains_second),
        early_total,
    )
    weights = (
        (query_weight, query_first, query_second),
        (keyvalue_weight, keyvalue_first, keyvalue_second),
        (output_weight, output_first, output_second),
        (router_weight, router_first, router_second),
        (norm_gains, gains_first, gains_second),
        (expert_in, expert_in_first, expert_in_second),
        (expert_out, expert_out_first, expert_out_second),
    )
    updates = []
    for state, grad, rate, decay in zip(
        weights, sums, learning_rates(), (DECAY, DECAY, DECAY, DECAY, 0.0, DECAY, DECAY)
    ):
        updates.extend(adam_update(*state, grad, rate, decay))
    return (mixed_out, tokens_grad, *updates)


def solution(mesh):
    in_specs = (
        P(("dp", "expert"), None),
        P(("dp", "expert"), None),
        P(("dp", "expert"), None),
        P(("dp", "expert"), None),
        P(("dp", "expert"), None),
        P(("dp", "expert"), None),
        P(("dp", "expert"), None),
        P(("dp", "expert"), None),
        P(("dp", "expert"), None),
        P(("dp", "expert"), None),
        P(("dp", "expert"), None),
        P(("dp", "expert"), None),
        P(("dp", "expert"), None),
        P(("dp", "expert"), None),
        P(("dp", "expert"), None),
        P(("dp", "expert"), None),
        P(None, ("dp", "expert")),
        P(None, ("dp", "expert")),
        P(None, ("dp", "expert")),
        P("expert", "dp", None),
        P("expert", "dp", None),
        P("expert", "dp", None),
        P("expert", "dp", None),
        P("expert", "dp", None),
        P("expert", "dp", None),
    )
    out_specs = (
        P(("dp", "expert"), None),
        P(("dp", "expert"), None),
        P(("dp", "expert"), None),
        P(("dp", "expert"), None),
        P(("dp", "expert"), None),
        P(("dp", "expert"), None),
        P(("dp", "expert"), None),
        P(("dp", "expert"), None),
        P(("dp", "expert"), None),
        P(("dp", "expert"), None),
        P(("dp", "expert"), None),
        P(("dp", "expert"), None),
        P(("dp", "expert"), None),
        P(("dp", "expert"), None),
        P(None, ("dp", "expert")),
        P(None, ("dp", "expert")),
        P(None, ("dp", "expert")),
        P("expert", "dp", None),
        P("expert", "dp", None),
        P("expert", "dp", None),
        P("expert", "dp", None),
        P("expert", "dp", None),
        P("expert", "dp", None),
    )
    def body(tokens, *rest):
        one_plane = mesh.shape["expert"] == 8 and rest[12].shape[1] == 8
        fits = one_plane and 3 * tokens.shape[0] == D
        return (plane_shards if fits else shards)(tokens, *rest)

    return jax.shard_map(body, mesh=mesh, in_specs=in_specs, out_specs=out_specs, check_vma=False)
```

```python
import functools

import jax
import jax.numpy as jnp
from jax import lax
from jax.experimental import pallas as pl
from jax.experimental.pallas import tpu as pltpu
from jax.sharding import PartitionSpec as P

D = 1536
FF = 768
HEADS = 12
KV_HEADS = 2
HEAD_DIM = 128
TOP = 4
STEP = 10


EPS = 1e-06
NEG = -1e30
BETA_ONE = 0.9
BETA_TWO = 0.999
ADAM_EPS = 1e-08
DECAY = 0.1
ROPE_BASE = 10000.0
RATE_SCALE = 2.5
GAIN_RATE = 0.6


def doc_tables(lengths, rows_count):
    position = jnp.arange(rows_count, dtype=jnp.int32)
    doc_ends = jnp.cumsum(lengths)
    doc_starts = doc_ends - lengths
    doc_index = jnp.sum((position[:, None] >= doc_ends[None, :]).astype(jnp.int32), 1)
    doc_hot = doc_index[:, None] == jnp.arange(lengths.shape[0], dtype=jnp.int32)[None, :]
    start_of = jnp.sum(jnp.where(doc_hot, doc_starts[None, :], 0), 1)
    offset = (position - start_of).astype(jnp.float32)
    frequency = ROPE_BASE ** (-2.0 * jnp.arange(HEAD_DIM // 2, dtype=jnp.float32) / HEAD_DIM)
    angles = offset[:, None] * frequency[None, :]
    allowed = (doc_index[:, None] == doc_index[None, :]) & (position[None, :] <= position[:, None])
    return (jnp.cos(angles), jnp.sin(angles), allowed)


def rotate(values, cos_table, sin_table):
    half_width = values.shape[-1] // 2
    first_half = values[..., :half_width]
    second_half = values[..., half_width:]
    cosine = cos_table[:, None, :]
    sine_part = sin_table[:, None, :]
    return jnp.concatenate(
        [
            first_half * cosine - second_half * sine_part,
            second_half * cosine + first_half * sine_part,
        ],
        -1,
    )


def rotate_back(grads, cos_table, sin_table):
    half_width = grads.shape[-1] // 2
    first_half = grads[..., :half_width]
    second_half = grads[..., half_width:]
    cosine = cos_table[:, None, :]
    sine_part = sin_table[:, None, :]
    return jnp.concatenate(
        [
            first_half * cosine + second_half * sine_part,
            second_half * cosine - first_half * sine_part,
        ],
        -1,
    )


def gelu_tanh(values):
    return jax.nn.gelu(values, approximate=True)


def learning_rates():
    return (
        RATE_SCALE * D ** (-0.5),
        RATE_SCALE * D ** (-0.5),
        RATE_SCALE * (D // 32) ** (-0.5),
        RATE_SCALE * (4 * D) ** (-0.5),
        GAIN_RATE,
        RATE_SCALE * D ** (-0.5),
        RATE_SCALE * (FF // 8) ** (-0.5),
    )


def adam_update(weight, first, second, grad, rate, decay):
    new_first = BETA_ONE * first + (1.0 - BETA_ONE) * grad
    new_second = BETA_TWO * second + (1.0 - BETA_TWO) * grad * grad
    first_hat = new_first / (1.0 - BETA_ONE**STEP)
    second_hat = new_second / (1.0 - BETA_TWO**STEP)
    new_weight = weight - rate * (first_hat / (jnp.sqrt(second_hat) + ADAM_EPS) + decay * weight)
    return (new_first, new_second, new_weight)


def shards(
    tokens,
    cotangent,
    routes,
    doc_lengths,
    query_weight,
    query_first,
    query_second,
    keyvalue_weight,
    keyvalue_first,
    keyvalue_second,
    output_weight,
    output_first,
    output_second,
    router_weight,
    router_first,
    router_second,
    norm_gains,
    gains_first,
    gains_second,
    expert_in,
    expert_in_first,
    expert_in_second,
    expert_out,
    expert_out_first,
    expert_out_second,
):
    rows_count = tokens.shape[0]
    experts = router_weight.shape[1]
    owners = lax.axis_size("expert")
    per_owner = expert_in.shape[0]
    capacity = 3 * rows_count * TOP // (2 * experts)
    groups = HEADS // KV_HEADS
    width_kv = KV_HEADS * HEAD_DIM
    score_scale = HEAD_DIM ** (-0.5)
    query_full, keyvalue_full, output_full, router_full, gains_full = (
        lax.all_gather(query_weight.astype(jnp.bfloat16), ("dp", "expert"), axis=0, tiled=True),
        lax.all_gather(keyvalue_weight.astype(jnp.bfloat16), ("dp", "expert"), axis=0, tiled=True),
        lax.all_gather(output_weight.astype(jnp.bfloat16), ("dp", "expert"), axis=0, tiled=True),
        lax.all_gather(router_weight.astype(jnp.bfloat16), ("dp", "expert"), axis=0, tiled=True),
        lax.all_gather(norm_gains.astype(jnp.bfloat16), ("dp", "expert"), axis=1, tiled=True),
    )
    in_full, out_full = (
        lax.all_gather(expert_in.astype(jnp.bfloat16), "dp", axis=1, tiled=True),
        lax.all_gather(expert_out.astype(jnp.bfloat16), "dp", axis=1, tiled=True),
    )
    gain_attn = gains_full[0].astype(jnp.float32)
    gain_moe = gains_full[1].astype(jnp.float32)
    cos_table, sin_table, allowed = doc_tables(doc_lengths[0], rows_count)
    inputs = tokens.astype(jnp.float32)
    inv_one = lax.rsqrt(jnp.mean(inputs * inputs, -1, keepdims=True) + EPS)
    normed_one = inputs * inv_one
    attn_in = (normed_one * gain_attn).astype(jnp.bfloat16)
    query_raw = jnp.dot(attn_in, query_full, preferred_element_type=jnp.float32)
    keyvalue_raw = jnp.dot(attn_in, keyvalue_full, preferred_element_type=jnp.float32)
    queries = (
        rotate(query_raw.reshape(rows_count, HEADS, HEAD_DIM), cos_table, sin_table)
        .astype(jnp.bfloat16)
        .reshape(rows_count, KV_HEADS, groups, HEAD_DIM)
    )
    keys_rot = rotate(
        keyvalue_raw[:, :width_kv].reshape(rows_count, KV_HEADS, HEAD_DIM), cos_table, sin_table
    ).astype(jnp.bfloat16)
    values_in = (
        keyvalue_raw[:, width_kv:].reshape(rows_count, KV_HEADS, HEAD_DIM).astype(jnp.bfloat16)
    )

    def score_table():
        raw_scores = (
            jnp.einsum("tkgd,skd->kgts", queries, keys_rot, preferred_element_type=jnp.float32)
            * score_scale
        )
        return jnp.where(allowed[None, None], raw_scores, NEG)

    scores = score_table()
    row_max = jnp.max(scores, -1, keepdims=True)
    exponent = jnp.exp(scores - row_max)
    totals = jnp.sum(exponent, -1, keepdims=True)
    probabilities = exponent / totals
    log_sum = row_max + jnp.log(totals)
    attended = jnp.einsum(
        "kgts,skd->tkgd",
        probabilities.astype(jnp.bfloat16),
        values_in,
        preferred_element_type=jnp.float32,
    )
    attended = attended.reshape(rows_count, HEADS * HEAD_DIM).astype(jnp.bfloat16)
    residual_mid = inputs + jnp.dot(attended, output_full, preferred_element_type=jnp.float32)
    inv_two = lax.rsqrt(jnp.mean(residual_mid * residual_mid, -1, keepdims=True) + EPS)
    normed_two = residual_mid * inv_two
    moe_in = (normed_two * gain_moe).astype(jnp.bfloat16)
    logits = jnp.dot(tokens, router_full, preferred_element_type=jnp.float32)
    expert_ids = jnp.arange(experts, dtype=jnp.int32)
    route_hot = routes[:, :, None] == expert_ids[None, None, :]
    picked = jnp.sum(jnp.where(route_hot, logits[:, None, :], 0.0), -1)
    gate_weights = jax.nn.softmax(picked, axis=-1)
    flat_routes = routes.reshape(-1)
    flat_hot = (flat_routes[:, None] == expert_ids[None, :]).astype(jnp.int32)
    slot_index = jnp.sum((jnp.cumsum(flat_hot, 0) - 1) * flat_hot, 1)
    destination = flat_routes * capacity + slot_index
    route_ids = jnp.arange(rows_count * TOP, dtype=jnp.int32)
    source_route = jnp.zeros((experts * capacity,), jnp.int32).at[destination].set(route_ids)
    slot_used = jnp.zeros((experts * capacity,), jnp.bool_).at[destination].set(True)
    source_token = source_route // TOP
    zero_row = jnp.zeros((), jnp.bfloat16)
    send_rows = jnp.where(slot_used[:, None], moe_in[source_token], zero_row).reshape(
        owners, per_owner, capacity, D
    )
    received = lax.all_to_all(send_rows, "expert", split_axis=0, concat_axis=0, tiled=True)
    hidden_pre = jnp.einsum("sicd,idf->sicf", received, in_full, preferred_element_type=jnp.float32)
    gate_part = hidden_pre[..., :FF]
    up_part = hidden_pre[..., FF:]
    activated, gelu_pull = jax.vjp(gelu_tanh, gate_part)
    product = (activated * up_part).astype(jnp.bfloat16)
    expert_rows = jnp.einsum(
        "sicf,ifd->sicd", product, out_full, preferred_element_type=jnp.float32
    ).astype(jnp.bfloat16)
    returned = lax.all_to_all(
        expert_rows, "expert", split_axis=0, concat_axis=0, tiled=True
    ).reshape(experts * capacity, D)
    routed = returned[destination].reshape(rows_count, TOP, D)
    block_out = residual_mid + jnp.sum(gate_weights[:, :, None] * routed, 1)
    mixed_out = block_out.astype(jnp.bfloat16)
    upstream = cotangent.astype(jnp.float32)
    gate_grad = jnp.einsum("tjd,td->tj", routed, cotangent, preferred_element_type=jnp.float32)
    picked_grad = gate_weights * (gate_grad - jnp.sum(gate_weights * gate_grad, -1, keepdims=True))
    logits_grad = jnp.sum(jnp.where(route_hot, picked_grad[:, :, None], 0.0), 1).astype(
        jnp.bfloat16
    )
    rows_grad = (
        (gate_weights[:, :, None] * upstream[:, None, :])
        .astype(jnp.bfloat16)
        .reshape(rows_count * TOP, D)
    )
    send_grad = jnp.where(slot_used[:, None], rows_grad[source_route], zero_row).reshape(
        owners, per_owner, capacity, D
    )
    received_grad = lax.all_to_all(send_grad, "expert", split_axis=0, concat_axis=0, tiled=True)
    product_grad = jnp.einsum(
        "sicd,ifd->sicf", received_grad, out_full, preferred_element_type=jnp.float32
    )
    out_weight_grad = jnp.einsum(
        "sicf,sicd->ifd", product, received_grad, preferred_element_type=jnp.float32
    )
    gate_part_grad = gelu_pull(product_grad * up_part)[0]
    up_part_grad = product_grad * activated
    hidden_grad = jnp.concatenate([gate_part_grad, up_part_grad], -1).astype(jnp.bfloat16)
    in_weight_grad = jnp.einsum(
        "sicd,sicf->idf", received, hidden_grad, preferred_element_type=jnp.float32
    )
    input_rows_grad = jnp.einsum(
        "sicf,idf->sicd", hidden_grad, in_full, preferred_element_type=jnp.float32
    ).astype(jnp.bfloat16)
    returned_grad = lax.all_to_all(
        input_rows_grad, "expert", split_axis=0, concat_axis=0, tiled=True
    ).reshape(experts * capacity, D)
    moe_in_grad = jnp.sum(
        returned_grad[destination].reshape(rows_count, TOP, D).astype(jnp.float32), 1
    )
    gain_two_grad = jnp.sum(moe_in_grad * normed_two, 0)
    scaled_two = moe_in_grad * gain_moe
    mid_grad = upstream + inv_two * (
        scaled_two - normed_two * jnp.mean(scaled_two * normed_two, -1, keepdims=True)
    )
    attn_out_grad = mid_grad.astype(jnp.bfloat16)
    output_weight_grad = jnp.einsum(
        "tc,td->cd", attended, attn_out_grad, preferred_element_type=jnp.float32
    )
    attended_grad = jnp.einsum(
        "td,cd->tc", attn_out_grad, output_full, preferred_element_type=jnp.float32
    )
    attended_grad = attended_grad.astype(jnp.bfloat16).reshape(
        rows_count, KV_HEADS, groups, HEAD_DIM
    )
    probs_again = jnp.exp(score_table() - log_sum)
    prob_grad = jnp.einsum(
        "tkgd,skd->kgts", attended_grad, values_in, preferred_element_type=jnp.float32
    )
    delta_sum = jnp.sum(probs_again * prob_grad, -1, keepdims=True)
    score_grad = (probs_again * (prob_grad - delta_sum)).astype(jnp.bfloat16)
    values_grad = jnp.einsum(
        "kgts,tkgd->skd",
        probs_again.astype(jnp.bfloat16),
        attended_grad,
        preferred_element_type=jnp.float32,
    )
    queries_grad = (
        jnp.einsum("kgts,skd->tkgd", score_grad, keys_rot, preferred_element_type=jnp.float32)
        * score_scale
    )
    keys_grad = (
        jnp.einsum("kgts,tkgd->skd", score_grad, queries, preferred_element_type=jnp.float32)
        * score_scale
    )
    query_raw_grad = rotate_back(
        queries_grad.reshape(rows_count, HEADS, HEAD_DIM), cos_table, sin_table
    )
    query_raw_grad = query_raw_grad.astype(jnp.bfloat16).reshape(rows_count, HEADS * HEAD_DIM)
    key_raw_grad = (
        rotate_back(keys_grad, cos_table, sin_table)
        .astype(jnp.bfloat16)
        .reshape(rows_count, width_kv)
    )
    keyvalue_grad = jnp.concatenate(
        [key_raw_grad, values_grad.astype(jnp.bfloat16).reshape(rows_count, width_kv)], -1
    )
    query_weight_grad = jnp.einsum(
        "tc,tf->cf", attn_in, query_raw_grad, preferred_element_type=jnp.float32
    )
    keyvalue_weight_grad = jnp.einsum(
        "tc,tf->cf", attn_in, keyvalue_grad, preferred_element_type=jnp.float32
    )
    attn_in_grad = jnp.einsum(
        "tf,cf->tc", query_raw_grad, query_full, preferred_element_type=jnp.float32
    )
    attn_in_grad = attn_in_grad + jnp.einsum(
        "tf,cf->tc", keyvalue_grad, keyvalue_full, preferred_element_type=jnp.float32
    )
    gain_one_grad = jnp.sum(attn_in_grad * normed_one, 0)
    scaled_one = attn_in_grad * gain_attn
    tokens_grad = mid_grad + inv_one * (
        scaled_one - normed_one * jnp.mean(scaled_one * normed_one, -1, keepdims=True)
    )
    tokens_grad = tokens_grad + jnp.einsum(
        "te,ce->tc", logits_grad, router_full, preferred_element_type=jnp.float32
    )
    router_weight_grad = jnp.einsum(
        "tc,te->ce", tokens, logits_grad, preferred_element_type=jnp.float32
    )
    gains_grad = jnp.stack([gain_one_grad, gain_two_grad], 0)
    reduced = (
        lax.psum_scatter(query_weight_grad, ("dp", "expert"), scatter_dimension=0, tiled=True),
        lax.psum_scatter(keyvalue_weight_grad, ("dp", "expert"), scatter_dimension=0, tiled=True),
        lax.psum_scatter(output_weight_grad, ("dp", "expert"), scatter_dimension=0, tiled=True),
        lax.psum_scatter(router_weight_grad, ("dp", "expert"), scatter_dimension=0, tiled=True),
        lax.psum_scatter(gains_grad, ("dp", "expert"), scatter_dimension=1, tiled=True),
    )
    expert_sums = (
        lax.psum_scatter(
            in_weight_grad.astype(jnp.bfloat16), "dp", scatter_dimension=1, tiled=True
        ).astype(jnp.float32),
        lax.psum_scatter(
            out_weight_grad.astype(jnp.bfloat16), "dp", scatter_dimension=1, tiled=True
        ).astype(jnp.float32),
    )
    rates = learning_rates()
    query_upd = adam_update(query_weight, query_first, query_second, reduced[0], rates[0], DECAY)
    keyvalue_upd = adam_update(
        keyvalue_weight, keyvalue_first, keyvalue_second, reduced[1], rates[1], DECAY
    )
    output_upd = adam_update(
        output_weight, output_first, output_second, reduced[2], rates[2], DECAY
    )
    router_upd = adam_update(
        router_weight, router_first, router_second, reduced[3], rates[3], DECAY
    )
    gains_upd = adam_update(norm_gains, gains_first, gains_second, reduced[4], rates[4], 0.0)
    in_upd = adam_update(
        expert_in, expert_in_first, expert_in_second, expert_sums[0], rates[5], DECAY
    )
    out_upd = adam_update(
        expert_out, expert_out_first, expert_out_second, expert_sums[1], rates[6], DECAY
    )
    return (
        mixed_out,
        tokens_grad,
        query_upd[0],
        query_upd[1],
        query_upd[2],
        keyvalue_upd[0],
        keyvalue_upd[1],
        keyvalue_upd[2],
        output_upd[0],
        output_upd[1],
        output_upd[2],
        router_upd[0],
        router_upd[1],
        router_upd[2],
        gains_upd[0],
        gains_upd[1],
        gains_upd[2],
        in_upd[0],
        in_upd[1],
        in_upd[2],
        out_upd[0],
        out_upd[1],
        out_upd[2],
    )


def flip(mask):
    return [(i, i ^ mask) for i in range(8)]


ACROSS_X, ACROSS_Y, ACROSS_CORE = flip(2), flip(4), flip(1)
FORWARD = [(i, i ^ (4 if i & 1 else 2)) for i in range(8)]


def after(value, *earlier):
    return lax.optimization_barrier((value, *earlier))[0]


def hold(*values):
    return lax.optimization_barrier(values)


def to_x(value):
    return lax.ppermute(value, "expert", ACROSS_X)


def to_y(value):
    return lax.ppermute(value, "expert", ACROSS_Y)


def to_core(value):
    return lax.ppermute(value, "expert", ACROSS_CORE)


def to_far(value):
    return lax.ppermute(value, "expert", flip(6))


def forward(value):
    return lax.ppermute(value, "expert", FORWARD)


def gather_plane(value, core):
    from_x, from_y = to_x(value), to_y(value)
    from_core = to_core(value)
    from_far = forward(jnp.where(core == 0, from_y, from_x))
    return [
        value,
        from_core,
        from_x,
        to_core(from_x),
        from_y,
        to_core(from_y),
        from_far,
        to_core(from_far),
    ]


def add_low(*terms):
    total = terms[0].astype(jnp.float32)
    for term in terms[1:]:
        total = total + term.astype(jnp.float32)
    return total.astype(jnp.bfloat16)


def add_low_wide(*terms):
    return sum([term.astype(jnp.float32) for term in terms])


def scatter_plane(parts, core):
    far = add_low(parts[6], to_core(parts[7]))
    relayed = forward(far)
    by_x = add_low(parts[2], to_core(parts[3]))
    by_y = add_low(parts[4], to_core(parts[5]))
    own = add_low(parts[0], to_core(parts[1]))
    zero = jnp.zeros((), jnp.bfloat16)
    by_x = add_low(by_x, jnp.where(core == 1, relayed, zero))
    by_y = add_low(by_y, jnp.where(core == 0, relayed, zero))
    return own, to_x(by_x), to_y(by_y)


def gather_column(value, ring):
    values = [value]
    for _ in range(len(ring) - 1):
        values.append(lax.ppermute(values[-1], "dp", ring))
    return values


def scatter_column(value, ring, place):
    count = len(ring)
    rows = value.shape[0] // count

    def piece(shard):
        return lax.dynamic_slice_in_dim(value, (shard % count) * rows, rows, 0)

    moving = piece(place + count - 1)
    for step in range(count - 2):
        moving = add_low(lax.ppermute(moving, "dp", ring), piece(place + count - 2 - step))
    return lax.ppermute(moving, "dp", ring).astype(jnp.float32) + piece(place).astype(jnp.float32)


def scatter_pieces(pieces, ring):
    moving = pieces[1]
    for piece in pieces[2:]:
        moving = add_low(lax.ppermute(moving, "dp", ring), piece)
    return lax.ppermute(moving, "dp", ring).astype(jnp.float32) + pieces[0].astype(jnp.float32)


def anywhere():
    return pl.BlockSpec(memory_space=pl.ANY)


def scalars():
    return pl.BlockSpec(memory_space=pltpu.SMEM)


def whole():
    return pl.BlockSpec(memory_space=pltpu.VMEM)


def small_cost():
    return pl.CostEstimate(flops=1024, bytes_accessed=1024, transcendentals=0)


def load_rows(blocks, start_ref, joined, sems, column=0, start=True):
    width = joined.shape[1]
    pieces, rows = blocks[0].shape[0], blocks[0].shape[1]
    copies = []
    for i, block in enumerate(blocks):
        for p in range(pieces):
            at = pl.multiple_of(start_ref[i * pieces + p], 16)
            copies.append(
                pltpu.make_async_copy(
                    block.at[p, :, pl.ds(column, width)],
                    joined.at[pl.ds(at, rows)],
                    sems.at[i * pieces + p],
                )
            )
    for copy in copies if start else []:
        copy.start()
    return copies


def wide_dot(left, right):
    return lax.dot_general(
        left, right, (((1,), (1,)), ((), ())), preferred_element_type=jnp.float32
    )


def tall_dot(left, right):
    return lax.dot_general(
        left, right, (((0,), (0,)), ((), ())), preferred_element_type=jnp.float32
    )


def load_weight(chunks, place_ref, buffer, sems, start=True):
    total = sum([chunk.shape[0] for chunk in chunks[::4]])
    copies, offset = [], 0
    for j, chunk in enumerate(chunks):
        rows = chunk.shape[0]
        at = pl.multiple_of(place_ref[j % 4] * total + offset, 16)
        copies.append(pltpu.make_async_copy(chunk, buffer.at[pl.ds(at, rows)], sems.at[j]))
        if j % 4 == 3:
            offset += rows
    for copy in copies if start else []:
        copy.start()
    return copies


LANES = 256
WIDE = 512


def turned(values, cosine, sine):
    return values * cosine + pltpu.roll(values, HEAD_DIM // 2, 1) * sine


def fill_bias(bias, first):
    row = lax.broadcasted_iota(jnp.int32, bias.shape, 0)
    column = lax.broadcasted_iota(jnp.int32, bias.shape, 1).astype(jnp.float32)
    row = row.astype(jnp.float32)
    bias[...] = jnp.where((column <= row) & (column >= first), 0.0, NEG)


def attend_kernel(planes, start_ref, tokens_ref, table_ref, routes_ref, *refs):
    blocks, refs = refs[:planes], refs[planes:]
    attn_in_out, heads_out, attended_out, residual_out, packed_out, *refs = refs
    log_ref, small_ref, gates_ref, *refs = refs
    weight, late, bias, table, attn_in_ref, heads_ref, attended_ref, *refs = refs
    residual_ref, packed_ref, sems, late_sems, out_sems = refs
    rows_count = tokens_ref.shape[0]
    width_q, width_kv = HEADS * HEAD_DIM, KV_HEADS * HEAD_DIM
    width = width_q + 2 * width_kv
    table_copy = pltpu.make_async_copy(table_ref, table, out_sems.at[0])
    table_copy.start()
    copies = load_rows(blocks, start_ref, weight, sems)
    late_copies = load_rows(blocks, start_ref, late, late_sems, weight.shape[1])
    table_copy.wait()
    leaving = []

    def store(source, target):
        leaving.append(pltpu.make_async_copy(source, target, out_sems.at[1 + len(leaving)]))
        leaving[-1].start()

    fill_bias(bias, table[:, 2 * HEAD_DIM : 2 * HEAD_DIM + 1])
    inputs = tokens_ref[...].astype(jnp.float32)
    inverse = lax.rsqrt(jnp.mean(inputs * inputs, -1, keepdims=True) + EPS)
    normed = inputs * inverse
    for copy in copies:
        copy.wait()
    small = jnp.transpose(weight[:, width:].astype(jnp.float32))
    small_ref[...] = small[:16, :]
    experts = small_ref.shape[0] - 8
    attn_in_ref[...] = (normed * small[experts : experts + 1, :]).astype(jnp.bfloat16)
    store(attn_in_ref, attn_in_out)
    cosine, sine = table[:, :HEAD_DIM], table[:, HEAD_DIM : 2 * HEAD_DIM]
    for at in range(0, width, LANES):
        raw = jnp.dot(
            attn_in_ref[...], weight[:, at : at + LANES], preferred_element_type=jnp.float32
        )
        for column in range(0, LANES, HEAD_DIM):
            values = raw[:, column : column + HEAD_DIM]
            if at + column < width_q + width_kv:
                values = turned(values, cosine, sine)
            heads_ref[:, at + column : at + column + HEAD_DIM] = values.astype(jnp.bfloat16)
    store(heads_ref, heads_out)

    logits = wide_dot(small_ref[...].astype(jnp.bfloat16), tokens_ref[...])[:experts, :]
    expert = lax.broadcasted_iota(jnp.int32, logits.shape, 0)
    routed = expert == routes_ref[:1, :]
    for choice in range(1, TOP):
        routed = routed | (expert == routes_ref[choice : choice + 1, :])
    logits = jnp.where(routed, logits, NEG)
    exponent = jnp.exp(logits - jnp.max(logits, 0, keepdims=True))
    exponent = jnp.where(routed, exponent, 0.0)
    gates = exponent / jnp.sum(exponent, 0, keepdims=True)
    gates_ref[...] = gates
    packed_ref[rows_count:, :] = jnp.concatenate(
        [split_row(gates), jnp.zeros((16 - experts, D), jnp.float32)], 0
    ).astype(jnp.bfloat16)
    store(packed_ref.at[pl.ds(rows_count, 16)], packed_out.at[pl.ds(rows_count, 16)])

    half = rows_count // 2
    for block in range(2):
        rows, reach = pl.ds(block * half, half), (block + 1) * half
        logs = jnp.zeros((half, 128), jnp.float32)
        lane = lax.broadcasted_iota(jnp.int32, logs.shape, 1)
        for head in range(HEADS):
            key_at = width_q + head // (HEADS // KV_HEADS) * HEAD_DIM
            value_at = key_at + width_kv
            scores = wide_dot(
                heads_ref[rows, head * HEAD_DIM : (head + 1) * HEAD_DIM],
                heads_ref[:reach, key_at : key_at + HEAD_DIM],
            )
            scores = scores * HEAD_DIM ** (-0.5) + bias[rows, :reach]
            peak = jnp.max(scores, -1, keepdims=True)
            exponent = jnp.exp(scores - peak)
            total = jnp.sum(exponent, -1, keepdims=True)
            mixed = jnp.dot(
                exponent.astype(jnp.bfloat16),
                heads_ref[:reach, value_at : value_at + HEAD_DIM],
                preferred_element_type=jnp.float32,
            )
            attended_ref[rows, head * HEAD_DIM : (head + 1) * HEAD_DIM] = (
                mixed * (1.0 / total)
            ).astype(jnp.bfloat16)
            logs = jnp.where(lane == head, peak + jnp.log(total), logs)
        log_ref[rows, :] = logs
        store(attended_ref.at[rows], attended_out.at[rows])
        if block == 0:
            for copy in late_copies:
                copy.wait()
        for at in range(0, D, LANES):
            residual_ref[rows, at : at + LANES] = tokens_ref[rows, at : at + LANES].astype(
                jnp.float32
            ) + jnp.dot(
                attended_ref[rows, :], late[:, at : at + LANES], preferred_element_type=jnp.float32
            )
        residual = residual_ref[rows, :]
        inverse = lax.rsqrt(jnp.mean(residual * residual, -1, keepdims=True) + EPS)
        packed_ref[rows, :] = (
            residual * inverse * small_ref[experts + 1 : experts + 2, :]
        ).astype(jnp.bfloat16)
        store(packed_ref.at[rows], packed_out.at[rows])
        store(residual_ref.at[rows], residual_out.at[rows])
    for copy in leaving:
        copy.wait()


def attend_call(starts, tokens, table, routes, blocks, width_early, experts):
    rows_count = tokens.shape[0]
    width = (HEADS + 2 * KV_HEADS) * HEAD_DIM
    low = jnp.bfloat16
    copies = len(blocks) * blocks[0].shape[0]
    moved = [
        ((rows_count, D), low),
        ((rows_count, width), low),
        ((rows_count, HEADS * HEAD_DIM), low),
        ((rows_count, D), jnp.float32),
        ((rows_count + 16, D), low),
    ]
    kept = [
        ((rows_count, 128), jnp.float32),
        ((16, D), jnp.float32),
        ((experts, rows_count), jnp.float32),
    ]
    return pl.pallas_call(
        functools.partial(attend_kernel, len(blocks)),
        out_shape=[jax.ShapeDtypeStruct(*shape) for shape in moved + kept],
        in_specs=[scalars(), whole(), anywhere(), whole()] + [anywhere()] * len(blocks),
        out_specs=[anywhere()] * len(moved) + [whole()] * len(kept),
        scratch_shapes=[
            pltpu.VMEM((D, width_early), low),
            pltpu.VMEM((D, D), low),
            pltpu.VMEM((rows_count, rows_count), jnp.float32),
            pltpu.VMEM(table.shape, jnp.float32),
            *[pltpu.VMEM(*shape) for shape in moved],
            pltpu.SemaphoreType.DMA((copies,)),
            pltpu.SemaphoreType.DMA((copies,)),
            pltpu.SemaphoreType.DMA((10,)),
        ],
        compiler_params=pltpu.CompilerParams(vmem_limit_bytes=62 << 20),
        cost_estimate=small_cost(),
        name="attend",
    )(starts, tokens, table, routes, *blocks)


def middle_back_kernel(planes, column, start_ref, *refs):
    terms, tails, refs = refs[:4], refs[4:8], refs[8:]
    residual_ref, small_ref, cot_ref, tokens_ref, gates_ref, refs = *refs[:5], refs[5:]
    blocks, refs = refs[:planes], refs[planes:]
    mid_ref, low_ref, attended_grad_ref, logits_grad_ref, small_grad_ref, weight, sems = refs
    step = pl.program_id(0)
    experts = gates_ref.shape[0]
    rows_count = gates_ref.shape[1]

    @pl.when(step == 0)
    def _():
        copies = load_rows(blocks, start_ref, weight, sems, column)
        del copies
        gates = gates_ref[...]
        parts = sum([tail[:experts, :].astype(jnp.float32) for tail in tails])
        grad = (
            parts[:, :rows_count]
            + parts[:, rows_count : 2 * rows_count]
            + parts[:, 2 * rows_count :]
        )
        grad = gates * (grad - jnp.sum(gates * grad, 0, keepdims=True))
        logits_grad_ref[...] = jnp.concatenate(
            [grad, jnp.zeros((16 - experts, rows_count), jnp.float32)], 0
        ).astype(jnp.bfloat16)
        small_grad_ref[...] = jnp.zeros_like(small_grad_ref)

    grad = sum([term[...].astype(jnp.float32) for term in terms])
    residual = residual_ref[...]
    inverse = lax.rsqrt(jnp.mean(residual * residual, -1, keepdims=True) + EPS)
    normed = residual * inverse
    product = grad * normed
    small_grad_ref[experts : experts + 1, :] += jnp.sum(product, 0, keepdims=True)
    tile = tokens_ref.shape[0]
    lanes = pl.ds(pl.multiple_of(step * tile, tile), tile)
    small_grad_ref[:experts, :] += jnp.dot(
        logits_grad_ref[:, lanes], tokens_ref[...], preferred_element_type=jnp.float32
    )[:experts, :]
    gain = small_ref[experts + 1 : experts + 2, :]
    mean = jnp.mean(product * gain, -1, keepdims=True)
    mid = cot_ref[...].astype(jnp.float32) + inverse * (grad * gain - normed * mean)
    mid_ref[...] = mid
    low_ref[...] = mid.astype(jnp.bfloat16)

    @pl.when(step == 0)
    def _():
        for copy in load_rows(blocks, start_ref, weight, sems, column, False):
            copy.wait()

    for at in range(0, D, LANES):
        attended_grad_ref[:, at : at + LANES] = wide_dot(
            low_ref[...], weight[at : at + LANES, :]
        ).astype(jnp.bfloat16)


def middle_back_call(
    starts, terms, residual, small, cotangent, tokens, gates, blocks, column
):
    rows_count = residual.shape[0]
    tile = rows_count // 2
    low = jnp.bfloat16
    tiled = pl.BlockSpec((tile, D), lambda i: (i, 0))
    fixed = lambda rows, columns: pl.BlockSpec((rows, columns), lambda i: (0, 0))
    tail = pl.BlockSpec((16, D), lambda i: (rows_count // 16, 0))
    return pl.pallas_call(
        functools.partial(middle_back_kernel, len(blocks), column),
        grid=(2,),
        out_shape=[
            jax.ShapeDtypeStruct((rows_count, D), jnp.float32),
            jax.ShapeDtypeStruct((rows_count, D), low),
            jax.ShapeDtypeStruct((rows_count, D), low),
            jax.ShapeDtypeStruct((16, rows_count), low),
            jax.ShapeDtypeStruct((16, D), jnp.float32),
        ],
        in_specs=[scalars()]
        + [tiled] * 4
        + [tail] * 4
        + [tiled, fixed(16, D), tiled, tiled, fixed(*gates.shape)]
        + [anywhere()] * len(blocks),
        out_specs=[tiled, tiled, tiled, fixed(16, rows_count), fixed(16, D)],
        scratch_shapes=[
            pltpu.VMEM((D, D), low),
            pltpu.SemaphoreType.DMA((len(blocks) * blocks[0].shape[0],)),
        ],
        compiler_params=pltpu.CompilerParams(vmem_limit_bytes=62 << 20),
        cost_estimate=small_cost(),
        name="middle_back",
    )(starts, *terms, *terms, residual, small, cotangent, tokens, gates, *blocks)


def attend_back_kernel(heads_ref, grad_ref, log_ref, table_ref, raw_ref, bias):
    rows_count = heads_ref.shape[0]
    width_q, width_kv = HEADS * HEAD_DIM, KV_HEADS * HEAD_DIM
    half = rows_count // 2
    scale = HEAD_DIM ** (-0.5)
    fill_bias(bias, table_ref[:, 2 * HEAD_DIM : 2 * HEAD_DIM + 1])
    cosine, sine = table_ref[:, :HEAD_DIM], -table_ref[:, HEAD_DIM : 2 * HEAD_DIM]
    for key_head in range(KV_HEADS):
        key_at = width_q + key_head * HEAD_DIM
        value_at = key_at + width_kv
        key_grads, value_grads = [], []
        for block in range(2):
            rows, reach = slice(block * half, (block + 1) * half), (block + 1) * half
            keys = heads_ref[:reach, key_at : key_at + HEAD_DIM]
            values = heads_ref[:reach, value_at : value_at + HEAD_DIM]
            key_grad = jnp.zeros((reach, HEAD_DIM), jnp.float32)
            value_grad = jnp.zeros((reach, HEAD_DIM), jnp.float32)
            for head in range(key_head * HEADS // KV_HEADS, (key_head + 1) * HEADS // KV_HEADS):
                columns = slice(head * HEAD_DIM, (head + 1) * HEAD_DIM)
                queries, grads = heads_ref[rows, columns], grad_ref[rows, columns]
                scores = wide_dot(queries, keys) * scale + bias[rows, :reach]
                chances = jnp.exp(scores - log_ref[rows, head : head + 1])
                pulled = wide_dot(grads, values)
                shift = jnp.sum(chances * pulled, -1, keepdims=True)
                score_grad = (chances * (pulled - shift)).astype(jnp.bfloat16)
                value_grad = value_grad + tall_dot(chances.astype(jnp.bfloat16), grads)
                key_grad = key_grad + tall_dot(score_grad, queries)
                query_grad = (
                    jnp.dot(score_grad, keys, preferred_element_type=jnp.float32) * scale
                )
                raw_ref[rows, columns] = turned(
                    query_grad, cosine[rows, :], sine[rows, :]
                ).astype(jnp.bfloat16)
            key_grads.append(key_grad)
            value_grads.append(value_grad)
        key_grad = jnp.concatenate([key_grads[0] + key_grads[1][:half], key_grads[1][half:]], 0)
        value_grad = jnp.concatenate(
            [value_grads[0] + value_grads[1][:half], value_grads[1][half:]], 0
        )
        raw_ref[:, key_at : key_at + HEAD_DIM] = turned(key_grad * scale, cosine, sine).astype(
            jnp.bfloat16
        )
        raw_ref[:, value_at : value_at + HEAD_DIM] = value_grad.astype(jnp.bfloat16)


def attend_back_call(heads, grads, logs, table):
    rows_count = heads.shape[0]
    return pl.pallas_call(
        attend_back_kernel,
        out_shape=jax.ShapeDtypeStruct(heads.shape, jnp.bfloat16),
        in_specs=[whole()] * 4,
        out_specs=whole(),
        scratch_shapes=[pltpu.VMEM((rows_count, rows_count), jnp.float32)],
        compiler_params=pltpu.CompilerParams(vmem_limit_bytes=62 << 20),
        cost_estimate=small_cost(),
        name="attend_back",
    )(heads, grads, logs, table)


def shard_grad_kernel(extra, start_ref, left_ref, right_ref, *refs):
    parts, grad, sems = refs[extra:-2], refs[-2], refs[-1]
    width = right_ref.shape[1]
    pairs, pieces, rows = parts[0].shape[:3]
    owners = 2 * pairs
    tall = owners * rows
    copies = []
    if extra:
        small = refs[0][...]
        small = jnp.concatenate([small, jnp.zeros((128 - small.shape[0], D), jnp.float32)], 0)
        grad[:, width:] = jnp.transpose(small).astype(jnp.bfloat16)
    for p in range(pieces):
        for at in range(0, width, WIDE):
            grad[p * tall : (p + 1) * tall, at : at + WIDE] = tall_dot(
                left_ref[:, p * tall : (p + 1) * tall], right_ref[:, at : at + WIDE]
            ).astype(jnp.bfloat16)
        to = lax.rem(start_ref[0] + pieces - p, pieces)
        for i in range(owners):
            at = pl.multiple_of(p * tall + start_ref[1 + i] * rows, 16)
            copy = pltpu.make_async_copy(
                grad.at[pl.ds(at, rows)], parts[i % 2].at[i // 2, to], sems.at[p * owners + i]
            )
            copy.start()
            copies.append(copy)
    for copy in copies:
        copy.wait()


def shard_grad_call(spots, left, right, pieces, owners, small=None):
    extra = [] if small is None else [small]
    width, height = right.shape[1] + 128 * len(extra), left.shape[1]
    rows = height // (pieces * owners)
    return pl.pallas_call(
        functools.partial(shard_grad_kernel, len(extra)),
        out_shape=[jax.ShapeDtypeStruct((owners // 2, pieces, rows, width), jnp.bfloat16)] * 2,
        in_specs=[scalars()] + [whole()] * (2 + len(extra)),
        out_specs=[anywhere()] * 2,
        scratch_shapes=[
            pltpu.VMEM((height, width), jnp.bfloat16),
            pltpu.SemaphoreType.DMA((pieces * owners,)),
        ],
        compiler_params=pltpu.CompilerParams(vmem_limit_bytes=62 << 20),
        cost_estimate=small_cost(),
        name="shard_grad",
    )(spots, left, right, *extra)


def entry_back_kernel(planes, start_ref, *refs):
    raw_ref, tokens_ref, mid_ref, small_ref, logits_grad_ref, refs = *refs[:5], refs[5:]
    blocks, refs = refs[:planes], refs[planes:]
    grad_ref, weight, sems = refs
    step = pl.program_id(0)
    width = raw_ref.shape[1]
    experts = small_ref.shape[0] - 8
    tile = tokens_ref.shape[0]

    @pl.when(step == 0)
    def _():
        for copy in load_rows(blocks, start_ref, weight, sems):
            copy.wait()

    for at in range(0, D, LANES):
        grad_ref[:, at : at + LANES] = wide_dot(raw_ref[...], weight[at : at + LANES, :width])
    inputs = tokens_ref[...].astype(jnp.float32)
    inverse = lax.rsqrt(jnp.mean(inputs * inputs, -1, keepdims=True) + EPS)
    normed = inputs * inverse
    grad = grad_ref[...]
    gain = small_ref[experts : experts + 1, :]
    mean = jnp.mean(grad * normed * gain, -1, keepdims=True)
    row = lax.broadcasted_iota(jnp.int32, (16, 1), 0)
    router = jnp.where(row < experts, small_ref[...], 0.0).astype(jnp.bfloat16)
    grad_ref[...] = (
        mid_ref[...]
        + inverse * (grad * gain - normed * mean)
        + tall_dot(logits_grad_ref[...], router)
    )


def entry_back_call(
    starts, raw_grad, tokens, mid_grad, small, logits_grad, blocks, width_early
):
    rows_count = tokens.shape[0]
    tile = rows_count // 2
    tiled = lambda columns: pl.BlockSpec((tile, columns), lambda i: (i, 0))
    fixed = lambda rows, columns: pl.BlockSpec((rows, columns), lambda i: (0, 0))
    return pl.pallas_call(
        functools.partial(entry_back_kernel, len(blocks)),
        grid=(2,),
        out_shape=jax.ShapeDtypeStruct((rows_count, D), jnp.float32),
        in_specs=[
            scalars(),
            tiled(raw_grad.shape[1]),
            tiled(D),
            tiled(D),
            fixed(16, D),
            pl.BlockSpec((16, tile), lambda i: (0, i)),
        ]
        + [anywhere()] * len(blocks),
        out_specs=tiled(D),
        scratch_shapes=[
            pltpu.VMEM((D, width_early), jnp.bfloat16),
            pltpu.SemaphoreType.DMA((len(blocks) * blocks[0].shape[0],)),
        ],
        compiler_params=pltpu.CompilerParams(vmem_limit_bytes=62 << 20),
        cost_estimate=small_cost(),
        name="entry_back",
    )(starts, raw_grad, tokens, mid_grad, small, logits_grad, *blocks)


def pipeline(loads, stores, body, count, later=()):
    coming = {}

    def fetch(i):
        coming[i] = loads(i, i % 2)
        for copy in coming[i]:
            copy.start()

    leaving = {}
    fetch(0)
    for copy in later:
        copy.start()
    for i in range(count):
        if i + 1 < count:
            fetch(i + 1)
        for copy in coming.pop(i):
            copy.wait()
        for copy in leaving.pop(i - 2, []):
            copy.wait()
        body(i, i % 2)
        leaving[i] = stores(i, i % 2)
        for copy in leaving[i]:
            copy.start()
    for i in sorted(leaving):
        for copy in leaving[i]:
            copy.wait()


def copies_of(pairs, sems):
    return [
        pltpu.make_async_copy(source, target, sems.at[j])
        for j, (source, target) in enumerate(pairs)
    ]


def hidden_kernel(count, pieces, tokens_count, place_ref, *refs):
    rows_in, chunks, refs = refs[:count], refs[count : count + pieces], refs[count + pieces :]
    outs, refs = refs[: 3 * count], refs[3 * count :]
    weight, rows, slope, product, gated, sems, in_sems, out_sems = refs
    weight_copies = load_weight(chunks, place_ref, weight, sems)

    def loads(i, slot):
        return copies_of([(rows_in[i], rows.at[slot])], in_sems.at[slot])

    def stores(i, slot):
        buffers = (slope, product, gated)
        return copies_of(
            [(buffer.at[slot], outs[j * count + i]) for j, buffer in enumerate(buffers)],
            out_sems.at[slot],
        )

    def body(i, slot):
        if i == 0:
            for copy in weight_copies:
                copy.wait()
        weights = spread(expert_row(rows[slot, tokens_count:, :], place_ref[4]), tokens_count)
        weights = jnp.concatenate([weights] * (LANES // 128), 1)
        for at in range(0, FF, LANES):
            gate = jnp.dot(
                rows[slot, :tokens_count, :],
                weight[:, at : at + LANES],
                preferred_element_type=jnp.float32,
            )
            up = jnp.dot(
                rows[slot, :tokens_count, :],
                weight[:, FF + at : FF + at + LANES],
                preferred_element_type=jnp.float32,
            )
            square = gate * gate
            bend = jnp.tanh(0.7978845608028654 * gate * (1.0 + 0.044715 * square))
            half = 0.5 + 0.5 * bend
            steep = half + 0.5 * gate * (1.0 - bend * bend) * (
                0.7978845608028654 + 0.10703222440890037 * square
            )
            active = gate * half
            both = (active * up).astype(jnp.bfloat16)
            slope[slot, :, at : at + LANES] = (up * steep).astype(jnp.bfloat16)
            slope[slot, :, FF + at : FF + at + LANES] = active.astype(jnp.bfloat16)
            product[slot, :, at : at + LANES] = both
            gated[slot, :, at : at + LANES] = (both.astype(jnp.float32) * weights).astype(
                jnp.bfloat16
            )

    pipeline(loads, stores, body, count)


def hidden_call(rows_in, chunks, places, tokens_count):
    count = len(rows_in)
    low = jnp.bfloat16
    widths = [2 * FF, FF, FF]
    outs = pl.pallas_call(
        functools.partial(hidden_kernel, count, len(chunks), tokens_count),
        out_shape=[
            jax.ShapeDtypeStruct((tokens_count, width), low)
            for width in widths
            for _ in range(count)
        ],
        in_specs=[scalars()] + [anywhere()] * (count + len(chunks)),
        out_specs=[anywhere()] * (3 * count),
        scratch_shapes=[
            pltpu.VMEM((D, 2 * FF), low),
            pltpu.VMEM((2, *rows_in[0].shape), low),
            *[pltpu.VMEM((2, tokens_count, width), low) for width in widths],
            pltpu.SemaphoreType.DMA((len(chunks),)),
            pltpu.SemaphoreType.DMA((2, 1)),
            pltpu.SemaphoreType.DMA((2, 3)),
        ],
        compiler_params=pltpu.CompilerParams(vmem_limit_bytes=62 << 20),
        cost_estimate=small_cost(),
        name="expert_hidden",
    )(places, *rows_in, *chunks)
    return outs[:count], outs[count : 2 * count], outs[2 * count :]


def spread(row, tokens_count):
    return jnp.transpose(jnp.broadcast_to(row, (128, tokens_count)))


def expert_row(block, expert):
    third = block.shape[1] // 3
    index = lax.broadcasted_iota(jnp.int32, block.shape, 0)
    row = jnp.sum(jnp.where(index == expert, block.astype(jnp.float32), 0.0), 0, keepdims=True)
    return row[:, :third] + row[:, third : 2 * third] + row[:, 2 * third :]


def split_row(row):
    high = row.astype(jnp.bfloat16)
    rest = row - high.astype(jnp.float32)
    middle = rest.astype(jnp.bfloat16)
    low = (rest - middle.astype(jnp.float32)).astype(jnp.bfloat16)
    return jnp.concatenate(
        [high.astype(jnp.float32), middle.astype(jnp.float32), low.astype(jnp.float32)], 1
    )


def pull_kernel(count, pieces, tokens_count, place_ref, *refs):
    packed, cots, slopes, products = (refs[i * count : (i + 1) * count] for i in range(4))
    refs = refs[4 * count :]
    in_chunks, out_chunks, refs = refs[: pieces[0]], refs[pieces[0] : sum(pieces)], refs[sum(pieces) :]
    row_grads, hidden_grads, refs = refs[:count], refs[count : 2 * count], refs[2 * count :]
    in_weight, out_weight, tail, cot, slope, product, grad, hidden, *sems = refs
    expert = place_ref[4]
    in_copies, out_copies = [], []

    def loads(i, slot):
        copies = copies_of(
            [
                (packed[i].at[pl.ds(tokens_count, 16)], tail.at[slot]),
                (cots[i], cot.at[slot]),
                (slopes[i], slope.at[slot]),
                (products[i], product.at[slot]),
            ],
            sems[2].at[slot],
        )
        return copies

    def stores(i, slot):
        return copies_of([(grad.at[slot], row_grads[i])], sems[3].at[slot])

    leaving = {}

    def body(i, slot):
        if i == 0:
            for copy in out_copies:
                copy.wait()
        if i >= 2:
            leaving.pop(i - 2).wait()
        weights = spread(expert_row(tail[slot], expert), tokens_count)
        weights = jnp.concatenate([weights] * (LANES // 128), 1)
        gate_grad = jnp.zeros((tokens_count, 1), jnp.float32)
        for at in range(0, FF, LANES):
            pulled = wide_dot(cot[slot], out_weight[at : at + LANES, :])
            both = product[slot, :, at : at + LANES].astype(jnp.float32)
            gate_grad = gate_grad + jnp.sum(pulled * both, 1, keepdims=True)
            pulled = pulled * weights
            for base in (at, FF + at):
                hidden[slot, :, base : base + LANES] = (
                    pulled * slope[slot, :, base : base + LANES].astype(jnp.float32)
                ).astype(jnp.bfloat16)
        row = jnp.transpose(jnp.broadcast_to(gate_grad, (tokens_count, 128)))[:1, :]
        parts = jnp.broadcast_to(split_row(row), (16, 3 * tokens_count))
        index = lax.broadcasted_iota(jnp.int32, parts.shape, 0)
        grad[slot, tokens_count:, :] = jnp.where(index == expert, parts, 0.0).astype(jnp.bfloat16)
        leaving[i] = pltpu.make_async_copy(hidden.at[slot], hidden_grads[i], sems[4].at[slot])
        leaving[i].start()
        if i == 0:
            for copy in in_copies:
                copy.wait()
        for at in range(0, D, LANES):
            grad[slot, :tokens_count, at : at + LANES] = wide_dot(
                hidden[slot], in_weight[at : at + LANES, :]
            ).astype(jnp.bfloat16)

    out_copies += load_weight(out_chunks, place_ref, out_weight, sems[1])
    in_copies += load_weight(in_chunks, place_ref, in_weight, sems[0], False)
    pipeline(loads, stores, body, count, in_copies)
    for i in sorted(leaving):
        leaving[i].wait()


def pull_call(packed, cots, slopes, products, in_chunks, out_chunks, places, tokens_count):
    count = len(packed)
    low = jnp.bfloat16
    out_shapes = [(tokens_count + 16, D), (tokens_count, 2 * FF)]
    outs = pl.pallas_call(
        functools.partial(
            pull_kernel, count, (len(in_chunks), len(out_chunks)), tokens_count
        ),
        out_shape=[jax.ShapeDtypeStruct(shape, low) for shape in out_shapes for _ in range(count)],
        in_specs=[scalars()] + [anywhere()] * (4 * count + len(in_chunks) + len(out_chunks)),
        out_specs=[anywhere()] * (2 * count),
        scratch_shapes=[
            pltpu.VMEM((D, 2 * FF), low),
            pltpu.VMEM((FF, D), low),
            pltpu.VMEM((2, 16, D), low),
            pltpu.VMEM((2, tokens_count, D), low),
            pltpu.VMEM((2, tokens_count, 2 * FF), low),
            pltpu.VMEM((2, tokens_count, FF), low),
            pltpu.VMEM((2, tokens_count + 16, D), low),
            pltpu.VMEM((2, tokens_count, 2 * FF), low),
            pltpu.SemaphoreType.DMA((len(in_chunks),)),
            pltpu.SemaphoreType.DMA((len(out_chunks),)),
            pltpu.SemaphoreType.DMA((2, 4)),
            pltpu.SemaphoreType.DMA((2, 1)),
            pltpu.SemaphoreType.DMA((2,)),
        ],
        compiler_params=pltpu.CompilerParams(vmem_limit_bytes=62 << 20),
        cost_estimate=small_cost(),
        name="expert_pull",
    )(places, *packed, *cots, *slopes, *products, *in_chunks, *out_chunks)
    return outs[:count], outs[count:]


def product_kernel(count, place_ref, *refs):
    gated, chunks, refs = refs[:count], refs[count : count + 4], refs[count + 4 :]
    rows_out, (weight, left, total, *sems) = refs[:count], refs[count:]
    weight_copies = load_weight(chunks, place_ref, weight, sems[0])

    def loads(i, slot):
        return copies_of([(gated[i], left.at[slot])], sems[1].at[slot])

    def stores(i, slot):
        return copies_of([(total.at[slot], rows_out[i])], sems[2].at[slot])

    def body(i, slot):
        if i == 0:
            for copy in weight_copies:
                copy.wait()
        for at in range(0, D, LANES):
            total[slot, :, at : at + LANES] = jnp.dot(
                left[slot], weight[:, at : at + LANES], preferred_element_type=jnp.float32
            ).astype(jnp.bfloat16)

    pipeline(loads, stores, body, count)


def product_call(gated, chunks, places):
    count, rows = len(gated), gated[0].shape[0]
    return pl.pallas_call(
        functools.partial(product_kernel, count),
        out_shape=[jax.ShapeDtypeStruct((rows, D), jnp.bfloat16)] * count,
        in_specs=[scalars()] + [anywhere()] * (count + 4),
        out_specs=[anywhere()] * count,
        scratch_shapes=[
            pltpu.VMEM((FF, D), jnp.bfloat16),
            pltpu.VMEM((2, rows, FF), jnp.bfloat16),
            pltpu.VMEM((2, rows, D), jnp.bfloat16),
            pltpu.SemaphoreType.DMA((4,)),
            pltpu.SemaphoreType.DMA((2, 1)),
            pltpu.SemaphoreType.DMA((2, 1)),
        ],
        compiler_params=pltpu.CompilerParams(vmem_limit_bytes=62 << 20),
        cost_estimate=small_cost(),
        name="expert_rows",
    )(places, *gated, *chunks)


def weight_grad_kernel(count, rows, *refs):
    left, right, grad = refs[:count], refs[count : 2 * count], refs[2 * count]
    total = tall_dot(left[0][:rows, :], right[0][:rows, :])
    for i in range(1, count):
        total = total + tall_dot(left[i][:rows, :], right[i][:rows, :])
    grad[...] = total.astype(grad.dtype)


def weight_grad_call(left, right, rows, tall, name):
    count = len(left)
    height, width = left[0].shape[1], right[0].shape[1]
    return pl.pallas_call(
        functools.partial(weight_grad_kernel, count, rows),
        grid=(height // tall, width // WIDE),
        out_shape=jax.ShapeDtypeStruct((height, width), jnp.bfloat16),
        in_specs=[pl.BlockSpec((rows, tall), lambda i, j: (0, i))] * count
        + [pl.BlockSpec((rows, WIDE), lambda i, j: (0, j))] * count,
        out_specs=pl.BlockSpec((tall, WIDE), lambda i, j: (i, j)),
        compiler_params=pltpu.CompilerParams(vmem_limit_bytes=62 << 20),
        cost_estimate=small_cost(),
        name=name,
    )(*left, *right)


def plane_shards(
    tokens,
    cotangent,
    routes,
    doc_lengths,
    query_weight,
    query_first,
    query_second,
    keyvalue_weight,
    keyvalue_first,
    keyvalue_second,
    output_weight,
    output_first,
    output_second,
    router_weight,
    router_first,
    router_second,
    norm_gains,
    gains_first,
    gains_second,
    expert_in,
    expert_in_first,
    expert_in_second,
    expert_out,
    expert_out_first,
    expert_out_second,
):
    rows_count = tokens.shape[0]
    experts = router_weight.shape[1]
    columns_dp, owners = lax.axis_size("dp"), lax.axis_size("expert")
    dp_index, expert_index = lax.axis_index("dp"), lax.axis_index("expert")
    core = expert_index & 1
    ring = [(i, (i + 1) % columns_dp) for i in range(columns_dp)]
    shard = query_weight.shape[0]
    width_q = HEADS * HEAD_DIM
    width_qkv = (HEADS + 2 * KV_HEADS) * HEAD_DIM
    low = jnp.bfloat16
    places = (dp_index - jnp.arange(columns_dp, dtype=jnp.int32)) % columns_dp
    starts = (
        (expert_index ^ jnp.arange(owners, dtype=jnp.int32))[:, None] + places[None, :] * owners
    ).reshape(-1) * shard
    places = jnp.concatenate([places, expert_index[None]]).astype(jnp.int32)
    spots = jnp.concatenate([dp_index[None], expert_index ^ jnp.arange(owners)]).astype(jnp.int32)

    position = jnp.arange(rows_count, dtype=jnp.int32)
    ends = jnp.cumsum(doc_lengths[0])
    first = jnp.max(jnp.where(position[:, None] >= ends[None, :], ends[None, :], 0), 1)
    offset = (position - first).astype(jnp.float32)
    frequency = ROPE_BASE ** (-2.0 * jnp.arange(HEAD_DIM // 2, dtype=jnp.float32) / HEAD_DIM)
    angles = offset[:, None] * frequency[None, :]
    cosine, sine = jnp.cos(angles), jnp.sin(angles)
    first = jnp.broadcast_to(first.astype(jnp.float32)[:, None], (rows_count, HEAD_DIM))
    table = jnp.concatenate([cosine, cosine, -sine, sine, first], 1)

    width_early = width_qkv + 128

    def cross(block):
        return to_x(block), to_y(block)

    def onward(from_x, from_y):
        return jnp.where(core == 0, from_y, from_x)

    sent = jnp.concatenate(
        [
            query_weight.astype(low),
            keyvalue_weight.astype(low),
            router_weight.astype(low),
            norm_gains.T.astype(low),
            jnp.zeros((shard, 128 - experts - 2), low),
            output_weight.astype(low),
        ],
        1,
    )

    def around(value):
        return lax.ppermute(value, "dp", ring)

    cot_x, cot_y = cross(cotangent)
    in_low, out_low = expert_in[0].astype(low), expert_out[0].astype(low)
    column = [sent, around(sent)]
    column.append(around(column[1]))
    column[2], in_low, out_low, table, routes_t = hold(
        column[2], in_low, out_low, table, routes.T
    )
    column.append(around(column[2]))
    joint = jnp.stack(column)
    cut = in_low.shape[0] * 3 // 4
    cot_x, cot_y, joint, in_low, out_low = hold(cot_x, cot_y, joint, in_low, out_low)
    in_near, in_rest, out_chunks = [in_low[:cut]], [in_low[cut:]], [out_low]

    joint_x, joint_y = cross(joint)
    joint_core = to_core(joint)
    in_near.append(around(in_near[0]))
    in_rest.append(around(in_rest[0]))
    joint_x, joint_y, joint_core, in_near, in_rest, cot_x, cot_y = hold(
        joint_x, joint_y, joint_core, in_near, in_rest, cot_x, cot_y
    )
    joint_far = forward(onward(joint_x, joint_y))
    joint_x2, joint_y2 = to_core(joint_x), to_core(joint_y)
    cot_x2 = to_core(cot_x)
    in_near.append(around(in_near[1]))
    outward = onward(cot_x, cot_y)
    joint_far, joint_x2, joint_y2, in_near, in_rest, cot_x2, cot_y, outward = hold(
        joint_far, joint_x2, joint_y2, in_near, in_rest, cot_x2, cot_y, outward
    )
    joint_far2 = to_core(joint_far)
    joint_far2, outward, cot_y, in_near, in_rest = hold(
        joint_far2, outward, cot_y, in_near, in_rest
    )
    plane = [joint, joint_core, joint_x, joint_x2, joint_y, joint_y2, joint_far, joint_far2]

    cot_far = forward(outward)
    cot_core, cot_y2 = to_core(cotangent), to_core(cot_y)
    in_near.append(around(in_near[2]))
    attn_in, heads, attended, residual_mid, packed, logs, small, gates = attend_call(
        starts, tokens, table, routes_t, plane, width_early, experts
    )
    packed, cot_far, cot_core, cot_y2, in_near, in_rest, out_chunks = hold(
        packed, cot_far, cot_core, cot_y2, in_near, in_rest, out_chunks
    )

    packed_x, packed_y = cross(packed)
    packed_core = to_core(packed)
    in_rest.append(around(in_rest[1]))
    in_rest.append(around(in_rest[2]))
    in_chunks = in_near + in_rest
    out_chunks.append(around(after(out_chunks[0], in_rest[3])))
    slopes, products, gated = [None] * 8, [None] * 8, [None] * 8
    packed_blocks = [packed, packed_core] + [None] * 6

    def hidden(order, *earlier):
        blocks = [packed_blocks[k] for k in order]
        blocks[0] = after(blocks[0], *earlier)
        for k, *outs in zip(order, *hidden_call(blocks, in_chunks, places, rows_count)):
            slopes[k], products[k], gated[k] = outs

    hidden((0, 1))
    packed_x, packed_y, gated[0], out_chunks, cot_far = hold(
        packed_x, packed_y, gated[0], out_chunks, cot_far
    )
    packed_x2, packed_y2 = to_core(packed_x), to_core(packed_y)
    packed_far = forward(onward(packed_x, packed_y))
    cot_far2 = to_core(cot_far)
    out_chunks.append(around(out_chunks[1]))
    cot_blocks = [cotangent, cot_core, cot_x, cot_x2, cot_y, cot_y2, cot_far, cot_far2]
    packed_blocks[2:6] = [packed_x, packed_x2, packed_y, packed_y2]
    hidden((2, 4, 3, 5))
    packed_far, out_chunks, gated[3] = hold(packed_far, out_chunks, gated[3])
    packed_far2 = to_core(packed_far)
    packed_blocks[6:] = hold(packed_far, packed_far2)
    out_chunks.append(around(after(out_chunks[2], packed_far2)))
    hidden((6, 7))
    out_grad = weight_grad_call(gated, cot_blocks, rows_count, FF, "expert_out_grad")
    out_grad, out_chunks = hold(out_grad, out_chunks)

    def column_piece(value, back):
        rows = value.shape[0] // columns_dp
        return lax.dynamic_slice_in_dim(value, places[back] * rows, rows, 0)

    moving = column_piece(out_grad, 1)
    row_grads, hidden_grads, rows_out = [None] * 8, [None] * 8, [None] * 8

    def pick(values, order):
        return [values[k] for k in order]

    def pull(order, *earlier):
        first_cot = after(cot_blocks[order[0]], *earlier)
        outs = pull_call(
            pick(packed_blocks, order),
            [first_cot] + pick(cot_blocks, order[1:]),
            pick(slopes, order),
            pick(products, order),
            in_chunks,
            out_chunks,
            places,
            rows_count,
        )
        for k, row_grad, hidden_grad in zip(order, *outs):
            row_grads[k], hidden_grads[k] = row_grad, hidden_grad

    def rows_of(order, *earlier):
        first_gated = after(gated[order[0]], *earlier)
        outs = product_call([first_gated] + pick(gated, order[1:]), out_chunks, places)
        for k, rows in zip(order, outs):
            rows_out[k] = rows

    zero = jnp.zeros((), low)

    def by_core(value, wanted):
        return jnp.where(core == wanted, value, zero)

    rows_of((7, 6), moving)
    rows_out[6], rows_out[7], moving = hold(rows_out[6], rows_out[7], moving)
    moved = around(moving)
    rows_back = to_core(rows_out[7])
    pull((7, 6), rows_out[6])
    moved, rows_back, row_grads[6], row_grads[7] = hold(
        moved, rows_back, row_grads[6], row_grads[7]
    )
    far_back = to_core(row_grads[7])
    rows_far = add_low(rows_out[6], rows_back)
    moving = add_low(moved, column_piece(out_grad, 2))
    far_back, rows_far, moving = hold(far_back, rows_far, moving)
    far = add_low(row_grads[6], far_back)
    far, rows_far, moving = hold(far, rows_far, moving)
    relayed, rows_relayed = forward(far), forward(rows_far)
    moved = around(moving)
    pull((0, 1, 3, 2, 5, 4), far, rows_far, moving)
    relayed, moved, row_grads[:6] = hold(relayed, moved, row_grads[:6])
    back_x, back_y = to_core(row_grads[3]), to_core(row_grads[5])
    back_own = to_core(row_grads[1])
    rows_of((5, 4, 3, 2, 1, 0), row_grads[0])
    moving = add_low(moved, column_piece(out_grad, 3))
    back_x, back_y, back_own, rows_out[:6], moving = hold(
        back_x, back_y, back_own, rows_out[:6], moving
    )
    by_x = add_low(row_grads[2], back_x, by_core(relayed, 1))
    by_y = add_low(row_grads[4], back_y, by_core(relayed, 0))
    by_x, by_y, moving, hidden_grads[0], rows_out[:6], rows_relayed = hold(
        by_x, by_y, moving, hidden_grads[0], rows_out[:6], rows_relayed
    )

    from_x, from_y = to_x(by_x), to_y(by_y)
    moved = around(moving)
    rows_backs = [to_core(rows_out[k]) for k in (3, 5)]
    in_grad = weight_grad_call(packed_blocks, hidden_grads, rows_count, FF, "expert_in_grad")
    rows_x = add_low(rows_out[2], rows_backs[0], by_core(rows_relayed, 1))
    rows_y = add_low(rows_out[4], rows_backs[1], by_core(rows_relayed, 0))
    cut = in_low.shape[0] * 5 // 8

    def in_pieces(back):
        piece = column_piece(in_grad, back)
        return piece[:cut], piece[cut:]

    near, rest = in_pieces(1)
    from_x, from_y, moved, near, rest, rows_out[:2], rows_x, rows_y = hold(
        from_x, from_y, moved, near, rest, rows_out[:2], rows_x, rows_y
    )
    expert_out_sum = moved.astype(jnp.float32) + column_piece(out_grad, 0).astype(jnp.float32)

    rows_from_x, rows_from_y = to_x(rows_x), to_y(rows_y)
    rows_back = to_core(rows_out[1])
    near_moved, rest_moved = around(near), around(rest)
    mid_grad, mid_low, attended_grad, logits_grad, small_grad = middle_back_call(
        starts, [after(row_grads[0], rows_x), back_own, from_x, from_y], residual_mid,
        small, cotangent, tokens, gates, plane, width_early,
    )
    raw_grad = attend_back_call(heads, attended_grad, logs, table)
    early_even, early_odd = shard_grad_call(spots, attn_in, raw_grad, columns_dp, owners)
    early_even, early_odd, mid_low, rows_back, near_moved, rest_moved = hold(
        early_even, early_odd, mid_low, rows_back, near_moved, rest_moved
    )
    rest = add_low(rest_moved, in_pieces(2)[1])
    rest, early_odd, rows_from_x, rows_from_y = hold(rest, early_odd, rows_from_x, rows_from_y)
    early_back = to_core(early_odd)
    rest_moved = around(rest)
    near = add_low(near_moved, in_pieces(2)[0])
    output_even, output_odd = shard_grad_call(
        spots, attended, mid_low, columns_dp, owners, small_grad
    )
    early_back, output_even, output_odd, near, rest_moved = hold(
        early_back, output_even, output_odd, near, rest_moved
    )
    near_moved = around(near)
    early_far = add_low(early_even[3], early_back[3])
    early_far, output_odd, output_even = hold(early_far, output_odd, output_even)

    early_relayed = forward(early_far)
    output_back = to_core(output_odd)
    tokens_grad = entry_back_call(
        starts, after(raw_grad, early_far), tokens, mid_grad, small, logits_grad,
        plane, width_early,
    )
    early_pairs = add_low(early_even[:3], early_back[:3])
    rest = add_low(rest_moved, in_pieces(3)[1])
    early_relayed, output_back, tokens_grad, early_pairs, near_moved, rest = hold(
        early_relayed, output_back, tokens_grad, early_pairs, near_moved, rest
    )
    early_x = add_low(early_pairs[1], by_core(early_relayed, 1))
    early_y = add_low(early_pairs[2], by_core(early_relayed, 0))
    output_far = add_low(output_even[3], output_back[3])
    near = add_low(near_moved, in_pieces(3)[0])
    early_x, early_y, output_far, near, expert_out_sum, rows_back = hold(
        early_x, early_y, output_far, near, expert_out_sum, rows_back
    )
    early_x, early_y, output_relayed = to_x(early_x), to_y(early_y), forward(output_far)
    near_moved, rest_moved = around(near), around(rest)
    output_pairs = add_low(output_even[:3], output_back[:3])
    block_out = residual_mid + add_low_wide(rows_out[0], rows_back, rows_from_x, rows_from_y)
    mixed_out = block_out.astype(low)
    early_x, early_y, output_relayed, output_pairs, near_moved, rest_moved = hold(
        early_x, early_y, output_relayed, output_pairs, near_moved, rest_moved
    )
    early_total = add_low(early_pairs[0], early_x, early_y)
    output_x = add_low(output_pairs[1], by_core(output_relayed, 1))
    output_y = add_low(output_pairs[2], by_core(output_relayed, 0))
    early_total, output_x, output_y = hold(early_total, output_x, output_y)

    def spread_pieces(total):
        return [total[0]] + [
            lax.ppermute(total[p], "dp", [(i, (i - p) % columns_dp) for i in range(columns_dp)])
            for p in range(1, columns_dp)
        ]

    early_pieces = spread_pieces(early_total)
    output_x, output_y = to_x(output_x), to_y(output_y)
    expert_in_sum = jnp.concatenate([near_moved, rest_moved]).astype(
        jnp.float32
    ) + column_piece(in_grad, 0).astype(jnp.float32)
    early_pieces, output_x, output_y = hold(early_pieces, output_x, output_y)
    output_total = add_low(output_pairs[0], output_x, output_y)
    output_pieces = spread_pieces(output_total)
    output_sum = add_low_wide(*output_pieces)
    summed = add_low_wide(*early_pieces)
    used = sent[:, :width_qkv].astype(jnp.float32)
    gain_one = sent[:, width_qkv + experts].astype(jnp.float32)
    gain_one_sum = jnp.sum(used * summed, 1) / gain_one
    at = width_qkv
    sums = (
        summed[:, :width_q],
        summed[:, width_q:at],
        output_sum[:, :D],
        output_sum[:, D : D + experts],
        jnp.stack([gain_one_sum, output_sum[:, D + experts]]),
        expert_in_sum[None],
        expert_out_sum[None],
    )
    (
        (query_weight, query_first, query_second),
        (keyvalue_weight, keyvalue_first, keyvalue_second),
        (output_weight, output_first, output_second),
        (router_weight, router_first, router_second),
        (norm_gains, gains_first, gains_second),
        _,
    ) = hold(
        (query_weight, query_first, query_second),
        (keyvalue_weight, keyvalue_first, keyvalue_second),
        (output_weight, output_first, output_second),
        (router_weight, router_first, router_second),
        (norm_gains, gains_first, gains_second),
        early_total,
    )
    weights = (
        (query_weight, query_first, query_second),
        (keyvalue_weight, keyvalue_first, keyvalue_second),
        (output_weight, output_first, output_second),
        (router_weight, router_first, router_second),
        (norm_gains, gains_first, gains_second),
        (expert_in, expert_in_first, expert_in_second),
        (expert_out, expert_out_first, expert_out_second),
    )
    updates = []
    for state, grad, rate, decay in zip(
        weights, sums, learning_rates(), (DECAY, DECAY, DECAY, DECAY, 0.0, DECAY, DECAY)
    ):
        updates.extend(adam_update(*state, grad, rate, decay))
    return (mixed_out, tokens_grad, *updates)


def solution(mesh):
    in_specs = (
        P(("dp", "expert"), None),
        P(("dp", "expert"), None),
        P(("dp", "expert"), None),
        P(("dp", "expert"), None),
        P(("dp", "expert"), None),
        P(("dp", "expert"), None),
        P(("dp", "expert"), None),
        P(("dp", "expert"), None),
        P(("dp", "expert"), None),
        P(("dp", "expert"), None),
        P(("dp", "expert"), None),
        P(("dp", "expert"), None),
        P(("dp", "expert"), None),
        P(("dp", "expert"), None),
        P(("dp", "expert"), None),
        P(("dp", "expert"), None),
        P(None, ("dp", "expert")),
        P(None, ("dp", "expert")),
        P(None, ("dp", "expert")),
        P("expert", "dp", None),
        P("expert", "dp", None),
        P("expert", "dp", None),
        P("expert", "dp", None),
        P("expert", "dp", None),
        P("expert", "dp", None),
    )
    out_specs = (
        P(("dp", "expert"), None),
        P(("dp", "expert"), None),
        P(("dp", "expert"), None),
        P(("dp", "expert"), None),
        P(("dp", "expert"), None),
        P(("dp", "expert"), None),
        P(("dp", "expert"), None),
        P(("dp", "expert"), None),
        P(("dp", "expert"), None),
        P(("dp", "expert"), None),
        P(("dp", "expert"), None),
        P(("dp", "expert"), None),
        P(("dp", "expert"), None),
        P(("dp", "expert"), None),
        P(None, ("dp", "expert")),
        P(None, ("dp", "expert")),
        P(None, ("dp", "expert")),
        P("expert", "dp", None),
        P("expert", "dp", None),
        P("expert", "dp", None),
        P("expert", "dp", None),
        P("expert", "dp", None),
        P("expert", "dp", None),
    )
    def body(tokens, *rest):
        one_plane = mesh.shape["expert"] == 8 and rest[12].shape[1] == 8
        fits = one_plane and 3 * tokens.shape[0] == D
        return (plane_shards if fits else shards)(tokens, *rest)

    return jax.shard_map(body, mesh=mesh, in_specs=in_specs, out_specs=out_specs, check_vma=False)
```

```python
import functools

import jax
import jax.numpy as jnp
from jax import lax
from jax.experimental import pallas as pl
from jax.experimental.pallas import tpu as pltpu
from jax.sharding import PartitionSpec as P

D = 1536
FF = 768
HEADS = 12
KV_HEADS = 2
HEAD_DIM = 128
TOP = 4
STEP = 10


EPS = 1e-06
NEG = -1e30
BETA_ONE = 0.9
BETA_TWO = 0.999
ADAM_EPS = 1e-08
DECAY = 0.1
ROPE_BASE = 10000.0
RATE_SCALE = 2.5
GAIN_RATE = 0.6


def doc_tables(lengths, rows_count):
    position = jnp.arange(rows_count, dtype=jnp.int32)
    doc_ends = jnp.cumsum(lengths)
    doc_starts = doc_ends - lengths
    doc_index = jnp.sum((position[:, None] >= doc_ends[None, :]).astype(jnp.int32), 1)
    doc_hot = doc_index[:, None] == jnp.arange(lengths.shape[0], dtype=jnp.int32)[None, :]
    start_of = jnp.sum(jnp.where(doc_hot, doc_starts[None, :], 0), 1)
    offset = (position - start_of).astype(jnp.float32)
    frequency = ROPE_BASE ** (-2.0 * jnp.arange(HEAD_DIM // 2, dtype=jnp.float32) / HEAD_DIM)
    angles = offset[:, None] * frequency[None, :]
    allowed = (doc_index[:, None] == doc_index[None, :]) & (position[None, :] <= position[:, None])
    return (jnp.cos(angles), jnp.sin(angles), allowed)


def rotate(values, cos_table, sin_table):
    half_width = values.shape[-1] // 2
    first_half = values[..., :half_width]
    second_half = values[..., half_width:]
    cosine = cos_table[:, None, :]
    sine_part = sin_table[:, None, :]
    return jnp.concatenate(
        [
            first_half * cosine - second_half * sine_part,
            second_half * cosine + first_half * sine_part,
        ],
        -1,
    )


def rotate_back(grads, cos_table, sin_table):
    half_width = grads.shape[-1] // 2
    first_half = grads[..., :half_width]
    second_half = grads[..., half_width:]
    cosine = cos_table[:, None, :]
    sine_part = sin_table[:, None, :]
    return jnp.concatenate(
        [
            first_half * cosine + second_half * sine_part,
            second_half * cosine - first_half * sine_part,
        ],
        -1,
    )


def gelu_tanh(values):
    return jax.nn.gelu(values, approximate=True)


def learning_rates():
    return (
        RATE_SCALE * D ** (-0.5),
        RATE_SCALE * D ** (-0.5),
        RATE_SCALE * (D // 32) ** (-0.5),
        RATE_SCALE * (4 * D) ** (-0.5),
        GAIN_RATE,
        RATE_SCALE * D ** (-0.5),
        RATE_SCALE * (FF // 8) ** (-0.5),
    )


def adam_update(weight, first, second, grad, rate, decay):
    new_first = BETA_ONE * first + (1.0 - BETA_ONE) * grad
    new_second = BETA_TWO * second + (1.0 - BETA_TWO) * grad * grad
    first_hat = new_first / (1.0 - BETA_ONE**STEP)
    second_hat = new_second / (1.0 - BETA_TWO**STEP)
    new_weight = weight - rate * (first_hat / (jnp.sqrt(second_hat) + ADAM_EPS) + decay * weight)
    return (new_first, new_second, new_weight)


def shards(
    tokens,
    cotangent,
    routes,
    doc_lengths,
    query_weight,
    query_first,
    query_second,
    keyvalue_weight,
    keyvalue_first,
    keyvalue_second,
    output_weight,
    output_first,
    output_second,
    router_weight,
    router_first,
    router_second,
    norm_gains,
    gains_first,
    gains_second,
    expert_in,
    expert_in_first,
    expert_in_second,
    expert_out,
    expert_out_first,
    expert_out_second,
):
    rows_count = tokens.shape[0]
    experts = router_weight.shape[1]
    owners = lax.axis_size("expert")
    per_owner = expert_in.shape[0]
    capacity = 3 * rows_count * TOP // (2 * experts)
    groups = HEADS // KV_HEADS
    width_kv = KV_HEADS * HEAD_DIM
    score_scale = HEAD_DIM ** (-0.5)
    query_full, keyvalue_full, output_full, router_full, gains_full = (
        lax.all_gather(query_weight.astype(jnp.bfloat16), ("dp", "expert"), axis=0, tiled=True),
        lax.all_gather(keyvalue_weight.astype(jnp.bfloat16), ("dp", "expert"), axis=0, tiled=True),
        lax.all_gather(output_weight.astype(jnp.bfloat16), ("dp", "expert"), axis=0, tiled=True),
        lax.all_gather(router_weight.astype(jnp.bfloat16), ("dp", "expert"), axis=0, tiled=True),
        lax.all_gather(norm_gains.astype(jnp.bfloat16), ("dp", "expert"), axis=1, tiled=True),
    )
    in_full, out_full = (
        lax.all_gather(expert_in.astype(jnp.bfloat16), "dp", axis=1, tiled=True),
        lax.all_gather(expert_out.astype(jnp.bfloat16), "dp", axis=1, tiled=True),
    )
    gain_attn = gains_full[0].astype(jnp.float32)
    gain_moe = gains_full[1].astype(jnp.float32)
    cos_table, sin_table, allowed = doc_tables(doc_lengths[0], rows_count)
    inputs = tokens.astype(jnp.float32)
    inv_one = lax.rsqrt(jnp.mean(inputs * inputs, -1, keepdims=True) + EPS)
    normed_one = inputs * inv_one
    attn_in = (normed_one * gain_attn).astype(jnp.bfloat16)
    query_raw = jnp.dot(attn_in, query_full, preferred_element_type=jnp.float32)
    keyvalue_raw = jnp.dot(attn_in, keyvalue_full, preferred_element_type=jnp.float32)
    queries = (
        rotate(query_raw.reshape(rows_count, HEADS, HEAD_DIM), cos_table, sin_table)
        .astype(jnp.bfloat16)
        .reshape(rows_count, KV_HEADS, groups, HEAD_DIM)
    )
    keys_rot = rotate(
        keyvalue_raw[:, :width_kv].reshape(rows_count, KV_HEADS, HEAD_DIM), cos_table, sin_table
    ).astype(jnp.bfloat16)
    values_in = (
        keyvalue_raw[:, width_kv:].reshape(rows_count, KV_HEADS, HEAD_DIM).astype(jnp.bfloat16)
    )

    def score_table():
        raw_scores = (
            jnp.einsum("tkgd,skd->kgts", queries, keys_rot, preferred_element_type=jnp.float32)
            * score_scale
        )
        return jnp.where(allowed[None, None], raw_scores, NEG)

    scores = score_table()
    row_max = jnp.max(scores, -1, keepdims=True)
    exponent = jnp.exp(scores - row_max)
    totals = jnp.sum(exponent, -1, keepdims=True)
    probabilities = exponent / totals
    log_sum = row_max + jnp.log(totals)
    attended = jnp.einsum(
        "kgts,skd->tkgd",
        probabilities.astype(jnp.bfloat16),
        values_in,
        preferred_element_type=jnp.float32,
    )
    attended = attended.reshape(rows_count, HEADS * HEAD_DIM).astype(jnp.bfloat16)
    residual_mid = inputs + jnp.dot(attended, output_full, preferred_element_type=jnp.float32)
    inv_two = lax.rsqrt(jnp.mean(residual_mid * residual_mid, -1, keepdims=True) + EPS)
    normed_two = residual_mid * inv_two
    moe_in = (normed_two * gain_moe).astype(jnp.bfloat16)
    logits = jnp.dot(tokens, router_full, preferred_element_type=jnp.float32)
    expert_ids = jnp.arange(experts, dtype=jnp.int32)
    route_hot = routes[:, :, None] == expert_ids[None, None, :]
    picked = jnp.sum(jnp.where(route_hot, logits[:, None, :], 0.0), -1)
    gate_weights = jax.nn.softmax(picked, axis=-1)
    flat_routes = routes.reshape(-1)
    flat_hot = (flat_routes[:, None] == expert_ids[None, :]).astype(jnp.int32)
    slot_index = jnp.sum((jnp.cumsum(flat_hot, 0) - 1) * flat_hot, 1)
    destination = flat_routes * capacity + slot_index
    route_ids = jnp.arange(rows_count * TOP, dtype=jnp.int32)
    source_route = jnp.zeros((experts * capacity,), jnp.int32).at[destination].set(route_ids)
    slot_used = jnp.zeros((experts * capacity,), jnp.bool_).at[destination].set(True)
    source_token = source_route // TOP
    zero_row = jnp.zeros((), jnp.bfloat16)
    send_rows = jnp.where(slot_used[:, None], moe_in[source_token], zero_row).reshape(
        owners, per_owner, capacity, D
    )
    received = lax.all_to_all(send_rows, "expert", split_axis=0, concat_axis=0, tiled=True)
    hidden_pre = jnp.einsum("sicd,idf->sicf", received, in_full, preferred_element_type=jnp.float32)
    gate_part = hidden_pre[..., :FF]
    up_part = hidden_pre[..., FF:]
    activated, gelu_pull = jax.vjp(gelu_tanh, gate_part)
    product = (activated * up_part).astype(jnp.bfloat16)
    expert_rows = jnp.einsum(
        "sicf,ifd->sicd", product, out_full, preferred_element_type=jnp.float32
    ).astype(jnp.bfloat16)
    returned = lax.all_to_all(
        expert_rows, "expert", split_axis=0, concat_axis=0, tiled=True
    ).reshape(experts * capacity, D)
    routed = returned[destination].reshape(rows_count, TOP, D)
    block_out = residual_mid + jnp.sum(gate_weights[:, :, None] * routed, 1)
    mixed_out = block_out.astype(jnp.bfloat16)
    upstream = cotangent.astype(jnp.float32)
    gate_grad = jnp.einsum("tjd,td->tj", routed, cotangent, preferred_element_type=jnp.float32)
    picked_grad = gate_weights * (gate_grad - jnp.sum(gate_weights * gate_grad, -1, keepdims=True))
    logits_grad = jnp.sum(jnp.where(route_hot, picked_grad[:, :, None], 0.0), 1).astype(
        jnp.bfloat16
    )
    rows_grad = (
        (gate_weights[:, :, None] * upstream[:, None, :])
        .astype(jnp.bfloat16)
        .reshape(rows_count * TOP, D)
    )
    send_grad = jnp.where(slot_used[:, None], rows_grad[source_route], zero_row).reshape(
        owners, per_owner, capacity, D
    )
    received_grad = lax.all_to_all(send_grad, "expert", split_axis=0, concat_axis=0, tiled=True)
    product_grad = jnp.einsum(
        "sicd,ifd->sicf", received_grad, out_full, preferred_element_type=jnp.float32
    )
    out_weight_grad = jnp.einsum(
        "sicf,sicd->ifd", product, received_grad, preferred_element_type=jnp.float32
    )
    gate_part_grad = gelu_pull(product_grad * up_part)[0]
    up_part_grad = product_grad * activated
    hidden_grad = jnp.concatenate([gate_part_grad, up_part_grad], -1).astype(jnp.bfloat16)
    in_weight_grad = jnp.einsum(
        "sicd,sicf->idf", received, hidden_grad, preferred_element_type=jnp.float32
    )
    input_rows_grad = jnp.einsum(
        "sicf,idf->sicd", hidden_grad, in_full, preferred_element_type=jnp.float32
    ).astype(jnp.bfloat16)
    returned_grad = lax.all_to_all(
        input_rows_grad, "expert", split_axis=0, concat_axis=0, tiled=True
    ).reshape(experts * capacity, D)
    moe_in_grad = jnp.sum(
        returned_grad[destination].reshape(rows_count, TOP, D).astype(jnp.float32), 1
    )
    gain_two_grad = jnp.sum(moe_in_grad * normed_two, 0)
    scaled_two = moe_in_grad * gain_moe
    mid_grad = upstream + inv_two * (
        scaled_two - normed_two * jnp.mean(scaled_two * normed_two, -1, keepdims=True)
    )
    attn_out_grad = mid_grad.astype(jnp.bfloat16)
    output_weight_grad = jnp.einsum(
        "tc,td->cd", attended, attn_out_grad, preferred_element_type=jnp.float32
    )
    attended_grad = jnp.einsum(
        "td,cd->tc", attn_out_grad, output_full, preferred_element_type=jnp.float32
    )
    attended_grad = attended_grad.astype(jnp.bfloat16).reshape(
        rows_count, KV_HEADS, groups, HEAD_DIM
    )
    probs_again = jnp.exp(score_table() - log_sum)
    prob_grad = jnp.einsum(
        "tkgd,skd->kgts", attended_grad, values_in, preferred_element_type=jnp.float32
    )
    delta_sum = jnp.sum(probs_again * prob_grad, -1, keepdims=True)
    score_grad = (probs_again * (prob_grad - delta_sum)).astype(jnp.bfloat16)
    values_grad = jnp.einsum(
        "kgts,tkgd->skd",
        probs_again.astype(jnp.bfloat16),
        attended_grad,
        preferred_element_type=jnp.float32,
    )
    queries_grad = (
        jnp.einsum("kgts,skd->tkgd", score_grad, keys_rot, preferred_element_type=jnp.float32)
        * score_scale
    )
    keys_grad = (
        jnp.einsum("kgts,tkgd->skd", score_grad, queries, preferred_element_type=jnp.float32)
        * score_scale
    )
    query_raw_grad = rotate_back(
        queries_grad.reshape(rows_count, HEADS, HEAD_DIM), cos_table, sin_table
    )
    query_raw_grad = query_raw_grad.astype(jnp.bfloat16).reshape(rows_count, HEADS * HEAD_DIM)
    key_raw_grad = (
        rotate_back(keys_grad, cos_table, sin_table)
        .astype(jnp.bfloat16)
        .reshape(rows_count, width_kv)
    )
    keyvalue_grad = jnp.concatenate(
        [key_raw_grad, values_grad.astype(jnp.bfloat16).reshape(rows_count, width_kv)], -1
    )
    query_weight_grad = jnp.einsum(
        "tc,tf->cf", attn_in, query_raw_grad, preferred_element_type=jnp.float32
    )
    keyvalue_weight_grad = jnp.einsum(
        "tc,tf->cf", attn_in, keyvalue_grad, preferred_element_type=jnp.float32
    )
    attn_in_grad = jnp.einsum(
        "tf,cf->tc", query_raw_grad, query_full, preferred_element_type=jnp.float32
    )
    attn_in_grad = attn_in_grad + jnp.einsum(
        "tf,cf->tc", keyvalue_grad, keyvalue_full, preferred_element_type=jnp.float32
    )
    gain_one_grad = jnp.sum(attn_in_grad * normed_one, 0)
    scaled_one = attn_in_grad * gain_attn
    tokens_grad = mid_grad + inv_one * (
        scaled_one - normed_one * jnp.mean(scaled_one * normed_one, -1, keepdims=True)
    )
    tokens_grad = tokens_grad + jnp.einsum(
        "te,ce->tc", logits_grad, router_full, preferred_element_type=jnp.float32
    )
    router_weight_grad = jnp.einsum(
        "tc,te->ce", tokens, logits_grad, preferred_element_type=jnp.float32
    )
    gains_grad = jnp.stack([gain_one_grad, gain_two_grad], 0)
    reduced = (
        lax.psum_scatter(query_weight_grad, ("dp", "expert"), scatter_dimension=0, tiled=True),
        lax.psum_scatter(keyvalue_weight_grad, ("dp", "expert"), scatter_dimension=0, tiled=True),
        lax.psum_scatter(output_weight_grad, ("dp", "expert"), scatter_dimension=0, tiled=True),
        lax.psum_scatter(router_weight_grad, ("dp", "expert"), scatter_dimension=0, tiled=True),
        lax.psum_scatter(gains_grad, ("dp", "expert"), scatter_dimension=1, tiled=True),
    )
    expert_sums = (
        lax.psum_scatter(
            in_weight_grad.astype(jnp.bfloat16), "dp", scatter_dimension=1, tiled=True
        ).astype(jnp.float32),
        lax.psum_scatter(
            out_weight_grad.astype(jnp.bfloat16), "dp", scatter_dimension=1, tiled=True
        ).astype(jnp.float32),
    )
    rates = learning_rates()
    query_upd = adam_update(query_weight, query_first, query_second, reduced[0], rates[0], DECAY)
    keyvalue_upd = adam_update(
        keyvalue_weight, keyvalue_first, keyvalue_second, reduced[1], rates[1], DECAY
    )
    output_upd = adam_update(
        output_weight, output_first, output_second, reduced[2], rates[2], DECAY
    )
    router_upd = adam_update(
        router_weight, router_first, router_second, reduced[3], rates[3], DECAY
    )
    gains_upd = adam_update(norm_gains, gains_first, gains_second, reduced[4], rates[4], 0.0)
    in_upd = adam_update(
        expert_in, expert_in_first, expert_in_second, expert_sums[0], rates[5], DECAY
    )
    out_upd = adam_update(
        expert_out, expert_out_first, expert_out_second, expert_sums[1], rates[6], DECAY
    )
    return (
        mixed_out,
        tokens_grad,
        query_upd[0],
        query_upd[1],
        query_upd[2],
        keyvalue_upd[0],
        keyvalue_upd[1],
        keyvalue_upd[2],
        output_upd[0],
        output_upd[1],
        output_upd[2],
        router_upd[0],
        router_upd[1],
        router_upd[2],
        gains_upd[0],
        gains_upd[1],
        gains_upd[2],
        in_upd[0],
        in_upd[1],
        in_upd[2],
        out_upd[0],
        out_upd[1],
        out_upd[2],
    )


def flip(mask):
    return [(i, i ^ mask) for i in range(8)]


ACROSS_X, ACROSS_Y, ACROSS_CORE = flip(2), flip(4), flip(1)
FORWARD = [(i, i ^ (4 if i & 1 else 2)) for i in range(8)]


def after(value, *earlier):
    return lax.optimization_barrier((value, *earlier))[0]


def hold(*values):
    return lax.optimization_barrier(values)


def to_x(value):
    return lax.ppermute(value, "expert", ACROSS_X)


def to_y(value):
    return lax.ppermute(value, "expert", ACROSS_Y)


def to_core(value):
    return lax.ppermute(value, "expert", ACROSS_CORE)


def to_far(value):
    return lax.ppermute(value, "expert", flip(6))


def forward(value):
    return lax.ppermute(value, "expert", FORWARD)


def gather_plane(value, core):
    from_x, from_y = to_x(value), to_y(value)
    from_core = to_core(value)
    from_far = forward(jnp.where(core == 0, from_y, from_x))
    return [
        value,
        from_core,
        from_x,
        to_core(from_x),
        from_y,
        to_core(from_y),
        from_far,
        to_core(from_far),
    ]


def add_low(*terms):
    total = terms[0].astype(jnp.float32)
    for term in terms[1:]:
        total = total + term.astype(jnp.float32)
    return total.astype(jnp.bfloat16)


def add_low_wide(*terms):
    return sum([term.astype(jnp.float32) for term in terms])


def scatter_plane(parts, core):
    far = add_low(parts[6], to_core(parts[7]))
    relayed = forward(far)
    by_x = add_low(parts[2], to_core(parts[3]))
    by_y = add_low(parts[4], to_core(parts[5]))
    own = add_low(parts[0], to_core(parts[1]))
    zero = jnp.zeros((), jnp.bfloat16)
    by_x = add_low(by_x, jnp.where(core == 1, relayed, zero))
    by_y = add_low(by_y, jnp.where(core == 0, relayed, zero))
    return own, to_x(by_x), to_y(by_y)


def gather_column(value, ring):
    values = [value]
    for _ in range(len(ring) - 1):
        values.append(lax.ppermute(values[-1], "dp", ring))
    return values


def scatter_column(value, ring, place):
    count = len(ring)
    rows = value.shape[0] // count

    def piece(shard):
        return lax.dynamic_slice_in_dim(value, (shard % count) * rows, rows, 0)

    moving = piece(place + count - 1)
    for step in range(count - 2):
        moving = add_low(lax.ppermute(moving, "dp", ring), piece(place + count - 2 - step))
    return lax.ppermute(moving, "dp", ring).astype(jnp.float32) + piece(place).astype(jnp.float32)


def scatter_pieces(pieces, ring):
    moving = pieces[1]
    for piece in pieces[2:]:
        moving = add_low(lax.ppermute(moving, "dp", ring), piece)
    return lax.ppermute(moving, "dp", ring).astype(jnp.float32) + pieces[0].astype(jnp.float32)


def anywhere():
    return pl.BlockSpec(memory_space=pl.ANY)


def scalars():
    return pl.BlockSpec(memory_space=pltpu.SMEM)


def whole():
    return pl.BlockSpec(memory_space=pltpu.VMEM)


def small_cost():
    return pl.CostEstimate(flops=1024, bytes_accessed=1024, transcendentals=0)


def load_rows(blocks, start_ref, joined, sems, column=0, start=True):
    width = joined.shape[1]
    pieces, rows = blocks[0].shape[0], blocks[0].shape[1]
    copies = []
    for i, block in enumerate(blocks):
        for p in range(pieces):
            at = pl.multiple_of(start_ref[i * pieces + p], 16)
            copies.append(
                pltpu.make_async_copy(
                    block.at[p, :, pl.ds(column, width)],
                    joined.at[pl.ds(at, rows)],
                    sems.at[i * pieces + p],
                )
            )
    for copy in copies if start else []:
        copy.start()
    return copies


def wide_dot(left, right):
    return lax.dot_general(
        left, right, (((1,), (1,)), ((), ())), preferred_element_type=jnp.float32
    )


def tall_dot(left, right):
    return lax.dot_general(
        left, right, (((0,), (0,)), ((), ())), preferred_element_type=jnp.float32
    )


def load_weight(chunks, place_ref, buffer, sems, start=True):
    total = sum([chunk.shape[0] for chunk in chunks[::4]])
    copies, offset = [], 0
    for j, chunk in enumerate(chunks):
        rows = chunk.shape[0]
        at = pl.multiple_of(place_ref[j % 4] * total + offset, 16)
        copies.append(pltpu.make_async_copy(chunk, buffer.at[pl.ds(at, rows)], sems.at[j]))
        if j % 4 == 3:
            offset += rows
    for copy in copies if start else []:
        copy.start()
    return copies


LANES = 256
WIDE = 512


def turned(values, cosine, sine):
    return values * cosine + pltpu.roll(values, HEAD_DIM // 2, 1) * sine


def fill_bias(bias, first):
    row = lax.broadcasted_iota(jnp.int32, bias.shape, 0)
    column = lax.broadcasted_iota(jnp.int32, bias.shape, 1).astype(jnp.float32)
    row = row.astype(jnp.float32)
    bias[...] = jnp.where((column <= row) & (column >= first), 0.0, NEG)


def attend_kernel(planes, start_ref, tokens_ref, table_ref, routes_ref, *refs):
    blocks, refs = refs[:planes], refs[planes:]
    attn_in_out, heads_out, attended_out, residual_out, packed_out, *refs = refs
    log_ref, small_ref, gates_ref, *refs = refs
    weight, late, bias, table, attn_in_ref, heads_ref, attended_ref, *refs = refs
    residual_ref, packed_ref, sems, late_sems, out_sems = refs
    rows_count = tokens_ref.shape[0]
    width_q, width_kv = HEADS * HEAD_DIM, KV_HEADS * HEAD_DIM
    width = width_q + 2 * width_kv
    table_copy = pltpu.make_async_copy(table_ref, table, out_sems.at[0])
    table_copy.start()
    copies = load_rows(blocks, start_ref, weight, sems)
    late_copies = load_rows(blocks, start_ref, late, late_sems, weight.shape[1])
    table_copy.wait()
    leaving = []

    def store(source, target):
        leaving.append(pltpu.make_async_copy(source, target, out_sems.at[1 + len(leaving)]))
        leaving[-1].start()

    fill_bias(bias, table[:, 2 * HEAD_DIM : 2 * HEAD_DIM + 1])
    inputs = tokens_ref[...].astype(jnp.float32)
    inverse = lax.rsqrt(jnp.mean(inputs * inputs, -1, keepdims=True) + EPS)
    normed = inputs * inverse
    for copy in copies:
        copy.wait()
    small = jnp.transpose(weight[:, width:].astype(jnp.float32))
    small_ref[...] = small[:16, :]
    experts = small_ref.shape[0] - 8
    attn_in_ref[...] = (normed * small[experts : experts + 1, :]).astype(jnp.bfloat16)
    store(attn_in_ref, attn_in_out)
    cosine, sine = table[:, :HEAD_DIM], table[:, HEAD_DIM : 2 * HEAD_DIM]
    for at in range(0, width, LANES):
        raw = jnp.dot(
            attn_in_ref[...], weight[:, at : at + LANES], preferred_element_type=jnp.float32
        )
        for column in range(0, LANES, HEAD_DIM):
            values = raw[:, column : column + HEAD_DIM]
            if at + column < width_q + width_kv:
                values = turned(values, cosine, sine)
            heads_ref[:, at + column : at + column + HEAD_DIM] = values.astype(jnp.bfloat16)
    store(heads_ref, heads_out)

    logits = wide_dot(small_ref[...].astype(jnp.bfloat16), tokens_ref[...])[:experts, :]
    expert = lax.broadcasted_iota(jnp.int32, logits.shape, 0)
    routed = expert == routes_ref[:1, :]
    for choice in range(1, TOP):
        routed = routed | (expert == routes_ref[choice : choice + 1, :])
    logits = jnp.where(routed, logits, NEG)
    exponent = jnp.exp(logits - jnp.max(logits, 0, keepdims=True))
    exponent = jnp.where(routed, exponent, 0.0)
    gates = exponent / jnp.sum(exponent, 0, keepdims=True)
    gates_ref[...] = gates
    packed_ref[rows_count:, :] = jnp.concatenate(
        [split_row(gates), jnp.zeros((16 - experts, D), jnp.float32)], 0
    ).astype(jnp.bfloat16)
    store(packed_ref.at[pl.ds(rows_count, 16)], packed_out.at[pl.ds(rows_count, 16)])

    half = rows_count // 2
    for block in range(2):
        rows, reach = pl.ds(block * half, half), (block + 1) * half
        logs = jnp.zeros((half, 128), jnp.float32)
        lane = lax.broadcasted_iota(jnp.int32, logs.shape, 1)
        for head in range(HEADS):
            key_at = width_q + head // (HEADS // KV_HEADS) * HEAD_DIM
            value_at = key_at + width_kv
            scores = wide_dot(
                heads_ref[rows, head * HEAD_DIM : (head + 1) * HEAD_DIM],
                heads_ref[:reach, key_at : key_at + HEAD_DIM],
            )
            scores = scores * HEAD_DIM ** (-0.5) + bias[rows, :reach]
            peak = jnp.max(scores, -1, keepdims=True)
            exponent = jnp.exp(scores - peak)
            total = jnp.sum(exponent, -1, keepdims=True)
            mixed = jnp.dot(
                exponent.astype(jnp.bfloat16),
                heads_ref[:reach, value_at : value_at + HEAD_DIM],
                preferred_element_type=jnp.float32,
            )
            attended_ref[rows, head * HEAD_DIM : (head + 1) * HEAD_DIM] = (
                mixed * (1.0 / total)
            ).astype(jnp.bfloat16)
            logs = jnp.where(lane == head, peak + jnp.log(total), logs)
        log_ref[rows, :] = logs
        store(attended_ref.at[rows], attended_out.at[rows])
        if block == 0:
            for copy in late_copies:
                copy.wait()
        for at in range(0, D, LANES):
            residual_ref[rows, at : at + LANES] = tokens_ref[rows, at : at + LANES].astype(
                jnp.float32
            ) + jnp.dot(
                attended_ref[rows, :], late[:, at : at + LANES], preferred_element_type=jnp.float32
            )
        residual = residual_ref[rows, :]
        inverse = lax.rsqrt(jnp.mean(residual * residual, -1, keepdims=True) + EPS)
        packed_ref[rows, :] = (
            residual * inverse * small_ref[experts + 1 : experts + 2, :]
        ).astype(jnp.bfloat16)
        store(packed_ref.at[rows], packed_out.at[rows])
        store(residual_ref.at[rows], residual_out.at[rows])
    for copy in leaving:
        copy.wait()


def attend_call(starts, tokens, table, routes, blocks, width_early, experts):
    rows_count = tokens.shape[0]
    width = (HEADS + 2 * KV_HEADS) * HEAD_DIM
    low = jnp.bfloat16
    copies = len(blocks) * blocks[0].shape[0]
    moved = [
        ((rows_count, D), low),
        ((rows_count, width), low),
        ((rows_count, HEADS * HEAD_DIM), low),
        ((rows_count, D), jnp.float32),
        ((rows_count + 16, D), low),
    ]
    kept = [
        ((rows_count, 128), jnp.float32),
        ((16, D), jnp.float32),
        ((experts, rows_count), jnp.float32),
    ]
    return pl.pallas_call(
        functools.partial(attend_kernel, len(blocks)),
        out_shape=[jax.ShapeDtypeStruct(*shape) for shape in moved + kept],
        in_specs=[scalars(), whole(), anywhere(), whole()] + [anywhere()] * len(blocks),
        out_specs=[anywhere()] * len(moved) + [whole()] * len(kept),
        scratch_shapes=[
            pltpu.VMEM((D, width_early), low),
            pltpu.VMEM((D, D), low),
            pltpu.VMEM((rows_count, rows_count), jnp.float32),
            pltpu.VMEM(table.shape, jnp.float32),
            *[pltpu.VMEM(*shape) for shape in moved],
            pltpu.SemaphoreType.DMA((copies,)),
            pltpu.SemaphoreType.DMA((copies,)),
            pltpu.SemaphoreType.DMA((10,)),
        ],
        compiler_params=pltpu.CompilerParams(vmem_limit_bytes=62 << 20),
        cost_estimate=small_cost(),
        name="attend",
    )(starts, tokens, table, routes, *blocks)


def middle_back_kernel(planes, column, start_ref, *refs):
    terms, tails, refs = refs[:4], refs[4:8], refs[8:]
    residual_ref, small_ref, cot_ref, tokens_ref, gates_ref, refs = *refs[:5], refs[5:]
    blocks, refs = refs[:planes], refs[planes:]
    mid_ref, low_ref, attended_grad_ref, logits_grad_ref, small_grad_ref, weight, sems = refs
    step = pl.program_id(0)
    experts = gates_ref.shape[0]
    rows_count = gates_ref.shape[1]

    @pl.when(step == 0)
    def _():
        copies = load_rows(blocks, start_ref, weight, sems, column)
        del copies
        gates = gates_ref[...]
        parts = sum([tail[:experts, :].astype(jnp.float32) for tail in tails])
        grad = (
            parts[:, :rows_count]
            + parts[:, rows_count : 2 * rows_count]
            + parts[:, 2 * rows_count :]
        )
        grad = gates * (grad - jnp.sum(gates * grad, 0, keepdims=True))
        logits_grad_ref[...] = jnp.concatenate(
            [grad, jnp.zeros((16 - experts, rows_count), jnp.float32)], 0
        ).astype(jnp.bfloat16)
        small_grad_ref[...] = jnp.zeros_like(small_grad_ref)

    grad = sum([term[...].astype(jnp.float32) for term in terms])
    residual = residual_ref[...]
    inverse = lax.rsqrt(jnp.mean(residual * residual, -1, keepdims=True) + EPS)
    normed = residual * inverse
    product = grad * normed
    small_grad_ref[experts : experts + 1, :] += jnp.sum(product, 0, keepdims=True)
    tile = tokens_ref.shape[0]
    lanes = pl.ds(pl.multiple_of(step * tile, tile), tile)
    small_grad_ref[:experts, :] += jnp.dot(
        logits_grad_ref[:, lanes], tokens_ref[...], preferred_element_type=jnp.float32
    )[:experts, :]
    gain = small_ref[experts + 1 : experts + 2, :]
    mean = jnp.mean(product * gain, -1, keepdims=True)
    mid = cot_ref[...].astype(jnp.float32) + inverse * (grad * gain - normed * mean)
    mid_ref[...] = mid
    low_ref[...] = mid.astype(jnp.bfloat16)

    @pl.when(step == 0)
    def _():
        for copy in load_rows(blocks, start_ref, weight, sems, column, False):
            copy.wait()

    for at in range(0, D, LANES):
        attended_grad_ref[:, at : at + LANES] = wide_dot(
            low_ref[...], weight[at : at + LANES, :]
        ).astype(jnp.bfloat16)


def middle_back_call(
    starts, terms, residual, small, cotangent, tokens, gates, blocks, column
):
    rows_count = residual.shape[0]
    tile = rows_count // 2
    low = jnp.bfloat16
    tiled = pl.BlockSpec((tile, D), lambda i: (i, 0))
    fixed = lambda rows, columns: pl.BlockSpec((rows, columns), lambda i: (0, 0))
    tail = pl.BlockSpec((16, D), lambda i: (rows_count // 16, 0))
    return pl.pallas_call(
        functools.partial(middle_back_kernel, len(blocks), column),
        grid=(2,),
        out_shape=[
            jax.ShapeDtypeStruct((rows_count, D), jnp.float32),
            jax.ShapeDtypeStruct((rows_count, D), low),
            jax.ShapeDtypeStruct((rows_count, D), low),
            jax.ShapeDtypeStruct((16, rows_count), low),
            jax.ShapeDtypeStruct((16, D), jnp.float32),
        ],
        in_specs=[scalars()]
        + [tiled] * 4
        + [tail] * 4
        + [tiled, fixed(16, D), tiled, tiled, fixed(*gates.shape)]
        + [anywhere()] * len(blocks),
        out_specs=[tiled, tiled, tiled, fixed(16, rows_count), fixed(16, D)],
        scratch_shapes=[
            pltpu.VMEM((D, D), low),
            pltpu.SemaphoreType.DMA((len(blocks) * blocks[0].shape[0],)),
        ],
        compiler_params=pltpu.CompilerParams(vmem_limit_bytes=62 << 20),
        cost_estimate=small_cost(),
        name="middle_back",
    )(starts, *terms, *terms, residual, small, cotangent, tokens, gates, *blocks)


def attend_back_kernel(heads_ref, grad_ref, log_ref, table_ref, raw_ref, bias):
    rows_count = heads_ref.shape[0]
    width_q, width_kv = HEADS * HEAD_DIM, KV_HEADS * HEAD_DIM
    half = rows_count // 2
    scale = HEAD_DIM ** (-0.5)
    fill_bias(bias, table_ref[:, 2 * HEAD_DIM : 2 * HEAD_DIM + 1])
    cosine, sine = table_ref[:, :HEAD_DIM], -table_ref[:, HEAD_DIM : 2 * HEAD_DIM]
    for key_head in range(KV_HEADS):
        key_at = width_q + key_head * HEAD_DIM
        value_at = key_at + width_kv
        key_grads, value_grads = [], []
        for block in range(2):
            rows, reach = slice(block * half, (block + 1) * half), (block + 1) * half
            keys = heads_ref[:reach, key_at : key_at + HEAD_DIM]
            values = heads_ref[:reach, value_at : value_at + HEAD_DIM]
            key_grad = jnp.zeros((reach, HEAD_DIM), jnp.float32)
            value_grad = jnp.zeros((reach, HEAD_DIM), jnp.float32)
            for head in range(key_head * HEADS // KV_HEADS, (key_head + 1) * HEADS // KV_HEADS):
                columns = slice(head * HEAD_DIM, (head + 1) * HEAD_DIM)
                queries, grads = heads_ref[rows, columns], grad_ref[rows, columns]
                scores = wide_dot(queries, keys) * scale + bias[rows, :reach]
                chances = jnp.exp(scores - log_ref[rows, head : head + 1])
                pulled = wide_dot(grads, values)
                shift = jnp.sum(chances * pulled, -1, keepdims=True)
                score_grad = (chances * (pulled - shift)).astype(jnp.bfloat16)
                value_grad = value_grad + tall_dot(chances.astype(jnp.bfloat16), grads)
                key_grad = key_grad + tall_dot(score_grad, queries)
                query_grad = (
                    jnp.dot(score_grad, keys, preferred_element_type=jnp.float32) * scale
                )
                raw_ref[rows, columns] = turned(
                    query_grad, cosine[rows, :], sine[rows, :]
                ).astype(jnp.bfloat16)
            key_grads.append(key_grad)
            value_grads.append(value_grad)
        key_grad = jnp.concatenate([key_grads[0] + key_grads[1][:half], key_grads[1][half:]], 0)
        value_grad = jnp.concatenate(
            [value_grads[0] + value_grads[1][:half], value_grads[1][half:]], 0
        )
        raw_ref[:, key_at : key_at + HEAD_DIM] = turned(key_grad * scale, cosine, sine).astype(
            jnp.bfloat16
        )
        raw_ref[:, value_at : value_at + HEAD_DIM] = value_grad.astype(jnp.bfloat16)


def attend_back_call(heads, grads, logs, table):
    rows_count = heads.shape[0]
    return pl.pallas_call(
        attend_back_kernel,
        out_shape=jax.ShapeDtypeStruct(heads.shape, jnp.bfloat16),
        in_specs=[whole()] * 4,
        out_specs=whole(),
        scratch_shapes=[pltpu.VMEM((rows_count, rows_count), jnp.float32)],
        compiler_params=pltpu.CompilerParams(vmem_limit_bytes=62 << 20),
        cost_estimate=small_cost(),
        name="attend_back",
    )(heads, grads, logs, table)


def shard_grad_kernel(extra, start_ref, left_ref, right_ref, *refs):
    parts, grad, sems = refs[extra:-2], refs[-2], refs[-1]
    width = right_ref.shape[1]
    pairs, pieces, rows = parts[0].shape[:3]
    owners = 2 * pairs
    tall = owners * rows
    copies = []
    if extra:
        small = refs[0][...]
        small = jnp.concatenate([small, jnp.zeros((128 - small.shape[0], D), jnp.float32)], 0)
        grad[:, width:] = jnp.transpose(small).astype(jnp.bfloat16)
    for p in range(pieces):
        for at in range(0, width, WIDE):
            grad[p * tall : (p + 1) * tall, at : at + WIDE] = tall_dot(
                left_ref[:, p * tall : (p + 1) * tall], right_ref[:, at : at + WIDE]
            ).astype(jnp.bfloat16)
        to = lax.rem(start_ref[0] + pieces - p, pieces)
        for i in range(owners):
            at = pl.multiple_of(p * tall + start_ref[1 + i] * rows, 16)
            copy = pltpu.make_async_copy(
                grad.at[pl.ds(at, rows)], parts[i % 2].at[i // 2, to], sems.at[p * owners + i]
            )
            copy.start()
            copies.append(copy)
    for copy in copies:
        copy.wait()


def shard_grad_call(spots, left, right, pieces, owners, small=None):
    extra = [] if small is None else [small]
    width, height = right.shape[1] + 128 * len(extra), left.shape[1]
    rows = height // (pieces * owners)
    return pl.pallas_call(
        functools.partial(shard_grad_kernel, len(extra)),
        out_shape=[jax.ShapeDtypeStruct((owners // 2, pieces, rows, width), jnp.bfloat16)] * 2,
        in_specs=[scalars()] + [whole()] * (2 + len(extra)),
        out_specs=[anywhere()] * 2,
        scratch_shapes=[
            pltpu.VMEM((height, width), jnp.bfloat16),
            pltpu.SemaphoreType.DMA((pieces * owners,)),
        ],
        compiler_params=pltpu.CompilerParams(vmem_limit_bytes=62 << 20),
        cost_estimate=small_cost(),
        name="shard_grad",
    )(spots, left, right, *extra)


def entry_back_kernel(planes, start_ref, *refs):
    raw_ref, tokens_ref, mid_ref, small_ref, logits_grad_ref, refs = *refs[:5], refs[5:]
    blocks, refs = refs[:planes], refs[planes:]
    grad_ref, weight, sems = refs
    step = pl.program_id(0)
    width = raw_ref.shape[1]
    experts = small_ref.shape[0] - 8
    tile = tokens_ref.shape[0]

    @pl.when(step == 0)
    def _():
        for copy in load_rows(blocks, start_ref, weight, sems):
            copy.wait()

    for at in range(0, D, LANES):
        grad_ref[:, at : at + LANES] = wide_dot(raw_ref[...], weight[at : at + LANES, :width])
    inputs = tokens_ref[...].astype(jnp.float32)
    inverse = lax.rsqrt(jnp.mean(inputs * inputs, -1, keepdims=True) + EPS)
    normed = inputs * inverse
    grad = grad_ref[...]
    gain = small_ref[experts : experts + 1, :]
    mean = jnp.mean(grad * normed * gain, -1, keepdims=True)
    row = lax.broadcasted_iota(jnp.int32, (16, 1), 0)
    router = jnp.where(row < experts, small_ref[...], 0.0).astype(jnp.bfloat16)
    grad_ref[...] = (
        mid_ref[...]
        + inverse * (grad * gain - normed * mean)
        + tall_dot(logits_grad_ref[...], router)
    )


def entry_back_call(
    starts, raw_grad, tokens, mid_grad, small, logits_grad, blocks, width_early
):
    rows_count = tokens.shape[0]
    tile = rows_count // 2
    tiled = lambda columns: pl.BlockSpec((tile, columns), lambda i: (i, 0))
    fixed = lambda rows, columns: pl.BlockSpec((rows, columns), lambda i: (0, 0))
    return pl.pallas_call(
        functools.partial(entry_back_kernel, len(blocks)),
        grid=(2,),
        out_shape=jax.ShapeDtypeStruct((rows_count, D), jnp.float32),
        in_specs=[
            scalars(),
            tiled(raw_grad.shape[1]),
            tiled(D),
            tiled(D),
            fixed(16, D),
            pl.BlockSpec((16, tile), lambda i: (0, i)),
        ]
        + [anywhere()] * len(blocks),
        out_specs=tiled(D),
        scratch_shapes=[
            pltpu.VMEM((D, width_early), jnp.bfloat16),
            pltpu.SemaphoreType.DMA((len(blocks) * blocks[0].shape[0],)),
        ],
        compiler_params=pltpu.CompilerParams(vmem_limit_bytes=62 << 20),
        cost_estimate=small_cost(),
        name="entry_back",
    )(starts, raw_grad, tokens, mid_grad, small, logits_grad, *blocks)


def pipeline(loads, stores, body, count, later=()):
    coming = {}

    def fetch(i):
        coming[i] = loads(i, i % 2)
        for copy in coming[i]:
            copy.start()

    leaving = {}
    fetch(0)
    for copy in later:
        copy.start()
    for i in range(count):
        if i + 1 < count:
            fetch(i + 1)
        for copy in coming.pop(i):
            copy.wait()
        for copy in leaving.pop(i - 2, []):
            copy.wait()
        body(i, i % 2)
        leaving[i] = stores(i, i % 2)
        for copy in leaving[i]:
            copy.start()
    for i in sorted(leaving):
        for copy in leaving[i]:
            copy.wait()


def copies_of(pairs, sems):
    return [
        pltpu.make_async_copy(source, target, sems.at[j])
        for j, (source, target) in enumerate(pairs)
    ]


def hidden_kernel(count, pieces, tokens_count, place_ref, *refs):
    rows_in, chunks, refs = refs[:count], refs[count : count + pieces], refs[count + pieces :]
    outs, refs = refs[: 3 * count], refs[3 * count :]
    weight, rows, slope, product, gated, sems, in_sems, out_sems = refs
    weight_copies = load_weight(chunks, place_ref, weight, sems)

    def loads(i, slot):
        return copies_of([(rows_in[i], rows.at[slot])], in_sems.at[slot])

    def stores(i, slot):
        buffers = (slope, product, gated)
        return copies_of(
            [(buffer.at[slot], outs[j * count + i]) for j, buffer in enumerate(buffers)],
            out_sems.at[slot],
        )

    def body(i, slot):
        if i == 0:
            for copy in weight_copies:
                copy.wait()
        weights = spread(expert_row(rows[slot, tokens_count:, :], place_ref[4]), tokens_count)
        weights = jnp.concatenate([weights] * (LANES // 128), 1)
        for at in range(0, FF, LANES):
            gate = jnp.dot(
                rows[slot, :tokens_count, :],
                weight[:, at : at + LANES],
                preferred_element_type=jnp.float32,
            )
            up = jnp.dot(
                rows[slot, :tokens_count, :],
                weight[:, FF + at : FF + at + LANES],
                preferred_element_type=jnp.float32,
            )
            square = gate * gate
            bend = jnp.tanh(0.7978845608028654 * gate * (1.0 + 0.044715 * square))
            half = 0.5 + 0.5 * bend
            steep = half + 0.5 * gate * (1.0 - bend * bend) * (
                0.7978845608028654 + 0.10703222440890037 * square
            )
            active = gate * half
            both = (active * up).astype(jnp.bfloat16)
            slope[slot, :, at : at + LANES] = (up * steep).astype(jnp.bfloat16)
            slope[slot, :, FF + at : FF + at + LANES] = active.astype(jnp.bfloat16)
            product[slot, :, at : at + LANES] = both
            gated[slot, :, at : at + LANES] = (both.astype(jnp.float32) * weights).astype(
                jnp.bfloat16
            )

    pipeline(loads, stores, body, count)


def hidden_call(rows_in, chunks, places, tokens_count):
    count = len(rows_in)
    low = jnp.bfloat16
    widths = [2 * FF, FF, FF]
    outs = pl.pallas_call(
        functools.partial(hidden_kernel, count, len(chunks), tokens_count),
        out_shape=[
            jax.ShapeDtypeStruct((tokens_count, width), low)
            for width in widths
            for _ in range(count)
        ],
        in_specs=[scalars()] + [anywhere()] * (count + len(chunks)),
        out_specs=[anywhere()] * (3 * count),
        scratch_shapes=[
            pltpu.VMEM((D, 2 * FF), low),
            pltpu.VMEM((2, *rows_in[0].shape), low),
            *[pltpu.VMEM((2, tokens_count, width), low) for width in widths],
            pltpu.SemaphoreType.DMA((len(chunks),)),
            pltpu.SemaphoreType.DMA((2, 1)),
            pltpu.SemaphoreType.DMA((2, 3)),
        ],
        compiler_params=pltpu.CompilerParams(vmem_limit_bytes=62 << 20),
        cost_estimate=small_cost(),
        name="expert_hidden",
    )(places, *rows_in, *chunks)
    return outs[:count], outs[count : 2 * count], outs[2 * count :]


def spread(row, tokens_count):
    return jnp.transpose(jnp.broadcast_to(row, (128, tokens_count)))


def expert_row(block, expert):
    third = block.shape[1] // 3
    index = lax.broadcasted_iota(jnp.int32, block.shape, 0)
    row = jnp.sum(jnp.where(index == expert, block.astype(jnp.float32), 0.0), 0, keepdims=True)
    return row[:, :third] + row[:, third : 2 * third] + row[:, 2 * third :]


def split_row(row):
    high = row.astype(jnp.bfloat16)
    rest = row - high.astype(jnp.float32)
    middle = rest.astype(jnp.bfloat16)
    low = (rest - middle.astype(jnp.float32)).astype(jnp.bfloat16)
    return jnp.concatenate(
        [high.astype(jnp.float32), middle.astype(jnp.float32), low.astype(jnp.float32)], 1
    )


def pull_kernel(count, pieces, tokens_count, place_ref, *refs):
    packed, cots, slopes, products = (refs[i * count : (i + 1) * count] for i in range(4))
    refs = refs[4 * count :]
    in_chunks, out_chunks, refs = refs[: pieces[0]], refs[pieces[0] : sum(pieces)], refs[sum(pieces) :]
    row_grads, hidden_grads, refs = refs[:count], refs[count : 2 * count], refs[2 * count :]
    in_weight, out_weight, tail, cot, slope, product, grad, hidden, *sems = refs
    expert = place_ref[4]
    in_copies, out_copies = [], []

    def loads(i, slot):
        copies = copies_of(
            [
                (packed[i].at[pl.ds(tokens_count, 16)], tail.at[slot]),
                (cots[i], cot.at[slot]),
                (slopes[i], slope.at[slot]),
                (products[i], product.at[slot]),
            ],
            sems[2].at[slot],
        )
        return copies

    def stores(i, slot):
        return copies_of([(grad.at[slot], row_grads[i])], sems[3].at[slot])

    leaving = {}

    def body(i, slot):
        if i == 0:
            for copy in out_copies:
                copy.wait()
        if i >= 2:
            leaving.pop(i - 2).wait()
        weights = spread(expert_row(tail[slot], expert), tokens_count)
        weights = jnp.concatenate([weights] * (LANES // 128), 1)
        gate_grad = jnp.zeros((tokens_count, 1), jnp.float32)
        for at in range(0, FF, LANES):
            pulled = wide_dot(cot[slot], out_weight[at : at + LANES, :])
            both = product[slot, :, at : at + LANES].astype(jnp.float32)
            gate_grad = gate_grad + jnp.sum(pulled * both, 1, keepdims=True)
            pulled = pulled * weights
            for base in (at, FF + at):
                hidden[slot, :, base : base + LANES] = (
                    pulled * slope[slot, :, base : base + LANES].astype(jnp.float32)
                ).astype(jnp.bfloat16)
        row = jnp.transpose(jnp.broadcast_to(gate_grad, (tokens_count, 128)))[:1, :]
        parts = jnp.broadcast_to(split_row(row), (16, 3 * tokens_count))
        index = lax.broadcasted_iota(jnp.int32, parts.shape, 0)
        grad[slot, tokens_count:, :] = jnp.where(index == expert, parts, 0.0).astype(jnp.bfloat16)
        leaving[i] = pltpu.make_async_copy(hidden.at[slot], hidden_grads[i], sems[4].at[slot])
        leaving[i].start()
        if i == 0:
            for copy in in_copies:
                copy.wait()
        for at in range(0, D, LANES):
            grad[slot, :tokens_count, at : at + LANES] = wide_dot(
                hidden[slot], in_weight[at : at + LANES, :]
            ).astype(jnp.bfloat16)

    out_copies += load_weight(out_chunks, place_ref, out_weight, sems[1])
    in_copies += load_weight(in_chunks, place_ref, in_weight, sems[0], False)
    pipeline(loads, stores, body, count, in_copies)
    for i in sorted(leaving):
        leaving[i].wait()


def pull_call(packed, cots, slopes, products, in_chunks, out_chunks, places, tokens_count):
    count = len(packed)
    low = jnp.bfloat16
    out_shapes = [(tokens_count + 16, D), (tokens_count, 2 * FF)]
    outs = pl.pallas_call(
        functools.partial(
            pull_kernel, count, (len(in_chunks), len(out_chunks)), tokens_count
        ),
        out_shape=[jax.ShapeDtypeStruct(shape, low) for shape in out_shapes for _ in range(count)],
        in_specs=[scalars()] + [anywhere()] * (4 * count + len(in_chunks) + len(out_chunks)),
        out_specs=[anywhere()] * (2 * count),
        scratch_shapes=[
            pltpu.VMEM((D, 2 * FF), low),
            pltpu.VMEM((FF, D), low),
            pltpu.VMEM((2, 16, D), low),
            pltpu.VMEM((2, tokens_count, D), low),
            pltpu.VMEM((2, tokens_count, 2 * FF), low),
            pltpu.VMEM((2, tokens_count, FF), low),
            pltpu.VMEM((2, tokens_count + 16, D), low),
            pltpu.VMEM((2, tokens_count, 2 * FF), low),
            pltpu.SemaphoreType.DMA((len(in_chunks),)),
            pltpu.SemaphoreType.DMA((len(out_chunks),)),
            pltpu.SemaphoreType.DMA((2, 4)),
            pltpu.SemaphoreType.DMA((2, 1)),
            pltpu.SemaphoreType.DMA((2,)),
        ],
        compiler_params=pltpu.CompilerParams(vmem_limit_bytes=62 << 20),
        cost_estimate=small_cost(),
        name="expert_pull",
    )(places, *packed, *cots, *slopes, *products, *in_chunks, *out_chunks)
    return outs[:count], outs[count:]


def product_kernel(count, place_ref, *refs):
    gated, chunks, refs = refs[:count], refs[count : count + 4], refs[count + 4 :]
    rows_out, (weight, left, total, *sems) = refs[:count], refs[count:]
    weight_copies = load_weight(chunks, place_ref, weight, sems[0])

    def loads(i, slot):
        return copies_of([(gated[i], left.at[slot])], sems[1].at[slot])

    def stores(i, slot):
        return copies_of([(total.at[slot], rows_out[i])], sems[2].at[slot])

    def body(i, slot):
        if i == 0:
            for copy in weight_copies:
                copy.wait()
        for at in range(0, D, LANES):
            total[slot, :, at : at + LANES] = jnp.dot(
                left[slot], weight[:, at : at + LANES], preferred_element_type=jnp.float32
            ).astype(jnp.bfloat16)

    pipeline(loads, stores, body, count)


def product_call(gated, chunks, places):
    count, rows = len(gated), gated[0].shape[0]
    return pl.pallas_call(
        functools.partial(product_kernel, count),
        out_shape=[jax.ShapeDtypeStruct((rows, D), jnp.bfloat16)] * count,
        in_specs=[scalars()] + [anywhere()] * (count + 4),
        out_specs=[anywhere()] * count,
        scratch_shapes=[
            pltpu.VMEM((FF, D), jnp.bfloat16),
            pltpu.VMEM((2, rows, FF), jnp.bfloat16),
            pltpu.VMEM((2, rows, D), jnp.bfloat16),
            pltpu.SemaphoreType.DMA((4,)),
            pltpu.SemaphoreType.DMA((2, 1)),
            pltpu.SemaphoreType.DMA((2, 1)),
        ],
        compiler_params=pltpu.CompilerParams(vmem_limit_bytes=62 << 20),
        cost_estimate=small_cost(),
        name="expert_rows",
    )(places, *gated, *chunks)


def weight_grad_kernel(count, rows, *refs):
    left, right, grad = refs[:count], refs[count : 2 * count], refs[2 * count]
    total = tall_dot(left[0][:rows, :], right[0][:rows, :])
    for i in range(1, count):
        total = total + tall_dot(left[i][:rows, :], right[i][:rows, :])
    grad[...] = total.astype(grad.dtype)


def weight_grad_call(left, right, rows, tall, wide, name):
    count = len(left)
    height, width = left[0].shape[1], right[0].shape[1]
    return pl.pallas_call(
        functools.partial(weight_grad_kernel, count, rows),
        grid=(height // tall, width // wide),
        out_shape=jax.ShapeDtypeStruct((height, width), jnp.bfloat16),
        in_specs=[pl.BlockSpec((rows, tall), lambda i, j: (0, i))] * count
        + [pl.BlockSpec((rows, wide), lambda i, j: (0, j))] * count,
        out_specs=pl.BlockSpec((tall, wide), lambda i, j: (i, j)),
        compiler_params=pltpu.CompilerParams(vmem_limit_bytes=62 << 20),
        cost_estimate=small_cost(),
        name=name,
    )(*left, *right)


def plane_shards(
    tokens,
    cotangent,
    routes,
    doc_lengths,
    query_weight,
    query_first,
    query_second,
    keyvalue_weight,
    keyvalue_first,
    keyvalue_second,
    output_weight,
    output_first,
    output_second,
    router_weight,
    router_first,
    router_second,
    norm_gains,
    gains_first,
    gains_second,
    expert_in,
    expert_in_first,
    expert_in_second,
    expert_out,
    expert_out_first,
    expert_out_second,
):
    rows_count = tokens.shape[0]
    experts = router_weight.shape[1]
    columns_dp, owners = lax.axis_size("dp"), lax.axis_size("expert")
    dp_index, expert_index = lax.axis_index("dp"), lax.axis_index("expert")
    core = expert_index & 1
    ring = [(i, (i + 1) % columns_dp) for i in range(columns_dp)]
    shard = query_weight.shape[0]
    width_q = HEADS * HEAD_DIM
    width_qkv = (HEADS + 2 * KV_HEADS) * HEAD_DIM
    low = jnp.bfloat16
    places = (dp_index - jnp.arange(columns_dp, dtype=jnp.int32)) % columns_dp
    starts = (
        (expert_index ^ jnp.arange(owners, dtype=jnp.int32))[:, None] + places[None, :] * owners
    ).reshape(-1) * shard
    places = jnp.concatenate([places, expert_index[None]]).astype(jnp.int32)
    spots = jnp.concatenate([dp_index[None], expert_index ^ jnp.arange(owners)]).astype(jnp.int32)

    position = jnp.arange(rows_count, dtype=jnp.int32)
    ends = jnp.cumsum(doc_lengths[0])
    first = jnp.max(jnp.where(position[:, None] >= ends[None, :], ends[None, :], 0), 1)
    offset = (position - first).astype(jnp.float32)
    frequency = ROPE_BASE ** (-2.0 * jnp.arange(HEAD_DIM // 2, dtype=jnp.float32) / HEAD_DIM)
    angles = offset[:, None] * frequency[None, :]
    cosine, sine = jnp.cos(angles), jnp.sin(angles)
    first = jnp.broadcast_to(first.astype(jnp.float32)[:, None], (rows_count, HEAD_DIM))
    table = jnp.concatenate([cosine, cosine, -sine, sine, first], 1)

    width_early = width_qkv + 128

    def cross(block):
        return to_x(block), to_y(block)

    def onward(from_x, from_y):
        return jnp.where(core == 0, from_y, from_x)

    sent = jnp.concatenate(
        [
            query_weight.astype(low),
            keyvalue_weight.astype(low),
            router_weight.astype(low),
            norm_gains.T.astype(low),
            jnp.zeros((shard, 128 - experts - 2), low),
            output_weight.astype(low),
        ],
        1,
    )

    def around(value):
        return lax.ppermute(value, "dp", ring)

    cot_x, cot_y = cross(cotangent)
    in_low, out_low = expert_in[0].astype(low), expert_out[0].astype(low)
    column = [sent, around(sent)]
    column.append(around(column[1]))
    column[2], in_low, out_low, table, routes_t = hold(
        column[2], in_low, out_low, table, routes.T
    )
    column.append(around(column[2]))
    joint = jnp.stack(column)
    cut = in_low.shape[0] * 2 // 3
    cot_x, cot_y, joint, in_low, out_low = hold(cot_x, cot_y, joint, in_low, out_low)
    in_near, in_rest, out_chunks = [in_low[:cut]], [in_low[cut:]], [out_low]

    joint_x, joint_y = cross(joint)
    joint_core = to_core(joint)
    in_near.append(around(in_near[0]))
    in_rest.append(around(in_rest[0]))
    joint_x, joint_y, joint_core, in_near, in_rest, cot_x, cot_y = hold(
        joint_x, joint_y, joint_core, in_near, in_rest, cot_x, cot_y
    )
    joint_far = forward(onward(joint_x, joint_y))
    joint_x2, joint_y2 = to_core(joint_x), to_core(joint_y)
    cot_x2 = to_core(cot_x)
    in_near.append(around(in_near[1]))
    outward = onward(cot_x, cot_y)
    joint_far, joint_x2, joint_y2, in_near, in_rest, cot_x2, cot_y, outward = hold(
        joint_far, joint_x2, joint_y2, in_near, in_rest, cot_x2, cot_y, outward
    )
    joint_far2 = to_core(joint_far)
    joint_far2, outward, cot_y, in_near, in_rest = hold(
        joint_far2, outward, cot_y, in_near, in_rest
    )
    plane = [joint, joint_core, joint_x, joint_x2, joint_y, joint_y2, joint_far, joint_far2]

    cot_far = forward(outward)
    cot_core, cot_y2 = to_core(cotangent), to_core(cot_y)
    in_near.append(around(in_near[2]))
    attn_in, heads, attended, residual_mid, packed, logs, small, gates = attend_call(
        starts, tokens, table, routes_t, plane, width_early, experts
    )
    packed, cot_far, cot_core, cot_y2, in_near, in_rest, out_chunks = hold(
        packed, cot_far, cot_core, cot_y2, in_near, in_rest, out_chunks
    )

    packed_x, packed_y = cross(packed)
    packed_core = to_core(packed)
    in_rest.append(around(in_rest[1]))
    in_rest.append(around(in_rest[2]))
    in_chunks = in_near + in_rest
    out_chunks.append(around(after(out_chunks[0], in_rest[3])))
    slopes, products, gated = [None] * 8, [None] * 8, [None] * 8
    packed_blocks = [packed, packed_core] + [None] * 6

    def hidden(order, *earlier):
        blocks = [packed_blocks[k] for k in order]
        blocks[0] = after(blocks[0], *earlier)
        for k, *outs in zip(order, *hidden_call(blocks, in_chunks, places, rows_count)):
            slopes[k], products[k], gated[k] = outs

    hidden((0, 1))
    packed_x, packed_y, gated[0], out_chunks, cot_far = hold(
        packed_x, packed_y, gated[0], out_chunks, cot_far
    )
    packed_x2, packed_y2 = to_core(packed_x), to_core(packed_y)
    packed_far = forward(onward(packed_x, packed_y))
    cot_far2 = to_core(cot_far)
    out_chunks.append(around(out_chunks[1]))
    cot_blocks = [cotangent, cot_core, cot_x, cot_x2, cot_y, cot_y2, cot_far, cot_far2]
    packed_blocks[2:6] = [packed_x, packed_x2, packed_y, packed_y2]
    hidden((2, 4, 3, 5))
    packed_far, out_chunks, gated[3] = hold(packed_far, out_chunks, gated[3])
    packed_far2 = to_core(packed_far)
    packed_blocks[6:] = hold(packed_far, packed_far2)
    out_chunks.append(around(after(out_chunks[2], packed_far2)))
    hidden((6, 7))
    out_grad = weight_grad_call(gated, cot_blocks, rows_count, FF, LANES, "expert_out_grad")
    out_grad, out_chunks = hold(out_grad, out_chunks)

    def column_piece(value, back):
        rows = value.shape[0] // columns_dp
        return lax.dynamic_slice_in_dim(value, places[back] * rows, rows, 0)

    moving = column_piece(out_grad, 1)
    row_grads, hidden_grads, rows_out = [None] * 8, [None] * 8, [None] * 8

    def pick(values, order):
        return [values[k] for k in order]

    def pull(order, *earlier):
        first_cot = after(cot_blocks[order[0]], *earlier)
        outs = pull_call(
            pick(packed_blocks, order),
            [first_cot] + pick(cot_blocks, order[1:]),
            pick(slopes, order),
            pick(products, order),
            in_chunks,
            out_chunks,
            places,
            rows_count,
        )
        for k, row_grad, hidden_grad in zip(order, *outs):
            row_grads[k], hidden_grads[k] = row_grad, hidden_grad

    def rows_of(order, *earlier):
        first_gated = after(gated[order[0]], *earlier)
        outs = product_call([first_gated] + pick(gated, order[1:]), out_chunks, places)
        for k, rows in zip(order, outs):
            rows_out[k] = rows

    zero = jnp.zeros((), low)

    def by_core(value, wanted):
        return jnp.where(core == wanted, value, zero)

    rows_of((7, 6), moving)
    rows_out[6], rows_out[7], moving = hold(rows_out[6], rows_out[7], moving)
    moved = around(moving)
    rows_back = to_core(rows_out[7])
    pull((7, 6), rows_out[6])
    moved, rows_back, row_grads[6], row_grads[7] = hold(
        moved, rows_back, row_grads[6], row_grads[7]
    )
    far_back = to_core(row_grads[7])
    rows_far = add_low(rows_out[6], rows_back)
    moving = add_low(moved, column_piece(out_grad, 2))
    far_back, rows_far, moving = hold(far_back, rows_far, moving)
    far = add_low(row_grads[6], far_back)
    far, rows_far, moving = hold(far, rows_far, moving)
    relayed, rows_relayed = forward(far), forward(rows_far)
    moved = around(moving)
    pull((0, 1, 3, 2, 5, 4), far, rows_far, moving)
    relayed, moved, row_grads[:6] = hold(relayed, moved, row_grads[:6])
    back_x, back_y = to_core(row_grads[3]), to_core(row_grads[5])
    back_own = to_core(row_grads[1])
    rows_of((5, 4, 3, 2, 1, 0), row_grads[0])
    moving = add_low(moved, column_piece(out_grad, 3))
    back_x, back_y, back_own, rows_out[:6], moving = hold(
        back_x, back_y, back_own, rows_out[:6], moving
    )
    by_x = add_low(row_grads[2], back_x, by_core(relayed, 1))
    by_y = add_low(row_grads[4], back_y, by_core(relayed, 0))
    by_x, by_y, moving, hidden_grads[0], rows_out[:6], rows_relayed = hold(
        by_x, by_y, moving, hidden_grads[0], rows_out[:6], rows_relayed
    )

    from_x, from_y = to_x(by_x), to_y(by_y)
    moved = around(moving)
    rows_backs = [to_core(rows_out[k]) for k in (3, 5)]
    in_grad = weight_grad_call(
        packed_blocks, hidden_grads, rows_count, FF, WIDE, "expert_in_grad"
    )
    rows_x = add_low(rows_out[2], rows_backs[0], by_core(rows_relayed, 1))
    rows_y = add_low(rows_out[4], rows_backs[1], by_core(rows_relayed, 0))
    cut = in_low.shape[0] * 5 // 8

    def in_pieces(back):
        piece = column_piece(in_grad, back)
        return piece[:cut], piece[cut:]

    near, rest = in_pieces(1)
    from_x, from_y, moved, near, rest, rows_out[:2], rows_x, rows_y = hold(
        from_x, from_y, moved, near, rest, rows_out[:2], rows_x, rows_y
    )
    expert_out_sum = moved.astype(jnp.float32) + column_piece(out_grad, 0).astype(jnp.float32)

    rows_from_x, rows_from_y = to_x(rows_x), to_y(rows_y)
    rows_back = to_core(rows_out[1])
    near_moved, rest_moved = around(near), around(rest)
    mid_grad, mid_low, attended_grad, logits_grad, small_grad = middle_back_call(
        starts, [after(row_grads[0], rows_x), back_own, from_x, from_y], residual_mid,
        small, cotangent, tokens, gates, plane, width_early,
    )
    raw_grad = attend_back_call(heads, attended_grad, logs, table)
    early_even, early_odd = shard_grad_call(spots, attn_in, raw_grad, columns_dp, owners)
    early_even, early_odd, mid_low, rows_back, near_moved, rest_moved = hold(
        early_even, early_odd, mid_low, rows_back, near_moved, rest_moved
    )
    rest = add_low(rest_moved, in_pieces(2)[1])
    rest, early_odd, rows_from_x, rows_from_y = hold(rest, early_odd, rows_from_x, rows_from_y)
    early_back = to_core(early_odd)
    rest_moved = around(rest)
    near = add_low(near_moved, in_pieces(2)[0])
    output_even, output_odd = shard_grad_call(
        spots, attended, mid_low, columns_dp, owners, small_grad
    )
    early_back, output_even, output_odd, near, rest_moved = hold(
        early_back, output_even, output_odd, near, rest_moved
    )
    near_moved = around(near)
    early_far = add_low(early_even[3], early_back[3])
    early_far, output_odd, output_even = hold(early_far, output_odd, output_even)

    early_relayed = forward(early_far)
    output_back = to_core(output_odd)
    tokens_grad = entry_back_call(
        starts, after(raw_grad, early_far), tokens, mid_grad, small, logits_grad,
        plane, width_early,
    )
    early_pairs = add_low(early_even[:3], early_back[:3])
    rest = add_low(rest_moved, in_pieces(3)[1])
    early_relayed, output_back, tokens_grad, early_pairs, near_moved, rest = hold(
        early_relayed, output_back, tokens_grad, early_pairs, near_moved, rest
    )
    early_x = add_low(early_pairs[1], by_core(early_relayed, 1))
    early_y = add_low(early_pairs[2], by_core(early_relayed, 0))
    output_far = add_low(output_even[3], output_back[3])
    near = add_low(near_moved, in_pieces(3)[0])
    early_x, early_y, output_far, near, expert_out_sum, rows_back = hold(
        early_x, early_y, output_far, near, expert_out_sum, rows_back
    )
    early_x, early_y, output_relayed = to_x(early_x), to_y(early_y), forward(output_far)
    near_moved, rest_moved = around(near), around(rest)
    output_pairs = add_low(output_even[:3], output_back[:3])
    block_out = residual_mid + add_low_wide(rows_out[0], rows_back, rows_from_x, rows_from_y)
    mixed_out = block_out.astype(low)
    early_x, early_y, output_relayed, output_pairs, near_moved, rest_moved = hold(
        early_x, early_y, output_relayed, output_pairs, near_moved, rest_moved
    )
    early_total = add_low(early_pairs[0], early_x, early_y)
    output_x = add_low(output_pairs[1], by_core(output_relayed, 1))
    output_y = add_low(output_pairs[2], by_core(output_relayed, 0))
    early_total, output_x, output_y = hold(early_total, output_x, output_y)

    def spread_pieces(total):
        return [total[0]] + [
            lax.ppermute(total[p], "dp", [(i, (i - p) % columns_dp) for i in range(columns_dp)])
            for p in range(1, columns_dp)
        ]

    early_pieces = spread_pieces(early_total)
    output_x, output_y = to_x(output_x), to_y(output_y)
    expert_in_sum = jnp.concatenate([near_moved, rest_moved]).astype(
        jnp.float32
    ) + column_piece(in_grad, 0).astype(jnp.float32)
    early_pieces, output_x, output_y = hold(early_pieces, output_x, output_y)
    output_total = add_low(output_pairs[0], output_x, output_y)
    output_pieces = spread_pieces(output_total)
    output_sum = add_low_wide(*output_pieces)
    summed = add_low_wide(*early_pieces)
    used = sent[:, :width_qkv].astype(jnp.float32)
    gain_one = sent[:, width_qkv + experts].astype(jnp.float32)
    gain_one_sum = jnp.sum(used * summed, 1) / gain_one
    at = width_qkv
    sums = (
        summed[:, :width_q],
        summed[:, width_q:at],
        output_sum[:, :D],
        output_sum[:, D : D + experts],
        jnp.stack([gain_one_sum, output_sum[:, D + experts]]),
        expert_in_sum[None],
        expert_out_sum[None],
    )
    (
        (query_weight, query_first, query_second),
        (keyvalue_weight, keyvalue_first, keyvalue_second),
        (output_weight, output_first, output_second),
        (router_weight, router_first, router_second),
        (norm_gains, gains_first, gains_second),
        _,
    ) = hold(
        (query_weight, query_first, query_second),
        (keyvalue_weight, keyvalue_first, keyvalue_second),
        (output_weight, output_first, output_second),
        (router_weight, router_first, router_second),
        (norm_gains, gains_first, gains_second),
        early_total,
    )
    weights = (
        (query_weight, query_first, query_second),
        (keyvalue_weight, keyvalue_first, keyvalue_second),
        (output_weight, output_first, output_second),
        (router_weight, router_first, router_second),
        (norm_gains, gains_first, gains_second),
        (expert_in, expert_in_first, expert_in_second),
        (expert_out, expert_out_first, expert_out_second),
    )
    updates = []
    for state, grad, rate, decay in zip(
        weights, sums, learning_rates(), (DECAY, DECAY, DECAY, DECAY, 0.0, DECAY, DECAY)
    ):
        updates.extend(adam_update(*state, grad, rate, decay))
    return (mixed_out, tokens_grad, *updates)


def solution(mesh):
    in_specs = (
        P(("dp", "expert"), None),
        P(("dp", "expert"), None),
        P(("dp", "expert"), None),
        P(("dp", "expert"), None),
        P(("dp", "expert"), None),
        P(("dp", "expert"), None),
        P(("dp", "expert"), None),
        P(("dp", "expert"), None),
        P(("dp", "expert"), None),
        P(("dp", "expert"), None),
        P(("dp", "expert"), None),
        P(("dp", "expert"), None),
        P(("dp", "expert"), None),
        P(("dp", "expert"), None),
        P(("dp", "expert"), None),
        P(("dp", "expert"), None),
        P(None, ("dp", "expert")),
        P(None, ("dp", "expert")),
        P(None, ("dp", "expert")),
        P("expert", "dp", None),
        P("expert", "dp", None),
        P("expert", "dp", None),
        P("expert", "dp", None),
        P("expert", "dp", None),
        P("expert", "dp", None),
    )
    out_specs = (
        P(("dp", "expert"), None),
        P(("dp", "expert"), None),
        P(("dp", "expert"), None),
        P(("dp", "expert"), None),
        P(("dp", "expert"), None),
        P(("dp", "expert"), None),
        P(("dp", "expert"), None),
        P(("dp", "expert"), None),
        P(("dp", "expert"), None),
        P(("dp", "expert"), None),
        P(("dp", "expert"), None),
        P(("dp", "expert"), None),
        P(("dp", "expert"), None),
        P(("dp", "expert"), None),
        P(None, ("dp", "expert")),
        P(None, ("dp", "expert")),
        P(None, ("dp", "expert")),
        P("expert", "dp", None),
        P("expert", "dp", None),
        P("expert", "dp", None),
        P("expert", "dp", None),
        P("expert", "dp", None),
        P("expert", "dp", None),
    )
    def body(tokens, *rest):
        one_plane = mesh.shape["expert"] == 8 and rest[12].shape[1] == 8
        fits = one_plane and 3 * tokens.shape[0] == D
        return (plane_shards if fits else shards)(tokens, *rest)

    return jax.shard_map(body, mesh=mesh, in_specs=in_specs, out_specs=out_specs, check_vma=False)
```
